256 devices in a mesh: rows: 16 (over z, core), feat: 16 (over y, x).
Axes of the slice: x: 4, y: 4, z: 8, core: 2. Of those that a mesh axis runs over, the one named last changes fastest.
Arguments:
- features: bfloat16 [4096, 2048], P('rows', 'feat'), may hold values from -6 to 6
- w_self: bfloat16 [2048, 2048], P(None, 'feat'), may hold values from -0.125 to 0.125
- w_neigh: bfloat16 [2048, 2048], P(None, 'feat'), may hold values from -0.25 to 0.25
- out_grad: bfloat16 [4096, 2048], P('rows', 'feat'), may hold values from -6 to 6
- tile_count: int32 [16], P('rows'), may hold values from 0 to 80, as said below
- tile_dst: int32 [16, 80], P('rows'), may hold values from 0 to 1
- tile_src: int32 [16, 80], P('rows'), may hold values from 0 to 31, as said below
- tile_weight: int32 [16, 80, 128, 128], P('rows'), may hold values from 0 to 3
Outputs:
- output: bfloat16 [4096, 2048], P('rows', 'feat')
- grad_features: bfloat16 [4096, 2048], P('rows', 'feat')
- grad_self: float32 [2048, 2048], P('rows', 'feat')
- grad_neigh: float32 [2048, 2048], P('rows', 'feat')
The draws below stay inside these ranges and needn't reach their ends.
Inputs may be any that keep to these rules, and one draw needn't show every extreme that they name: Row group g uses the first tile_count[g] slots of its lists; the others are ignored. One row group has exactly 80 in every draw. `tile_src`: A destination and source pair may repeat; repeated tiles add. Over all its slots, row group g names at most one distinct source tile among the 2 tiles of any one row group, and in every draw some row group names exactly 1 of one row group's tiles within its used slots.
All inputs are finite; a program needn't handle non-finite values.
Results may differ from the reference program's by a relative error of at most 0.005.
Values may be sent and summed in bfloat16 or wider, within the bound.
No kernel may reach another device: no remote copies, remote signals or barrier semaphores. Data moves between devices by JAX's collectives and lax.ppermute only.
A program may use at most 64 MiB of HBM per device.

```python
import jax
import jax.numpy as jnp
from jax import lax

F = 2048
TILE = 128
TILES_DEV = 2
MAXT = 80
GROUPS = 16
NODES = 4096
SRC_CAP = 1


def busiest_group(key):
    return jax.random.randint(jax.random.fold_in(key, 7), (), 0, GROUPS, dtype=jnp.int32)


def draw_tile_count(key, part):
    busiest = busiest_group(key)
    key = jax.random.fold_in(key, 11)
    base_counts = jax.random.randint(key, (GROUPS,), MAXT // 6, MAXT // 2 + 1, dtype=jnp.int32)
    return jnp.where(jnp.arange(GROUPS, dtype=jnp.int32) == busiest, jnp.int32(MAXT), base_counts).astype(jnp.int32)


def draw_tile_dst(key, part):
    key = jax.random.fold_in(key, 23)
    return jax.random.randint(key, (GROUPS, MAXT), 0, TILES_DEV, dtype=jnp.int32)


def draw_tile_src(key, part):
    busiest = busiest_group(key)
    key = jax.random.fold_in(key, 37)
    perm_key, owner_key, pick_key = jax.random.split(key, 3)
    perm_keys = jax.random.split(perm_key, GROUPS * GROUPS)
    orders = jax.vmap(lambda one_key: jax.random.permutation(one_key, TILES_DEV))(perm_keys)
    orders = orders.reshape(GROUPS, GROUPS, TILES_DEV)[:, :, :SRC_CAP].astype(jnp.int32)
    owner_ids = jnp.arange(GROUPS, dtype=jnp.int32)[None, :, None]
    candidates = owner_ids * TILES_DEV + orders
    owners = jax.random.randint(owner_key, (GROUPS, MAXT), 0, GROUPS, dtype=jnp.int32)
    picks = jax.random.randint(pick_key, (GROUPS, MAXT), 0, SRC_CAP, dtype=jnp.int32)
    group_ids = jnp.broadcast_to(jnp.arange(GROUPS, dtype=jnp.int32)[:, None], (GROUPS, MAXT))
    sources = candidates[group_ids, owners, picks]
    neighbour = (busiest + 1) % GROUPS
    forced = candidates[busiest, neighbour]
    slot_ids = jnp.arange(MAXT, dtype=jnp.int32)
    forced_row = jnp.where(slot_ids < SRC_CAP, forced[jnp.minimum(slot_ids, SRC_CAP - 1)], sources[busiest])
    is_busiest = (jnp.arange(GROUPS, dtype=jnp.int32) == busiest)[:, None]
    return jnp.where(is_busiest, forced_row[None, :], sources).astype(jnp.int32)


def draw_tile_weight(key, part):
    key = jax.random.fold_in(key, 53)
    first_key, second_key = jax.random.split(key)
    present = jax.random.randint(first_key, (GROUPS, MAXT, TILE, TILE), 0, 16, dtype=jnp.int32) == 0
    values = jax.random.randint(second_key, (GROUPS, MAXT, TILE, TILE), 1, 4, dtype=jnp.int32)
    return jnp.where(present, values, jnp.int32(0)).astype(jnp.int32)


def block_levels(own_key, shape, shards, smallest, high):
    factor_of = 1.0
    for dim, blocks in shards:
        draws = jax.random.uniform(jax.random.fold_in(jax.random.fold_in(own_key, 6), dim), (blocks,), jnp.float32, smallest / len(shards), high / len(shards))
        factor_of = factor_of * jnp.repeat(jnp.exp(draws), shape[dim] // blocks).reshape((-1,) + (1,) * (len(shape) - 1 - dim))
    return factor_of


def normal_values(key, dims, spread, limit, shards=(), kind=jnp.bfloat16):
    array = jax.random.normal(key, dims, jnp.float32) * spread
    if len(shards) > 0:
        array = block_levels(key, dims, shards, -0.22, 0.18) * array
    return jnp.clip(array, min=-limit, max=limit).astype(kind)


def setup_inputs(seed: int = 0) -> dict:
    seeds = jax.random.split(jax.random.key(seed), 9)
    return {
        "features": normal_values(seeds[0], (NODES, F), 1.0, 6.0, ((0, 16), (1, 16))),
        "w_self": normal_values(seeds[1], (F, F), F ** -0.5, 0.125, ((1, 16),)),
        "w_neigh": normal_values(seeds[2], (F, F), (F // 4) ** -0.5, 0.25, ((1, 16),)),
        "out_grad": normal_values(seeds[3], (NODES, F), 1.0, 6.0, ((0, 16), (1, 16))),
        "tile_count": draw_tile_count(jax.random.fold_in(seeds[8], 71), 0),
        "tile_dst": draw_tile_dst(jax.random.fold_in(seeds[8], 71), 0),
        "tile_src": draw_tile_src(jax.random.fold_in(seeds[8], 71), 0),
        "tile_weight": draw_tile_weight(jax.random.fold_in(seeds[8], 71), 0),
    }


def tile_lists(tile_count, tile_dst, tile_src, tile_weight):
    group_ids = jnp.repeat(jnp.arange(GROUPS, dtype=jnp.int32), MAXT)
    slot_ids = jnp.tile(jnp.arange(MAXT, dtype=jnp.int32), GROUPS)
    in_use = slot_ids < tile_count[group_ids]
    dst_rows = ((group_ids * TILES_DEV + tile_dst.reshape(-1)) * TILE).astype(jnp.int32)
    src_rows = (tile_src.reshape(-1) * TILE).astype(jnp.int32)
    weights = tile_weight.reshape(GROUPS * MAXT, TILE, TILE)
    return in_use, dst_rows, src_rows, weights


def apply_forward(source, lists):
    in_use, dst_rows, src_rows, weights = lists

    def step(total, entry):
        used_flag, dst_row, src_row, tile_w = entry
        source_rows = lax.dynamic_slice_in_dim(source, src_row, TILE, 0)
        product = jnp.dot(tile_w.astype(jnp.bfloat16), source_rows, preferred_element_type=jnp.float32)
        product = jnp.where(used_flag, product, jnp.float32(0.0))
        current = lax.dynamic_slice_in_dim(total, dst_row, TILE, 0)
        return lax.dynamic_update_slice_in_dim(total, current + product, dst_row, 0), None

    total = jnp.zeros((NODES, source.shape[1]), jnp.float32)
    total, _ = lax.scan(step, total, (in_use, dst_rows, src_rows, weights))
    return total


def apply_adjoint(source, lists):
    in_use, dst_rows, src_rows, weights = lists

    def step(total, entry):
        used_flag, dst_row, src_row, tile_w = entry
        source_rows = lax.dynamic_slice_in_dim(source, dst_row, TILE, 0)
        product = lax.dot_general(tile_w.astype(jnp.bfloat16), source_rows, (((0,), (0,)), ((), ())), preferred_element_type=jnp.float32)
        product = jnp.where(used_flag, product, jnp.float32(0.0))
        current = lax.dynamic_slice_in_dim(total, src_row, TILE, 0)
        return lax.dynamic_update_slice_in_dim(total, current + product, src_row, 0), None

    total = jnp.zeros((NODES, source.shape[1]), jnp.float32)
    total, _ = lax.scan(step, total, (in_use, dst_rows, src_rows, weights))
    return total


def reference(features, w_self, w_neigh, out_grad, tile_count, tile_dst, tile_src, tile_weight):
    lists = tile_lists(tile_count, tile_dst, tile_src, tile_weight)
    in_use, dst_rows, src_rows, weights = lists
    row_sums = jnp.sum(weights, axis=2).astype(jnp.float32)
    row_sums = jnp.where(in_use[:, None], row_sums, jnp.float32(0.0))
    node_index = (dst_rows[:, None] + jnp.arange(TILE, dtype=jnp.int32)[None, :]).reshape(-1)
    degree = jnp.zeros((NODES,), jnp.float32).at[node_index].add(row_sums.reshape(-1))
    inverse = 1.0 / jnp.maximum(degree, jnp.float32(1.0))
    aggregated = (apply_forward(features, lists) * inverse[:, None]).astype(jnp.bfloat16)
    preact = jnp.dot(features, w_self, preferred_element_type=jnp.float32) + jnp.dot(aggregated, w_neigh, preferred_element_type=jnp.float32)
    sigmoid_pre = jax.nn.sigmoid(preact)
    output = (preact * sigmoid_pre).astype(jnp.bfloat16)
    preact_grad = (out_grad.astype(jnp.float32) * sigmoid_pre * (1.0 + preact * (1.0 - sigmoid_pre))).astype(jnp.bfloat16)
    contract_rows = (((0,), (0,)), ((), ()))
    grad_self = lax.dot_general(features, preact_grad, contract_rows, preferred_element_type=jnp.float32)
    grad_neigh = lax.dot_general(aggregated, preact_grad, contract_rows, preferred_element_type=jnp.float32)
    contract_cols = (((1,), (1,)), ((), ()))
    direct_grad = lax.dot_general(preact_grad, w_self, contract_cols, preferred_element_type=jnp.float32)
    aggregated_grad = lax.dot_general(preact_grad, w_neigh, contract_cols, preferred_element_type=jnp.float32)
    scaled_grad = (aggregated_grad * inverse[:, None]).astype(jnp.bfloat16)
    grad_features = (direct_grad + apply_adjoint(scaled_grad, lists)).astype(jnp.bfloat16)
    return output, grad_features, grad_self, grad_neigh
```

```python
import functools

import jax
import jax.numpy as jnp
from jax import lax
from jax.experimental import pallas as pl
from jax.experimental.pallas import tpu as pltpu
from jax.sharding import Mesh, PartitionSpec as P

F32 = jnp.float32
BF16 = jnp.bfloat16
T = 128
CHUNK = 10
LIMIT = 48 * 1024 * 1024
VMEM = pl.BlockSpec(memory_space=pltpu.VMEM)
SMEM = pl.BlockSpec(memory_space=pltpu.SMEM)
HBM = pl.BlockSpec(memory_space=pl.ANY)
PARAMS = pltpu.CompilerParams(vmem_limit_bytes=LIMIT)


def dot(a, b):
    return jnp.dot(a, b, preferred_element_type=F32)


def adjacency_kernel(count_ref, dst_ref, src_ref, weight_ref, adj_ref, inv_ref, flag_ref, sel_ref, buf, acc, sems):
    count = count_ref[0]
    slots = weight_ref.shape[0]
    groups = acc.shape[0]

    def chunk_copy(index):
        part = pl.ds(index * CHUNK, CHUNK)
        return pltpu.make_async_copy(weight_ref.at[part], buf.at[part], sems.at[index])

    for index in range(slots // CHUNK):

        @pl.when(index * CHUNK < count)
        def _():
            chunk_copy(index).start()

    acc[...] = jnp.zeros_like(acc)
    for owner in range(groups):
        sel_ref[owner] = 0
    for index in range(slots // CHUNK):

        @pl.when(index * CHUNK < count)
        def _():
            chunk_copy(index).wait()

            def add_tile(slot, carry):
                source = src_ref[slot]
                owner = source // 2
                sel_ref[owner] = source - 2 * owner
                rows = pl.ds(pl.multiple_of(dst_ref[slot] * T, T), T)
                acc[owner, rows, :] = acc[owner, rows, :] + buf[slot]
                return carry

            lax.fori_loop(index * CHUNK, jnp.minimum(count, (index + 1) * CHUNK), add_tile, 0)

    total = acc[0]
    for owner in range(groups):
        if owner > 0:
            total = total + acc[owner]
        adj_ref[:, owner * T : (owner + 1) * T] = acc[owner].astype(F32).astype(BF16)
    degree = jnp.sum(total.astype(F32), axis=1, keepdims=True)
    inv_ref[...] = jnp.broadcast_to(1.0 / jnp.maximum(degree, 1.0), inv_ref.shape)
    row = lax.broadcasted_iota(jnp.int32, flag_ref.shape, 0)
    flags = jnp.zeros(flag_ref.shape, F32)
    for owner in range(groups):
        flags = jnp.where(row == owner, sel_ref[owner].astype(F32), flags)
    flag_ref[...] = flags.astype(BF16)


def neighbour_product_kernel(x_ref, w_ref, flag_ref, pay_ref):
    parts = x_ref.shape[0]
    rows = x_ref.shape[1]
    total = dot(x_ref[0], w_ref[0:T, :])
    for part in range(1, parts):
        total = total + dot(x_ref[part], w_ref[part * T : (part + 1) * T, :])
    product = total.astype(BF16)
    flags = flag_ref[...]
    for copy in range(pay_ref.shape[0]):
        pay_ref[copy, 0:rows, :] = product
        pay_ref[copy, rows:, :] = flags


def self_product_kernel(x_ref, w_ref, z_ref):
    parts = x_ref.shape[0]
    total = dot(x_ref[0], w_ref[0:T, :])
    for part in range(1, parts):
        total = total + dot(x_ref[part], w_ref[part * T : (part + 1) * T, :])
    z_ref[...] = total


def activation_kernel(
    place_ref, sel_ref, adj_ref, inv_ref, own_ref, other_ref, z_ref, og_ref,
    out_ref, gt_ref, pay_ref, mask_ref, chosen,
):
    core = place_ref[0]
    me = place_ref[1]
    rows = z_ref.shape[0]
    flag_rows = own_ref.shape[1] - rows
    row = lax.broadcasted_iota(jnp.int32, (flag_rows, T), 0)
    for chip in range(own_ref.shape[0]):
        for ref, owner in ((own_ref, 2 * chip + core), (other_ref, 2 * chip + 1 - core)):
            start = pl.multiple_of(sel_ref[owner] * T, T)
            chosen[pl.ds(pl.multiple_of(owner * T, T), T), :] = ref[chip, pl.ds(start, T), :]
            flags = ref[chip, rows:, :].astype(F32)
            mask_ref[pl.ds(owner, 1), :] = jnp.sum(jnp.where(row == me, flags, 0.0), axis=0, keepdims=True)
    adj = adj_ref[...]
    inverse = inv_ref[...]
    z = z_ref[...] + inverse * dot(adj, chosen[...])
    sig = 1.0 / (1.0 + jnp.exp(-z))
    out_ref[...] = (z * sig).astype(BF16)
    grad = (og_ref[...].astype(F32) * sig * (1.0 + z * (1.0 - sig))).astype(BF16).astype(F32)
    gt_ref[...] = grad.T.astype(BF16)
    scaled = (grad * inverse).T.astype(BF16)
    spread = dot(scaled, adj)
    for owner in range(pay_ref.shape[0]):
        pay_ref[owner] = spread[:, owner * T : (owner + 1) * T].astype(BF16)


def self_grad_kernel(gt_ref, x_ref, part_ref):
    gt = gt_ref[...]
    for part in range(x_ref.shape[0]):
        part_ref[part] = dot(gt, x_ref[part])


def feature_grad_kernel(came_ref, mask_ref, gt_ref, ws_ref, wn_ref, bt_ref, pay_ref):
    low = jnp.zeros((T, T), F32)
    high = jnp.zeros((T, T), F32)
    for sender in range(came_ref.shape[0]):
        came = came_ref[sender].astype(F32)
        is_high = mask_ref[sender : sender + 1, :] > 0.5
        low = low + jnp.where(is_high, 0.0, came)
        high = high + jnp.where(is_high, came, 0.0)
    bt = jnp.concatenate([low, high], axis=1).astype(BF16)
    bt_ref[...] = bt
    gt = gt_ref[...]
    for part in range(pay_ref.shape[0]):
        span = slice(part * T, (part + 1) * T)
        pay_ref[part] = (dot(ws_ref[span, :], gt) + dot(wn_ref[span, :], bt)).astype(BF16)


def neigh_grad_kernel(place_ref, bt_ref, x_ref, keep_ref, send_ref):
    core = place_ref[0]
    bt = bt_ref[...]
    for chip in range(keep_ref.shape[0]):
        keep_ref[chip] = dot(bt, x_ref[2 * chip + core])
        send_ref[chip] = dot(bt, x_ref[2 * chip + 1 - core]).astype(BF16)


def sum_kernel(parts_ref, out_ref):
    total = parts_ref[0].astype(F32)
    for part in range(1, parts_ref.shape[0]):
        total = total + parts_ref[part].astype(F32)
    out_ref[...] = total.T.astype(out_ref.dtype)


def call(kernel, ins, outs, in_specs=None, out_specs=None, scratch=()):
    shapes = tuple(jax.ShapeDtypeStruct(shape, dtype) for shape, dtype in outs)
    return pl.pallas_call(
        kernel,
        out_shape=shapes,
        in_specs=in_specs or [VMEM] * len(ins),
        out_specs=tuple(out_specs or [VMEM] * len(outs)),
        scratch_shapes=list(scratch),
        compiler_params=PARAMS,
        name=kernel.__name__,
    )(*ins)


def per_device(features, w_self, w_neigh, out_grad, tile_count, tile_dst, tile_src, tile_weight, chips, parts):
    rows = features.shape[0]
    groups = 2 * chips
    slots = tile_weight.shape[1]
    core = lax.axis_index("c")
    place = jnp.stack([core, lax.axis_index("z") * 2 + core]).astype(jnp.int32)
    swap = [(0, 1), (1, 0)]

    x_all = lax.all_to_all(
        jnp.broadcast_to(features[None], (parts, rows, T)), ("y", "x"), 0, 0, tiled=True
    )
    adj, inverse, flags, sel = call(
        adjacency_kernel,
        (tile_count, tile_dst[0], tile_src[0], tile_weight[0]),
        [((rows, groups * T), BF16), ((rows, T), F32), ((groups, T), BF16), ((groups,), jnp.int32)],
        in_specs=[SMEM, SMEM, SMEM, HBM],
        out_specs=[VMEM, VMEM, VMEM, SMEM],
        scratch=[
            pltpu.VMEM((slots, T, T), jnp.int32),
            pltpu.VMEM((groups, rows, T), jnp.int32),
            pltpu.SemaphoreType.DMA((slots // CHUNK,)),
        ],
    )
    (y_pay,) = call(
        neighbour_product_kernel, (x_all, w_neigh, flags), [((chips, rows + groups, T), BF16)]
    )
    y_own = lax.all_to_all(y_pay, "z", 0, 0, tiled=True)
    (z_self,) = call(self_product_kernel, (x_all, w_self), [((rows, T), F32)])
    y_other = lax.ppermute(y_own, "c", swap)
    output, gt, c_pay, mask = call(
        activation_kernel,
        (place, sel, adj, inverse, y_own, y_other, z_self, out_grad),
        [((rows, T), BF16), ((T, rows), BF16), ((groups, T, T), BF16), ((groups, T), F32)],
        in_specs=[SMEM, SMEM] + [VMEM] * 6,
        scratch=[pltpu.VMEM((groups * T, T), BF16)],
    )
    c_all = lax.all_to_all(c_pay, ("z", "c"), 0, 0, tiled=True)
    (self_part,) = call(self_grad_kernel, (gt, x_all), [((groups, T, T), F32)])
    grad_self = lax.psum_scatter(self_part, ("z", "c"), scatter_dimension=0, tiled=True)[0].T
    bt, p_pay = call(
        feature_grad_kernel,
        (c_all, mask, gt, w_self, w_neigh),
        [((T, rows), BF16), ((parts, T, rows), BF16)],
    )
    p_all = lax.all_to_all(p_pay, ("y", "x"), 0, 0, tiled=True)
    keep, send = call(
        neigh_grad_kernel,
        (place, bt, x_all),
        [((chips, T, T), F32), ((chips, T, T), BF16)],
        in_specs=[SMEM, VMEM, VMEM],
    )
    came = lax.ppermute(send, "c", swap)
    n_all = lax.all_to_all((keep + came.astype(F32)).astype(BF16), "z", 0, 0, tiled=True)
    (grad_features,) = call(sum_kernel, (p_all,), [((rows, T), BF16)])
    (grad_neigh,) = call(sum_kernel, (n_all,), [((T, T), F32)])
    return output, grad_features, grad_self, grad_neigh


def solution(mesh):
    row_count, part_count = mesh.shape["rows"], mesh.shape["feat"]
    split = Mesh(mesh.devices.reshape(row_count // 2, 2, 4, part_count // 4), ("z", "c", "y", "x"))
    rows, feat = ("z", "c"), ("y", "x")
    return jax.shard_map(
        functools.partial(per_device, chips=row_count // 2, parts=part_count),
        mesh=split,
        in_specs=(
            P(rows, feat),
            P(None, feat),
            P(None, feat),
            P(rows, feat),
            P(rows),
            P(rows, None),
            P(rows, None),
            P(rows, None, None, None),
        ),
        out_specs=(P(rows, feat),) * 4,
        check_vma=False,
    )
```

```python
import functools

import jax
import jax.numpy as jnp
from jax import lax
from jax.experimental import pallas as pl
from jax.experimental.pallas import tpu as pltpu
from jax.sharding import Mesh, PartitionSpec as P

F32 = jnp.float32
BF16 = jnp.bfloat16
T = 128
CHUNK = 10
LIMIT = 48 * 1024 * 1024
VMEM = pl.BlockSpec(memory_space=pltpu.VMEM)
SMEM = pl.BlockSpec(memory_space=pltpu.SMEM)
HBM = pl.BlockSpec(memory_space=pl.ANY)
PARAMS = pltpu.CompilerParams(vmem_limit_bytes=LIMIT)


def dot(a, b):
    return jnp.dot(a, b, preferred_element_type=F32)


def halves(block):
    high = block.astype(BF16)
    return jnp.concatenate([high, (block - high.astype(F32)).astype(BF16)], axis=0)


def adjacency_kernel(count_ref, dst_ref, src_ref, weight_ref, adj_ref, inv_ref, flag_ref, sel_ref, buf, acc, sems):
    count = count_ref[0]
    slots = weight_ref.shape[0]
    groups = acc.shape[0]

    def chunk_copy(index):
        part = pl.ds(index * CHUNK, CHUNK)
        return pltpu.make_async_copy(weight_ref.at[part], buf.at[part], sems.at[index])

    for index in range(slots // CHUNK):

        @pl.when(index * CHUNK < count)
        def _():
            chunk_copy(index).start()

    acc[...] = jnp.zeros_like(acc)
    for owner in range(groups):
        sel_ref[owner] = 0
    for index in range(slots // CHUNK):

        @pl.when(index * CHUNK < count)
        def _():
            chunk_copy(index).wait()

            def add_tile(slot, carry):
                source = src_ref[slot]
                owner = source // 2
                sel_ref[owner] = source - 2 * owner
                rows = pl.ds(pl.multiple_of(dst_ref[slot] * T, T), T)
                acc[owner, rows, :] = acc[owner, rows, :] + buf[slot]
                return carry

            lax.fori_loop(index * CHUNK, jnp.minimum(count, (index + 1) * CHUNK), add_tile, 0)

    total = acc[0]
    for owner in range(groups):
        if owner > 0:
            total = total + acc[owner]
        adj_ref[:, owner * T : (owner + 1) * T] = acc[owner].astype(F32).astype(BF16)
    degree = jnp.sum(total.astype(F32), axis=1, keepdims=True)
    inv_ref[...] = jnp.broadcast_to(1.0 / jnp.maximum(degree, 1.0), inv_ref.shape)
    row = lax.broadcasted_iota(jnp.int32, flag_ref.shape, 0)
    flags = jnp.zeros(flag_ref.shape, F32)
    for owner in range(groups):
        flags = jnp.where(row == owner, sel_ref[owner].astype(F32), flags)
    flag_ref[...] = flags.astype(BF16)


def spread_kernel(x_ref, pay_ref):
    block = x_ref[...]
    for copy in range(pay_ref.shape[0]):
        pay_ref[copy] = block


def neighbour_product_kernel(x_ref, w_ref, flag_ref, pay_ref):
    parts = x_ref.shape[0]
    rows = x_ref.shape[1]
    total = dot(x_ref[0], w_ref[0:T, :])
    for part in range(1, parts):
        total = total + dot(x_ref[part], w_ref[part * T : (part + 1) * T, :])
    product = total.astype(BF16)
    flags = flag_ref[...]
    for copy in range(pay_ref.shape[0]):
        pay_ref[copy, 0:rows, :] = product
        pay_ref[copy, rows:, :] = flags


def self_product_kernel(x_ref, w_ref, z_ref):
    parts = x_ref.shape[0]
    total = dot(x_ref[0], w_ref[0:T, :])
    for part in range(1, parts):
        total = total + dot(x_ref[part], w_ref[part * T : (part + 1) * T, :])
    z_ref[...] = total


def activation_kernel(
    place_ref, sel_ref, adj_ref, inv_ref, own_ref, other_ref, z_ref, og_ref,
    out_ref, gt_ref, pay_ref, mask_ref, chosen,
):
    core = place_ref[0]
    me = place_ref[1]
    rows = z_ref.shape[0]
    flag_rows = own_ref.shape[1] - rows
    row = lax.broadcasted_iota(jnp.int32, (flag_rows, T), 0)
    for chip in range(own_ref.shape[0]):
        for ref, owner in ((own_ref, 2 * chip + core), (other_ref, 2 * chip + 1 - core)):
            start = pl.multiple_of(sel_ref[owner] * T, T)
            chosen[pl.ds(pl.multiple_of(owner * T, T), T), :] = ref[chip, pl.ds(start, T), :]
            flags = ref[chip, rows:, :].astype(F32)
            mask_ref[pl.ds(owner, 1), :] = jnp.sum(jnp.where(row == me, flags, 0.0), axis=0, keepdims=True)
    adj = adj_ref[...]
    inverse = inv_ref[...]
    z = z_ref[...] + inverse * dot(adj, chosen[...])
    sig = 1.0 / (1.0 + jnp.exp(-z))
    out_ref[...] = (z * sig).astype(BF16)
    grad = (og_ref[...].astype(F32) * sig * (1.0 + z * (1.0 - sig))).astype(BF16).astype(F32)
    gt_ref[...] = grad.T.astype(BF16)
    spread = dot(halves((grad * inverse).T), adj)
    spread = spread[0:T] + spread[T:]
    for owner in range(pay_ref.shape[0]):
        pay_ref[owner] = spread[:, owner * T : (owner + 1) * T].astype(BF16)


def feature_grad_kernel(came_ref, mask_ref, gt_ref, ws_ref, wn_ref, bt_ref, pay_ref):
    low = jnp.zeros((T, T), F32)
    high = jnp.zeros((T, T), F32)
    for sender in range(came_ref.shape[0]):
        came = came_ref[sender].astype(F32)
        is_high = mask_ref[sender : sender + 1, :] > 0.5
        low = low + jnp.where(is_high, 0.0, came)
        high = high + jnp.where(is_high, came, 0.0)
    both = halves(jnp.concatenate([low, high], axis=1))
    bt = both[0:T]
    bt_ref[...] = both
    gt = gt_ref[...]
    for part in range(pay_ref.shape[0]):
        span = slice(part * T, (part + 1) * T)
        pay_ref[part] = (dot(ws_ref[span, :], gt) + dot(wn_ref[span, :], bt)).astype(BF16)


def weight_grad_kernel(place_ref, gt_ref, bt_ref, x_ref, keep_ref, send_ref):
    core = place_ref[0]
    left = jnp.concatenate([gt_ref[...], bt_ref[...]], axis=0)
    for chip in range(keep_ref.shape[0]):
        kept = dot(left, x_ref[2 * chip + core])
        sent = dot(left, x_ref[2 * chip + 1 - core])
        keep_ref[chip, 0:T] = kept[0:T]
        keep_ref[chip, T:] = kept[T : 2 * T] + kept[2 * T :]
        send_ref[chip, 0:T] = sent[0:T].astype(BF16)
        send_ref[chip, T:] = (sent[T : 2 * T] + sent[2 * T :]).astype(BF16)


def pair_kernel(keep_ref, came_ref, pay_ref):
    pay_ref[...] = (keep_ref[...] + came_ref[...].astype(F32)).astype(BF16)


def weight_sum_kernel(parts_ref, self_ref, neigh_ref):
    total = parts_ref[0].astype(F32)
    for part in range(1, parts_ref.shape[0]):
        total = total + parts_ref[part].astype(F32)
    self_ref[...] = total[0:T].T
    neigh_ref[...] = total[T:].T


def sum_kernel(parts_ref, out_ref):
    total = parts_ref[0].astype(F32)
    for part in range(1, parts_ref.shape[0]):
        total = total + parts_ref[part].astype(F32)
    out_ref[...] = total.T.astype(out_ref.dtype)


def call(kernel, ins, outs, in_specs=None, out_specs=None, scratch=()):
    shapes = tuple(jax.ShapeDtypeStruct(shape, dtype) for shape, dtype in outs)
    return pl.pallas_call(
        kernel,
        out_shape=shapes,
        in_specs=in_specs or [VMEM] * len(ins),
        out_specs=tuple(out_specs or [VMEM] * len(outs)),
        scratch_shapes=list(scratch),
        compiler_params=PARAMS,
        name=kernel.__name__,
    )(*ins)


def per_device(features, w_self, w_neigh, out_grad, tile_count, tile_dst, tile_src, tile_weight, chips, parts):
    rows = features.shape[0]
    groups = 2 * chips
    slots = tile_weight.shape[1]
    core = lax.axis_index("c")
    place = jnp.stack([core, lax.axis_index("z") * 2 + core]).astype(jnp.int32)
    swap = [(0, 1), (1, 0)]

    (x_pay,) = call(spread_kernel, (features,), [((parts, rows, T), BF16)])
    x_all = lax.all_to_all(x_pay, ("y", "x"), 0, 0, tiled=True)
    adj, inverse, flags, sel = call(
        adjacency_kernel,
        (tile_count, tile_dst[0], tile_src[0], tile_weight[0]),
        [((rows, groups * T), BF16), ((rows, T), F32), ((groups, T), BF16), ((groups,), jnp.int32)],
        in_specs=[SMEM, SMEM, SMEM, HBM],
        out_specs=[VMEM, VMEM, VMEM, SMEM],
        scratch=[
            pltpu.VMEM((slots, T, T), jnp.int32),
            pltpu.VMEM((groups, rows, T), jnp.int32),
            pltpu.SemaphoreType.DMA((slots // CHUNK,)),
        ],
    )
    (y_pay,) = call(
        neighbour_product_kernel, (x_all, w_neigh, flags), [((chips, rows + groups, T), BF16)]
    )
    y_own = lax.all_to_all(y_pay, "z", 0, 0, tiled=True)
    (z_self,) = call(self_product_kernel, (x_all, w_self), [((rows, T), F32)])
    y_other = lax.ppermute(y_own, "c", swap)
    output, gt, c_pay, mask = call(
        activation_kernel,
        (place, sel, adj, inverse, y_own, y_other, z_self, out_grad),
        [((rows, T), BF16), ((T, rows), BF16), ((groups, T, T), BF16), ((groups, T), F32)],
        in_specs=[SMEM, SMEM] + [VMEM] * 6,
        scratch=[pltpu.VMEM((groups * T, T), BF16)],
    )
    c_all = lax.all_to_all(c_pay, ("z", "c"), 0, 0, tiled=True)
    bt, p_pay = call(
        feature_grad_kernel,
        (c_all, mask, gt, w_self, w_neigh),
        [((2 * T, rows), BF16), ((parts, T, rows), BF16)],
    )
    p_all = lax.all_to_all(p_pay, ("y", "x"), 0, 0, tiled=True)
    keep, send = call(
        weight_grad_kernel,
        (place, gt, bt, x_all),
        [((chips, 2 * T, T), F32), ((chips, 2 * T, T), BF16)],
        in_specs=[SMEM, VMEM, VMEM, VMEM],
    )
    came = lax.ppermute(send, "c", swap)
    (w_pay,) = call(pair_kernel, (keep, came), [((chips, 2 * T, T), BF16)])
    w_all = lax.all_to_all(w_pay, "z", 0, 0, tiled=True)
    (grad_features,) = call(sum_kernel, (p_all,), [((rows, T), BF16)])
    grad_self, grad_neigh = call(weight_sum_kernel, (w_all,), [((T, T), F32)] * 2)
    return output, grad_features, grad_self, grad_neigh


def solution(mesh):
    row_count, part_count = mesh.shape["rows"], mesh.shape["feat"]
    split = Mesh(mesh.devices.reshape(row_count // 2, 2, 4, part_count // 4), ("z", "c", "y", "x"))
    rows, feat = ("z", "c"), ("y", "x")
    return jax.shard_map(
        functools.partial(per_device, chips=row_count // 2, parts=part_count),
        mesh=split,
        in_specs=(
            P(rows, feat),
            P(None, feat),
            P(None, feat),
            P(rows, feat),
            P(rows),
            P(rows, None),
            P(rows, None),
            P(rows, None, None, None),
        ),
        out_specs=(P(rows, feat),) * 4,
        check_vma=False,
    )
```

```python
import functools

import jax
import jax.numpy as jnp
from jax import lax
from jax.experimental import pallas as pl
from jax.experimental.pallas import tpu as pltpu
from jax.sharding import Mesh, PartitionSpec as P

F32 = jnp.float32
BF16 = jnp.bfloat16
T = 128
CHUNK = 10
MIB = 1024 * 1024
VMEM = pl.BlockSpec(memory_space=pltpu.VMEM)
SMEM = pl.BlockSpec(memory_space=pltpu.SMEM)
ANY = pl.BlockSpec(memory_space=pl.ANY)
HBM = pl.BlockSpec(memory_space=pltpu.HBM)


def dot(a, b):
    return jnp.dot(a, b, preferred_element_type=F32)


def halves(block):
    high = block.astype(BF16)
    return jnp.concatenate([high, (block - high.astype(F32)).astype(BF16)], axis=0)


def adjacency_kernel(count_ref, dst_ref, src_ref, weight_ref, adj_ref, inv_ref, flag_ref, sel_ref, buf, acc, sems):
    count = count_ref[0]
    slots = weight_ref.shape[0]
    groups = acc.shape[0]

    def chunk_copy(index):
        part = pl.ds(index * CHUNK, CHUNK)
        return pltpu.make_async_copy(weight_ref.at[part], buf.at[part], sems.at[index])

    for index in range(slots // CHUNK):

        @pl.when(index * CHUNK < count)
        def _():
            chunk_copy(index).start()

    acc[...] = jnp.zeros_like(acc)
    for owner in range(groups):
        sel_ref[owner] = 0
    for index in range(slots // CHUNK):

        @pl.when(index * CHUNK < count)
        def _():
            chunk_copy(index).wait()

            def add_tile(slot, carry):
                source = src_ref[slot]
                owner = source // 2
                sel_ref[owner] = source - 2 * owner
                rows = pl.ds(pl.multiple_of(dst_ref[slot] * T, T), T)
                acc[owner, rows, :] = acc[owner, rows, :] + buf[slot]
                return carry

            lax.fori_loop(index * CHUNK, jnp.minimum(count, (index + 1) * CHUNK), add_tile, 0)

    total = acc[0]
    for owner in range(groups):
        if owner > 0:
            total = total + acc[owner]
        adj_ref[:, owner * T : (owner + 1) * T] = acc[owner].astype(F32).astype(BF16)
    degree = jnp.sum(total.astype(F32), axis=1, keepdims=True)
    inv_ref[...] = jnp.broadcast_to(1.0 / jnp.maximum(degree, 1.0), inv_ref.shape)
    row = lax.broadcasted_iota(jnp.int32, flag_ref.shape, 0)
    flags = jnp.zeros(flag_ref.shape, F32)
    for owner in range(groups):
        flags = jnp.where(row == owner, sel_ref[owner].astype(F32), flags)
    flag_ref[...] = flags.astype(BF16)


def spread_kernel(x_ref, pay_ref, sems):
    copies = [
        pltpu.make_async_copy(x_ref, pay_ref.at[copy], sems.at[copy]) for copy in range(pay_ref.shape[0])
    ]
    for copy in copies:
        copy.start()
    for copy in copies:
        copy.wait()


def neighbour_product_kernel(x_ref, w_ref, flag_ref, pay_ref):
    parts = x_ref.shape[0]
    rows = x_ref.shape[1]
    total = dot(x_ref[0], w_ref[0:T, :])
    for part in range(1, parts):
        total = total + dot(x_ref[part], w_ref[part * T : (part + 1) * T, :])
    product = total.astype(BF16)
    flags = flag_ref[...]
    for copy in range(pay_ref.shape[0]):
        pay_ref[copy, 0:rows, :] = product
        pay_ref[copy, rows:, :] = flags


def self_product_kernel(x_ref, w_ref, z_ref):
    parts = x_ref.shape[0]
    total = dot(x_ref[0], w_ref[0:T, :])
    for part in range(1, parts):
        total = total + dot(x_ref[part], w_ref[part * T : (part + 1) * T, :])
    z_ref[...] = total


def activation_kernel(
    place_ref, sel_ref, adj_ref, inv_ref, own_ref, other_ref, z_ref, og_ref,
    out_ref, gt_ref, pay_ref, mask_ref, chosen,
):
    core = place_ref[0]
    me = place_ref[1]
    rows = z_ref.shape[0]
    flag_rows = own_ref.shape[1] - rows
    row = lax.broadcasted_iota(jnp.int32, (flag_rows, T), 0)
    for chip in range(own_ref.shape[0]):
        for ref, owner in ((own_ref, 2 * chip + core), (other_ref, 2 * chip + 1 - core)):
            start = pl.multiple_of(sel_ref[owner] * T, T)
            chosen[pl.ds(pl.multiple_of(owner * T, T), T), :] = ref[chip, pl.ds(start, T), :]
            flags = ref[chip, rows:, :].astype(F32)
            mask_ref[pl.ds(owner, 1), :] = jnp.sum(jnp.where(row == me, flags, 0.0), axis=0, keepdims=True)
    adj = adj_ref[...]
    inverse = inv_ref[...]
    z = z_ref[...] + inverse * dot(adj, chosen[...])
    sig = 1.0 / (1.0 + jnp.exp(-z))
    out_ref[...] = (z * sig).astype(BF16)
    grad = (og_ref[...].astype(F32) * sig * (1.0 + z * (1.0 - sig))).astype(BF16).astype(F32)
    gt_ref[...] = grad.T.astype(BF16)
    spread = dot(halves((grad * inverse).T), adj)
    spread = spread[0:T] + spread[T:]
    for owner in range(pay_ref.shape[0]):
        pay_ref[owner] = spread[:, owner * T : (owner + 1) * T].astype(BF16)


def feature_grad_kernel(came_ref, mask_ref, gt_ref, ws_ref, wn_ref, bt_ref, pay_ref, buf, sems):
    low = jnp.zeros((T, T), F32)
    high = jnp.zeros((T, T), F32)
    for sender in range(came_ref.shape[0]):
        came = came_ref[sender].astype(F32)
        is_high = mask_ref[sender : sender + 1, :] > 0.5
        low = low + jnp.where(is_high, 0.0, came)
        high = high + jnp.where(is_high, came, 0.0)
    both = halves(jnp.concatenate([low, high], axis=1))
    bt = both[0:T]
    bt_ref[...] = both
    gt = gt_ref[...]
    copies = []
    for part in range(pay_ref.shape[0]):
        span = slice(part * T, (part + 1) * T)
        buf[part] = (dot(ws_ref[span, :], gt) + dot(wn_ref[span, :], bt)).astype(BF16)
        copies.append(pltpu.make_async_copy(buf.at[part], pay_ref.at[part], sems.at[part]))
        copies[-1].start()
    for copy in copies:
        copy.wait()


def weight_grad_kernel(place_ref, gt_ref, bt_ref, x_ref, keep_ref, send_ref):
    core = place_ref[0]
    here = place_ref[2]
    chips = keep_ref.shape[0]
    left = jnp.concatenate([gt_ref[...], bt_ref[...]], axis=0)
    for step in range(chips):
        chip = lax.rem(here + step, chips)
        kept = dot(left, x_ref[2 * chip + core])
        sent = dot(left, x_ref[2 * chip + 1 - core])
        keep_ref[step, 0:T] = kept[0:T]
        keep_ref[step, T:] = kept[T : 2 * T] + kept[2 * T :]
        send_ref[step, 0:T] = sent[0:T].astype(BF16)
        send_ref[step, T:] = (sent[T : 2 * T] + sent[2 * T :]).astype(BF16)


def pair_kernel(keep_ref, came_ref, own_ref, *pay_refs):
    own_ref[...] = keep_ref[0] + came_ref[0].astype(F32)
    for step, pay_ref in enumerate(pay_refs, 1):
        pay_ref[...] = (keep_ref[step] + came_ref[step].astype(F32)).astype(BF16)


def weight_sum_kernel(own_ref, *refs):
    parts, (self_ref, neigh_ref) = refs[:-2], refs[-2:]
    total = own_ref[...]
    for part in parts:
        total = total + part[...].astype(F32)
    self_ref[...] = total[0:T].T
    neigh_ref[...] = total[T:].T


def sum_kernel(parts_ref, out_ref):
    total = parts_ref[0].astype(F32)
    for part in range(1, parts_ref.shape[0]):
        total = total + parts_ref[part].astype(F32)
    out_ref[...] = total.T.astype(out_ref.dtype)


def call(kernel, ins, outs, in_specs=None, out_specs=None, scratch=(), limit=12):
    shapes = tuple(jax.ShapeDtypeStruct(shape, dtype) for shape, dtype in outs)
    return pl.pallas_call(
        kernel,
        out_shape=shapes,
        in_specs=in_specs or [VMEM] * len(ins),
        out_specs=tuple(out_specs or [VMEM] * len(outs)),
        scratch_shapes=list(scratch),
        compiler_params=pltpu.CompilerParams(vmem_limit_bytes=limit * MIB),
        name=kernel.__name__,
    )(*ins)


def per_device(features, w_self, w_neigh, out_grad, tile_count, tile_dst, tile_src, tile_weight, chips, parts):
    rows = features.shape[0]
    groups = 2 * chips
    slots = tile_weight.shape[1]
    core = lax.axis_index("c")
    here = lax.axis_index("z")
    place = jnp.stack([core, here * 2 + core, here]).astype(jnp.int32)
    swap = [(0, 1), (1, 0)]

    (x_pay,) = call(
        spread_kernel,
        (features,),
        [((parts, rows, T), BF16)],
        in_specs=[ANY],
        out_specs=[HBM],
        scratch=[pltpu.SemaphoreType.DMA((parts,))],
    )
    x_all = lax.all_to_all(x_pay, ("y", "x"), 0, 0, tiled=True)
    adj, inverse, flags, sel = call(
        adjacency_kernel,
        (tile_count, tile_dst[0], tile_src[0], tile_weight[0]),
        [((rows, groups * T), BF16), ((rows, T), F32), ((groups, T), BF16), ((groups,), jnp.int32)],
        in_specs=[SMEM, SMEM, SMEM, ANY],
        out_specs=[VMEM, VMEM, VMEM, SMEM],
        scratch=[
            pltpu.VMEM((slots, T, T), jnp.int32),
            pltpu.VMEM((groups, rows, T), jnp.int32),
            pltpu.SemaphoreType.DMA((slots // CHUNK,)),
        ],
        limit=20,
    )
    (y_pay,) = call(
        neighbour_product_kernel, (x_all, w_neigh, flags), [((chips, rows + groups, T), BF16)]
    )
    y_own = lax.all_to_all(y_pay, "z", 0, 0, tiled=True)
    (z_self,) = call(self_product_kernel, (x_all, w_self), [((rows, T), F32)])
    y_other = lax.ppermute(y_own, "c", swap)
    output, gt, c_pay, mask = call(
        activation_kernel,
        (place, sel, adj, inverse, y_own, y_other, z_self, out_grad),
        [((rows, T), BF16), ((T, rows), BF16), ((groups, T, T), BF16), ((groups, T), F32)],
        in_specs=[SMEM, SMEM] + [VMEM] * 6,
        scratch=[pltpu.VMEM((groups * T, T), BF16)],
    )
    c_all = lax.all_to_all(c_pay, ("z", "c"), 0, 0, tiled=True)
    bt, p_pay = call(
        feature_grad_kernel,
        (c_all, mask, gt, w_self, w_neigh),
        [((2 * T, rows), BF16), ((parts, T, rows), BF16)],
        out_specs=[VMEM, HBM],
        scratch=[pltpu.VMEM((parts, T, rows), BF16), pltpu.SemaphoreType.DMA((parts,))],
    )
    p_all = lax.all_to_all(p_pay, ("y", "x"), 0, 0, tiled=True)
    keep, send = call(
        weight_grad_kernel,
        (place, gt, bt, x_all),
        [((chips, 2 * T, T), F32), ((chips, 2 * T, T), BF16)],
        in_specs=[SMEM, VMEM, VMEM, VMEM],
    )
    came = lax.ppermute(send, "c", swap)
    own, *w_pay = call(
        pair_kernel,
        (keep, came),
        [((2 * T, T), F32)] + [((2 * T, T), BF16)] * (chips - 1),
    )
    w_came = [
        lax.ppermute(block, "z", [(chip, (chip + step) % chips) for chip in range(chips)])
        for step, block in enumerate(w_pay, 1)
    ]
    (grad_features,) = call(sum_kernel, (p_all,), [((rows, T), BF16)])
    grad_self, grad_neigh = call(weight_sum_kernel, (own, *w_came), [((T, T), F32)] * 2)
    return output, grad_features, grad_self, grad_neigh


def solution(mesh):
    row_count, part_count = mesh.shape["rows"], mesh.shape["feat"]
    split = Mesh(mesh.devices.reshape(row_count // 2, 2, 4, part_count // 4), ("z", "c", "y", "x"))
    rows, feat = ("z", "c"), ("y", "x")
    return jax.shard_map(
        functools.partial(per_device, chips=row_count // 2, parts=part_count),
        mesh=split,
        in_specs=(
            P(rows, feat),
            P(None, feat),
            P(None, feat),
            P(rows, feat),
            P(rows),
            P(rows, None),
            P(rows, None),
            P(rows, None, None, None),
        ),
        out_specs=(P(rows, feat),) * 4,
        check_vma=False,
    )
```

```python
import functools

import jax
import jax.numpy as jnp
from jax import lax
from jax.experimental import pallas as pl
from jax.experimental.pallas import tpu as pltpu
from jax.sharding import Mesh, PartitionSpec as P

F32 = jnp.float32
BF16 = jnp.bfloat16
T = 128
CHUNK = 10
MIB = 1024 * 1024
VMEM = pl.BlockSpec(memory_space=pltpu.VMEM)
SMEM = pl.BlockSpec(memory_space=pltpu.SMEM)
ANY = pl.BlockSpec(memory_space=pl.ANY)
HBM = pl.BlockSpec(memory_space=pltpu.HBM)


def dot(a, b):
    return jnp.dot(a, b, preferred_element_type=F32)


def far_first(chips):
    return tuple(sorted(range(1, chips), key=lambda step: abs(step - chips // 2)))


def halves(block):
    high = block.astype(BF16)
    return jnp.concatenate([high, (block - high.astype(F32)).astype(BF16)], axis=0)


def adjacency_kernel(count_ref, dst_ref, src_ref, weight_ref, adj_ref, inv_ref, flag_ref, sel_ref, buf, acc, sems):
    count = count_ref[0]
    slots = weight_ref.shape[0]
    groups = acc.shape[0]

    def chunk_copy(index):
        part = pl.ds(index * CHUNK, CHUNK)
        return pltpu.make_async_copy(weight_ref.at[part], buf.at[part], sems.at[index])

    for index in range(slots // CHUNK):

        @pl.when(index * CHUNK < count)
        def _():
            chunk_copy(index).start()

    acc[...] = jnp.zeros_like(acc)
    for owner in range(groups):
        sel_ref[owner] = 0
    for index in range(slots // CHUNK):

        @pl.when(index * CHUNK < count)
        def _():
            chunk_copy(index).wait()

            def add_tile(slot, carry):
                source = src_ref[0, slot]
                owner = source // 2
                sel_ref[owner] = source - 2 * owner
                rows = pl.ds(pl.multiple_of(dst_ref[0, slot] * T, T), T)
                acc[owner, rows, :] = acc[owner, rows, :] + buf[slot]
                return carry

            lax.fori_loop(index * CHUNK, jnp.minimum(count, (index + 1) * CHUNK), add_tile, 0)

    total = acc[0]
    for owner in range(groups):
        if owner > 0:
            total = total + acc[owner]
        adj_ref[owner] = acc[owner].astype(F32).astype(BF16)
    degree = jnp.sum(total.astype(F32), axis=1, keepdims=True)
    inv_ref[...] = jnp.broadcast_to(1.0 / jnp.maximum(degree, 1.0), inv_ref.shape)
    row = lax.broadcasted_iota(jnp.int32, flag_ref.shape, 0)
    flags = jnp.zeros(flag_ref.shape, F32)
    for owner in range(groups):
        flags = jnp.where(row == owner, sel_ref[owner].astype(F32), flags)
    flag_ref[...] = flags.astype(BF16)


def spread_kernel(x_ref, pay_ref, sems):
    copies = [
        pltpu.make_async_copy(x_ref, pay_ref.at[copy], sems.at[copy]) for copy in range(pay_ref.shape[0])
    ]
    for copy in copies:
        copy.start()
    for copy in copies:
        copy.wait()


def neighbour_product_kernel(x_ref, w_ref, flag_ref, pay_ref):
    parts = x_ref.shape[0]
    rows = x_ref.shape[1]
    total = dot(x_ref[0], w_ref[0:T, :])
    for part in range(1, parts):
        total = total + dot(x_ref[part], w_ref[part * T : (part + 1) * T, :])
    product = total.astype(BF16)
    flags = flag_ref[...]
    for copy in range(pay_ref.shape[0]):
        pay_ref[copy, 0:rows, :] = product
        pay_ref[copy, rows:, :] = flags


def chosen_tile(ref, sel_ref, chip, owner):
    return ref[chip, pl.ds(pl.multiple_of(sel_ref[owner] * T, T), T), :]


def half_kernel(place_ref, sel_ref, x_ref, w_ref, adj_ref, inv_ref, own_ref, z_ref):
    core = place_ref[0]
    total = dot(x_ref[0], w_ref[0:T, :])
    for part in range(1, x_ref.shape[0]):
        total = total + dot(x_ref[part], w_ref[part * T : (part + 1) * T, :])
    summed = jnp.zeros(z_ref.shape, F32)
    for chip in range(own_ref.shape[0]):
        owner = 2 * chip + core
        summed = summed + dot(adj_ref[owner], chosen_tile(own_ref, sel_ref, chip, owner))
    z_ref[...] = total + inv_ref[...] * summed


def activation_kernel(
    place_ref, sel_ref, adj_ref, inv_ref, other_ref, z_ref, og_ref, x_ref, out_ref, gt_ref, pay_ref, x_same_ref
):
    core = place_ref[0]
    summed = jnp.zeros(z_ref.shape, F32)
    for chip in range(other_ref.shape[0]):
        owner = 2 * chip + 1 - core
        summed = summed + dot(adj_ref[owner], chosen_tile(other_ref, sel_ref, chip, owner))
    inverse = inv_ref[...]
    z = z_ref[...] + inverse * summed
    sig = 1.0 / (1.0 + jnp.exp(-z))
    grad = (og_ref[...].astype(F32) * sig * (1.0 + z * (1.0 - sig))).astype(BF16).astype(F32)
    scaled = halves((grad * inverse).T)
    for owner in range(pay_ref.shape[0]):
        spread = dot(scaled, adj_ref[owner])
        pay_ref[owner] = (spread[0:T] + spread[T:]).astype(BF16)
    out_ref[...] = (z * sig).astype(BF16)
    gt_ref[...] = grad.T.astype(BF16)


def mask_kernel(place_ref, own_ref, other_ref, mask_ref):
    core = place_ref[0]
    me = place_ref[1]
    flag_rows = mask_ref.shape[0]
    start = own_ref.shape[1] - flag_rows
    row = lax.broadcasted_iota(jnp.int32, (flag_rows, T), 0)
    for chip in range(own_ref.shape[0]):
        for ref, owner in ((own_ref, 2 * chip + core), (other_ref, 2 * chip + 1 - core)):
            flags = ref[chip, start:, :].astype(F32)
            mask_ref[pl.ds(owner, 1), :] = jnp.sum(jnp.where(row == me, flags, 0.0), axis=0, keepdims=True)


def feature_grad_kernel(came_ref, mask_ref, gt_ref, ws_ref, wn_ref, bt_ref, pay_ref, buf, sems):
    low = jnp.zeros((T, T), F32)
    high = jnp.zeros((T, T), F32)
    for sender in range(came_ref.shape[0]):
        came = came_ref[sender].astype(F32)
        is_high = mask_ref[sender : sender + 1, :] > 0.5
        low = low + jnp.where(is_high, 0.0, came)
        high = high + jnp.where(is_high, came, 0.0)
    both = halves(jnp.concatenate([low, high], axis=1))
    bt = both[0:T]
    bt_ref[...] = both
    gt = gt_ref[...]
    copies = []
    for part in range(pay_ref.shape[0]):
        span = slice(part * T, (part + 1) * T)
        buf[part] = (dot(ws_ref[span, :], gt) + dot(wn_ref[span, :], bt)).astype(BF16)
        copies.append(pltpu.make_async_copy(buf.at[part], pay_ref.at[part], sems.at[part]))
        copies[-1].start()
    for copy in copies:
        copy.wait()


def weight_grad_kernel(place_ref, gt_ref, bt_ref, gt_pair_ref, bt_pair_ref, x_ref, x_pair_ref, own_ref, *pay_refs):
    core = place_ref[0]
    here = place_ref[2]
    chips = len(pay_refs) + 1
    left = jnp.concatenate([gt_ref[...], bt_ref[...]], axis=0)
    left_pair = jnp.concatenate([gt_pair_ref[...], bt_pair_ref[...]], axis=0)
    for step, pay_ref in zip(far_first(chips) + (0,), pay_refs + (own_ref,)):
        owner = 2 * lax.rem(here + step, chips) + core
        total = dot(left, x_ref[owner]) + dot(left_pair, x_pair_ref[owner])
        pay_ref[0:T] = total[0:T].astype(pay_ref.dtype)
        pay_ref[T:] = (total[T : 2 * T] + total[2 * T :]).astype(pay_ref.dtype)


def weight_sum_kernel(own_ref, *refs):
    parts, (self_ref, neigh_ref) = refs[:-2], refs[-2:]
    total = own_ref[...]
    for part in parts:
        total = total + part[...].astype(F32)
    self_ref[...] = total[0:T].T
    neigh_ref[...] = total[T:].T


def sum_kernel(parts_ref, out_ref):
    total = parts_ref[0].astype(F32)
    for part in range(1, parts_ref.shape[0]):
        total = total + parts_ref[part].astype(F32)
    out_ref[...] = total.T.astype(out_ref.dtype)


def call(kernel, ins, outs, in_specs=None, out_specs=None, scratch=(), limit=12, aliases=None):
    shapes = tuple(
        pltpu.HBM(shape, dtype) if spec is HBM else jax.ShapeDtypeStruct(shape, dtype)
        for (shape, dtype), spec in zip(outs, out_specs or [VMEM] * len(outs))
    )
    ins = [
        pltpu.with_memory_space_constraint(value, pltpu.HBM) if spec is HBM else value
        for value, spec in zip(ins, in_specs or [VMEM] * len(ins))
    ]
    return pl.pallas_call(
        kernel,
        out_shape=shapes,
        in_specs=in_specs or [VMEM] * len(ins),
        out_specs=tuple(out_specs or [VMEM] * len(outs)),
        scratch_shapes=list(scratch),
        input_output_aliases=aliases or {},
        compiler_params=pltpu.CompilerParams(vmem_limit_bytes=limit * MIB),
        name=kernel.__name__,
    )(*ins)


def per_device(features, w_self, w_neigh, out_grad, tile_count, tile_dst, tile_src, tile_weight, chips, parts):
    rows = features.shape[0]
    groups = 2 * chips
    slots = tile_weight.shape[1]
    core = lax.axis_index("c")
    here = lax.axis_index("z")
    place = jnp.stack([core, here * 2 + core, here]).astype(jnp.int32)
    swap = [(0, 1), (1, 0)]

    (x_pay,) = call(
        spread_kernel,
        (features,),
        [((parts, rows, T), BF16)],
        in_specs=[HBM],
        out_specs=[HBM],
        scratch=[pltpu.SemaphoreType.DMA((parts,))],
    )
    x_all = lax.all_to_all(x_pay, ("y", "x"), 0, 0, tiled=True)
    adj, inverse, flags, sel = call(
        adjacency_kernel,
        (tile_count, tile_dst, tile_src, tile_weight[0]),
        [((groups, rows, T), BF16), ((rows, T), F32), ((groups, T), BF16), ((groups,), jnp.int32)],
        in_specs=[SMEM, SMEM, SMEM, HBM],
        out_specs=[VMEM, VMEM, VMEM, SMEM],
        scratch=[
            pltpu.VMEM((slots, T, T), jnp.int32),
            pltpu.VMEM((groups, rows, T), jnp.int32),
            pltpu.SemaphoreType.DMA((slots // CHUNK,)),
        ],
        limit=20,
    )
    (y_pay,) = call(
        neighbour_product_kernel, (x_all, w_neigh, flags), [((chips, rows + groups, T), BF16)]
    )
    y_own = lax.all_to_all(y_pay, "z", 0, 0, tiled=True)
    y_other = lax.ppermute(y_own, "c", swap)
    (z_half,) = call(
        half_kernel,
        (place, sel, x_all, w_self, adj, inverse, y_own),
        [((rows, T), F32)],
        in_specs=[SMEM, SMEM] + [VMEM] * 5,
    )
    output, gt, c_pay, x_late = call(
        activation_kernel,
        (place, sel, adj, inverse, y_other, z_half, out_grad, x_all),
        [((rows, T), BF16), ((T, rows), BF16), ((groups, T, T), BF16), (x_all.shape, BF16)],
        in_specs=[SMEM, SMEM] + [VMEM] * 5 + [ANY],
        out_specs=[VMEM] * 3 + [ANY],
        aliases={7: 3},
    )
    c_all = lax.all_to_all(c_pay, ("z", "c"), 0, 0, tiled=True)
    gt_pair = lax.ppermute(gt, "c", swap)
    x_pair = lax.ppermute(x_late, "c", swap)
    (mask,) = call(
        mask_kernel, (place, y_own, y_other), [((groups, T), F32)], in_specs=[SMEM, VMEM, VMEM]
    )
    bt, p_pay = call(
        feature_grad_kernel,
        (c_all, mask, gt, w_self, w_neigh),
        [((2 * T, rows), BF16), ((parts, T, rows), BF16)],
        out_specs=[VMEM, HBM],
        scratch=[pltpu.VMEM((parts, T, rows), BF16), pltpu.SemaphoreType.DMA((parts,))],
    )
    bt_pair = lax.ppermute(bt, "c", swap)
    p_all = lax.all_to_all(p_pay, ("y", "x"), 0, 0, tiled=True)
    own, *w_pay = call(
        weight_grad_kernel,
        (place, gt, bt, gt_pair, bt_pair, x_late, x_pair),
        [((2 * T, T), F32)] + [((2 * T, T), BF16)] * (chips - 1),
        in_specs=[SMEM] + [VMEM] * 6,
    )
    w_came = [
        lax.ppermute(block, "z", [(chip, (chip + step) % chips) for chip in range(chips)])
        for step, block in zip(far_first(chips), w_pay)
    ]
    (grad_features,) = call(sum_kernel, (p_all,), [((rows, T), BF16)])
    grad_self, grad_neigh = call(weight_sum_kernel, (own, *w_came), [((T, T), F32)] * 2)
    return output, grad_features, grad_self, grad_neigh


def solution(mesh):
    row_count, part_count = mesh.shape["rows"], mesh.shape["feat"]
    split = Mesh(mesh.devices.reshape(row_count // 2, 2, 4, part_count // 4), ("z", "c", "y", "x"))
    rows, feat = ("z", "c"), ("y", "x")
    return jax.shard_map(
        functools.partial(per_device, chips=row_count // 2, parts=part_count),
        mesh=split,
        in_specs=(
            P(rows, feat),
            P(None, feat),
            P(None, feat),
            P(rows, feat),
            P(rows),
            P(rows, None),
            P(rows, None),
            P(rows, None, None, None),
        ),
        out_specs=(P(rows, feat),) * 4,
        check_vma=False,
    )
```

```python
import functools

import jax
import jax.numpy as jnp
from jax import lax
from jax.experimental import pallas as pl
from jax.experimental.pallas import tpu as pltpu
from jax.sharding import Mesh, PartitionSpec as P

F32 = jnp.float32
BF16 = jnp.bfloat16
T = 128
CHUNK = 10
MIB = 1024 * 1024
VMEM = pl.BlockSpec(memory_space=pltpu.VMEM)
SMEM = pl.BlockSpec(memory_space=pltpu.SMEM)
ANY = pl.BlockSpec(memory_space=pl.ANY)
HBM = pl.BlockSpec(memory_space=pltpu.HBM)


def dot(a, b):
    return jnp.dot(a, b, preferred_element_type=F32)


def far_first(chips):
    return tuple(sorted(range(1, chips), key=lambda step: abs(step - chips // 2)))


def halves(block):
    high = block.astype(BF16)
    return jnp.concatenate([high, (block - high.astype(F32)).astype(BF16)], axis=0)


def setup_kernel(
    count_ref, dst_hbm, src_hbm, x_hbm, weight_ref, pay_ref, adj_ref, inv_ref, flag_ref, sel_ref,
    dst_ref, src_ref, x_ref, buf, acc, in_sems, out_sems, sems,
):
    count = count_ref[0]
    slots = weight_ref.shape[0]
    groups = acc.shape[0]

    def chunk_copy(index):
        part = pl.ds(index * CHUNK, CHUNK)
        return pltpu.make_async_copy(weight_ref.at[part], buf.at[part], sems.at[index])

    ins = [
        pltpu.make_async_copy(source, target, in_sems.at[index])
        for index, (source, target) in enumerate(((x_hbm, x_ref), (dst_hbm, dst_ref), (src_hbm, src_ref)))
    ]
    outs = [
        pltpu.make_async_copy(x_ref, pay_ref.at[copy], out_sems.at[copy]) for copy in range(pay_ref.shape[0])
    ]
    for copy in ins:
        copy.start()
    for index in range(slots // CHUNK):

        @pl.when(index * CHUNK < count)
        def _():
            chunk_copy(index).start()

    acc[...] = jnp.zeros_like(acc)
    for owner in range(groups):
        sel_ref[owner] = 0
    ins[0].wait()
    for copy in outs:
        copy.start()
    ins[1].wait()
    ins[2].wait()
    for index in range(slots // CHUNK):

        @pl.when(index * CHUNK < count)
        def _():
            chunk_copy(index).wait()

            def add_tile(slot, carry):
                source = src_ref[0, slot]
                owner = source // 2
                sel_ref[owner] = source - 2 * owner
                rows = pl.ds(pl.multiple_of(dst_ref[0, slot] * T, T), T)
                acc[owner, rows, :] = acc[owner, rows, :] + buf[slot]
                return carry

            lax.fori_loop(index * CHUNK, jnp.minimum(count, (index + 1) * CHUNK), add_tile, 0)

    total = acc[0]
    for owner in range(groups):
        if owner > 0:
            total = total + acc[owner]
        adj_ref[owner] = acc[owner].astype(F32).astype(BF16)
    degree = jnp.sum(total.astype(F32), axis=1, keepdims=True)
    inv_ref[...] = jnp.broadcast_to(1.0 / jnp.maximum(degree, 1.0), inv_ref.shape)
    row = lax.broadcasted_iota(jnp.int32, flag_ref.shape, 0)
    flags = jnp.zeros(flag_ref.shape, F32)
    for owner in range(groups):
        flags = jnp.where(row == owner, sel_ref[owner].astype(F32), flags)
    flag_ref[...] = flags.astype(BF16)
    for copy in outs:
        copy.wait()


def neighbour_product_kernel(x_ref, w_ref, flag_ref, pay_ref):
    parts = x_ref.shape[0]
    rows = x_ref.shape[1]
    total = dot(x_ref[0], w_ref[0:T, :])
    for part in range(1, parts):
        total = total + dot(x_ref[part], w_ref[part * T : (part + 1) * T, :])
    product = total.astype(BF16)
    flags = flag_ref[...]
    for copy in range(pay_ref.shape[0]):
        pay_ref[copy, 0:rows, :] = product
        pay_ref[copy, rows:, :] = flags


def chosen_tile(ref, sel_ref, chip, owner):
    return ref[chip, pl.ds(pl.multiple_of(sel_ref[owner] * T, T), T), :]


def half_kernel(place_ref, sel_ref, x_ref, w_ref, adj_ref, inv_ref, own_ref, z_ref):
    core = place_ref[0]
    total = dot(x_ref[0], w_ref[0:T, :])
    for part in range(1, x_ref.shape[0]):
        total = total + dot(x_ref[part], w_ref[part * T : (part + 1) * T, :])
    summed = jnp.zeros(z_ref.shape, F32)
    for chip in range(own_ref.shape[0]):
        owner = 2 * chip + core
        summed = summed + dot(adj_ref[owner], chosen_tile(own_ref, sel_ref, chip, owner))
    z_ref[...] = total + inv_ref[...] * summed


def activation_kernel(
    place_ref, sel_ref, adj_ref, inv_ref, own_ref, other_ref, z_ref, og_ref,
    out_ref, gt_ref, pay_ref, mask_ref,
):
    core = place_ref[0]
    me = place_ref[1]
    rows = z_ref.shape[0]
    summed = jnp.zeros(z_ref.shape, F32)
    for chip in range(other_ref.shape[0]):
        owner = 2 * chip + 1 - core
        summed = summed + dot(adj_ref[owner], chosen_tile(other_ref, sel_ref, chip, owner))
    inverse = inv_ref[...]
    z = z_ref[...] + inverse * summed
    sig = 1.0 / (1.0 + jnp.exp(-z))
    grad = (og_ref[...].astype(F32) * sig * (1.0 + z * (1.0 - sig))).astype(BF16).astype(F32)
    scaled = halves((grad * inverse).T)
    for owner in range(pay_ref.shape[0]):
        spread = dot(scaled, adj_ref[owner])
        pay_ref[owner] = (spread[0:T] + spread[T:]).astype(BF16)
    out_ref[...] = (z * sig).astype(BF16)
    gt_ref[...] = grad.T.astype(BF16)
    row = lax.broadcasted_iota(jnp.int32, mask_ref.shape, 0)
    for chip in range(own_ref.shape[0]):
        for ref, owner in ((own_ref, 2 * chip + core), (other_ref, 2 * chip + 1 - core)):
            flags = ref[chip, rows:, :].astype(F32)
            mask_ref[pl.ds(owner, 1), :] = jnp.sum(jnp.where(row == me, flags, 0.0), axis=0, keepdims=True)


def feature_grad_kernel(came_ref, mask_ref, gt_ref, ws_ref, wn_ref, bt_ref, pay_ref, buf, sems):
    low = jnp.zeros((T, T), F32)
    high = jnp.zeros((T, T), F32)
    for sender in range(came_ref.shape[0]):
        came = came_ref[sender].astype(F32)
        is_high = mask_ref[sender : sender + 1, :] > 0.5
        low = low + jnp.where(is_high, 0.0, came)
        high = high + jnp.where(is_high, came, 0.0)
    both = halves(jnp.concatenate([low, high], axis=1))
    bt = both[0:T]
    bt_ref[...] = both
    gt = gt_ref[...]
    copies = []
    for part in range(pay_ref.shape[0]):
        span = slice(part * T, (part + 1) * T)
        buf[part] = (dot(ws_ref[span, :], gt) + dot(wn_ref[span, :], bt)).astype(BF16)
        copies.append(pltpu.make_async_copy(buf.at[part], pay_ref.at[part], sems.at[part]))
        copies[-1].start()
    for copy in copies:
        copy.wait()


def weight_grad_kernel(place_ref, gt_ref, bt_ref, x_ref, keep_ref, send_ref):
    core = place_ref[0]
    here = place_ref[2]
    chips = keep_ref.shape[0]
    left = jnp.concatenate([gt_ref[...], bt_ref[...]], axis=0)
    for slot, step in enumerate(far_first(chips) + (0,)):
        chip = lax.rem(here + step, chips)
        kept = dot(left, x_ref[2 * chip + core])
        sent = dot(left, x_ref[2 * chip + 1 - core])
        keep_ref[slot, 0:T] = kept[0:T]
        keep_ref[slot, T:] = kept[T : 2 * T] + kept[2 * T :]
        send_ref[slot, 0:T] = sent[0:T].astype(BF16)
        send_ref[slot, T:] = (sent[T : 2 * T] + sent[2 * T :]).astype(BF16)


def pair_kernel(keep_ref, came_ref, *pay_refs):
    for slot, pay_ref in enumerate(pay_refs):
        pay_ref[...] = (keep_ref[slot] + came_ref[slot].astype(F32)).astype(pay_ref.dtype)


def weight_sum_kernel(own_ref, done_ref, *refs):
    parts, (self_ref, neigh_ref, same_ref) = refs[:-3], refs[-3:]
    total = own_ref[...]
    for part in parts:
        total = total + part[...].astype(F32)
    self_ref[...] = total[0:T].T
    neigh_ref[...] = total[T:].T


def sum_kernel(parts_ref, out_ref):
    total = parts_ref[0].astype(F32)
    for part in range(1, parts_ref.shape[0]):
        total = total + parts_ref[part].astype(F32)
    out_ref[...] = total.T.astype(out_ref.dtype)


def call(kernel, ins, outs, in_specs=None, out_specs=None, scratch=(), limit=12, aliases=None):
    shapes = tuple(
        pltpu.HBM(shape, dtype) if spec is HBM else jax.ShapeDtypeStruct(shape, dtype)
        for (shape, dtype), spec in zip(outs, out_specs or [VMEM] * len(outs))
    )
    ins = [
        pltpu.with_memory_space_constraint(value, pltpu.HBM) if spec is HBM else value
        for value, spec in zip(ins, in_specs or [VMEM] * len(ins))
    ]
    return pl.pallas_call(
        kernel,
        out_shape=shapes,
        in_specs=in_specs or [VMEM] * len(ins),
        out_specs=tuple(out_specs or [VMEM] * len(outs)),
        scratch_shapes=list(scratch),
        input_output_aliases=aliases or {},
        compiler_params=pltpu.CompilerParams(vmem_limit_bytes=limit * MIB),
        name=kernel.__name__,
    )(*ins)


def per_device(features, w_self, w_neigh, out_grad, tile_count, tile_dst, tile_src, tile_weight, chips, parts):
    rows = features.shape[0]
    groups = 2 * chips
    slots = tile_weight.shape[1]
    core = lax.axis_index("c")
    here = lax.axis_index("z")
    place = jnp.stack([core, here * 2 + core, here]).astype(jnp.int32)
    swap = [(0, 1), (1, 0)]

    x_pay, adj, inverse, flags, sel = call(
        setup_kernel,
        (tile_count, tile_dst, tile_src, features, tile_weight[0]),
        [
            ((parts, rows, T), BF16),
            ((groups, rows, T), BF16),
            ((rows, T), F32),
            ((groups, T), BF16),
            ((groups,), jnp.int32),
        ],
        in_specs=[SMEM, HBM, HBM, HBM, HBM],
        out_specs=[HBM, VMEM, VMEM, VMEM, SMEM],
        scratch=[
            pltpu.SMEM(tile_dst.shape, jnp.int32),
            pltpu.SMEM(tile_src.shape, jnp.int32),
            pltpu.VMEM((rows, T), BF16),
            pltpu.VMEM((slots, T, T), jnp.int32),
            pltpu.VMEM((groups, rows, T), jnp.int32),
            pltpu.SemaphoreType.DMA((3,)),
            pltpu.SemaphoreType.DMA((parts,)),
            pltpu.SemaphoreType.DMA((slots // CHUNK,)),
        ],
        limit=20,
    )
    x_all = lax.all_to_all(x_pay, ("y", "x"), 0, 0, tiled=True)
    (y_pay,) = call(
        neighbour_product_kernel, (x_all, w_neigh, flags), [((chips, rows + groups, T), BF16)]
    )
    y_own = lax.all_to_all(y_pay, "z", 0, 0, tiled=True)
    y_other = lax.ppermute(y_own, "c", swap)
    (z_half,) = call(
        half_kernel,
        (place, sel, x_all, w_self, adj, inverse, y_own),
        [((rows, T), F32)],
        in_specs=[SMEM, SMEM] + [VMEM] * 5,
    )
    output, gt, c_pay, mask = call(
        activation_kernel,
        (place, sel, adj, inverse, y_own, y_other, z_half, out_grad),
        [((rows, T), BF16), ((T, rows), BF16), ((groups, T, T), BF16), ((groups, T), F32)],
        in_specs=[SMEM, SMEM] + [VMEM] * 6,
    )
    c_all = lax.all_to_all(c_pay, ("z", "c"), 0, 0, tiled=True)
    bt, p_pay = call(
        feature_grad_kernel,
        (c_all, mask, gt, w_self, w_neigh),
        [((2 * T, rows), BF16), ((parts, T, rows), BF16)],
        out_specs=[VMEM, HBM],
        scratch=[pltpu.VMEM((parts, T, rows), BF16), pltpu.SemaphoreType.DMA((parts,))],
    )
    p_all = lax.all_to_all(p_pay, ("y", "x"), 0, 0, tiled=True)
    keep, send = call(
        weight_grad_kernel,
        (place, gt, bt, x_all),
        [((chips, 2 * T, T), F32), ((chips, 2 * T, T), BF16)],
        in_specs=[SMEM] + [VMEM] * 3,
    )
    came = lax.ppermute(send, "c", swap)
    *w_pay, own = call(
        pair_kernel, (keep, came), [((2 * T, T), BF16)] * (chips - 1) + [((2 * T, T), F32)]
    )
    w_came = [
        lax.ppermute(block, "z", [(chip, (chip + step) % chips) for chip in range(chips)])
        for step, block in zip(far_first(chips), w_pay)
    ]
    (grad_features,) = call(sum_kernel, (p_all,), [((rows, T), BF16)])
    grad_self, grad_neigh, grad_features = call(
        weight_sum_kernel,
        (own, grad_features, *w_came),
        [((T, T), F32), ((T, T), F32), ((rows, T), BF16)],
        in_specs=[VMEM, ANY] + [VMEM] * (chips - 1),
        out_specs=[VMEM, VMEM, ANY],
        aliases={1: 2},
    )
    return output, grad_features, grad_self, grad_neigh


def solution(mesh):
    row_count, part_count = mesh.shape["rows"], mesh.shape["feat"]
    split = Mesh(mesh.devices.reshape(row_count // 2, 2, 4, part_count // 4), ("z", "c", "y", "x"))
    rows, feat = ("z", "c"), ("y", "x")
    return jax.shard_map(
        functools.partial(per_device, chips=row_count // 2, parts=part_count),
        mesh=split,
        in_specs=(
            P(rows, feat),
            P(None, feat),
            P(None, feat),
            P(rows, feat),
            P(rows),
            P(rows, None),
            P(rows, None),
            P(rows, None, None, None),
        ),
        out_specs=(P(rows, feat),) * 4,
        check_vma=False,
    )
```

```python
import functools

import jax
import jax.numpy as jnp
from jax import lax
from jax.experimental import pallas as pl
from jax.experimental.pallas import tpu as pltpu
from jax.sharding import Mesh, PartitionSpec as P

F32 = jnp.float32
BF16 = jnp.bfloat16
T = 128
CHUNK = 10
MIB = 1024 * 1024
VMEM = pl.BlockSpec(memory_space=pltpu.VMEM)
SMEM = pl.BlockSpec(memory_space=pltpu.SMEM)
ANY = pl.BlockSpec(memory_space=pl.ANY)
HBM = pl.BlockSpec(memory_space=pltpu.HBM)


def dot(a, b):
    return jnp.dot(a, b, preferred_element_type=F32)


def halves(block):
    high = block.astype(BF16)
    return jnp.concatenate([high, (block - high.astype(F32)).astype(BF16)], axis=0)


def add_halves(block):
    half = block.shape[0] // 2
    return block[0:half] + block[half:]


def spread_kernel(x_hbm, pay_ref, x_ref, in_sem, sems):
    copies = [
        pltpu.make_async_copy(x_ref, pay_ref.at[copy], sems.at[copy]) for copy in range(pay_ref.shape[0])
    ]
    came = pltpu.make_async_copy(x_hbm, x_ref, in_sem)
    came.start()
    came.wait()
    for copy in copies:
        copy.start()
    for copy in copies:
        copy.wait()


def neighbour_kernel(x_ref, w_ref, y_ref):
    total = dot(x_ref[0], w_ref[0:T, :])
    for part in range(1, x_ref.shape[0]):
        total = total + dot(x_ref[part], w_ref[part * T : (part + 1) * T, :])
    y_ref[...] = total.astype(BF16)


def self_kernel(x_ref, w_ref, z_ref):
    total = dot(x_ref[0], w_ref[0:T, :])
    for part in range(1, x_ref.shape[0]):
        total = total + dot(x_ref[part], w_ref[part * T : (part + 1) * T, :])
    z_ref[...] = total


def pair_kernel(place_ref, y_ref, y_pair_ref, pair_ref):
    core = place_ref[0]
    pair_ref[core] = y_ref[...]
    pair_ref[1 - core] = y_pair_ref[...]


def adjacency_kernel(
    count_ref, dst_hbm, src_hbm, weight_ref, adj_ref, inv_ref, sel_ref, dst_ref, src_ref, buf, acc, in_sems, sems
):
    count = count_ref[0]
    slots = weight_ref.shape[0]
    groups = acc.shape[0]

    def chunk_copy(index):
        part = pl.ds(index * CHUNK, CHUNK)
        return pltpu.make_async_copy(weight_ref.at[part], buf.at[part], sems.at[index])

    ins = [
        pltpu.make_async_copy(source, target, in_sems.at[index])
        for index, (source, target) in enumerate(((dst_hbm, dst_ref), (src_hbm, src_ref)))
    ]
    for copy in ins:
        copy.start()
    for index in range(slots // CHUNK):

        @pl.when(index * CHUNK < count)
        def _():
            chunk_copy(index).start()

    acc[...] = jnp.zeros_like(acc)
    for owner in range(groups):
        sel_ref[owner] = 0
    for copy in ins:
        copy.wait()
    for index in range(slots // CHUNK):

        @pl.when(index * CHUNK < count)
        def _():
            chunk_copy(index).wait()

            def add_tile(slot, carry):
                source = src_ref[0, slot]
                owner = source // 2
                sel_ref[owner] = source - 2 * owner
                rows = pl.ds(pl.multiple_of(dst_ref[0, slot] * T, T), T)
                acc[owner, rows, :] = acc[owner, rows, :] + buf[slot]
                return carry

            lax.fori_loop(index * CHUNK, jnp.minimum(count, (index + 1) * CHUNK), add_tile, 0)

    total = acc[0]
    for owner in range(groups):
        if owner > 0:
            total = total + acc[owner]
        adj_ref[owner] = acc[owner].astype(F32).astype(BF16)
    degree = jnp.sum(total.astype(F32), axis=1, keepdims=True)
    inv_ref[...] = jnp.broadcast_to(1.0 / jnp.maximum(degree, 1.0), inv_ref.shape)


def chip_at(place_ref, step):
    chips = 8
    return lax.rem(place_ref[1] + step + chips, chips)


def aggregate_kernel(
    place_ref, sel_ref, sel_pair_ref, adj_ref, adj_pair_ref, pair_ref, one_ref, two_ref, three_ref, far_ref,
    mine_ref, theirs_ref,
):
    core, here, way = place_ref[0], place_ref[1], place_ref[2]
    sources = []
    for step, ref in ((1, one_ref), (2, two_ref), (3, three_ref)):
        chip = chip_at(place_ref, -step * way)
        sources += [(ref.at[side], 2 * chip + side) for side in range(2)]
    sources.append((far_ref, 2 * chip_at(place_ref, 4) + core))
    local = [(pair_ref.at[side], 2 * here + side) for side in range(2)]

    def summed(adj, sel, tiles):
        total = jnp.zeros(mine_ref.shape, F32)
        for ref, owner in tiles:
            total = total + dot(adj[owner], ref[pl.ds(pl.multiple_of(sel[owner] * T, T), T), :])
        return total

    theirs_ref[...] = summed(adj_pair_ref, sel_pair_ref, sources)
    mine_ref[...] = summed(adj_ref, sel_ref, sources + local)


def activation_kernel(inv_ref, mine_ref, came_ref, z_ref, og_ref, out_ref, both_ref):
    inverse = inv_ref[...]
    z = z_ref[...] + inverse * (mine_ref[...] + came_ref[...])
    sig = 1.0 / (1.0 + jnp.exp(-z))
    out_ref[...] = (z * sig).astype(BF16)
    grad = (og_ref[...].astype(F32) * sig * (1.0 + z * (1.0 - sig))).astype(BF16).astype(F32)
    both_ref[0:T, :] = grad.T.astype(BF16)
    both_ref[T:, :] = halves((grad * inverse).T)


def targets(place_ref, one_ref, two_ref, three_ref, far_ref, own_ref):
    core, here, way = place_ref[0], place_ref[1], place_ref[2]
    places = [(far_ref, 2 * chip_at(place_ref, 4) + core)]
    for step, ref in ((3, three_ref), (2, two_ref), (1, one_ref)):
        chip = chip_at(place_ref, step * way)
        places += [(ref.at[side], 2 * chip + side) for side in range(2)]
    places.append((own_ref, 2 * here + core))
    return places


def transpose_kernel(
    place_ref, sel_ref, sel_pair_ref, adj_ref, adj_pair_ref, both_ref, both_pair_ref, x_ref, *out_refs
):
    left = both_ref[T:, :]
    left_pair = both_pair_ref[T:, :]
    for ref, owner in targets(place_ref, *out_refs[:-1]):
        ours = add_halves(dot(left, adj_ref[owner]))
        theirs = add_halves(dot(left_pair, adj_pair_ref[owner]))
        ours_high = sel_ref[owner] == 1
        theirs_high = sel_pair_ref[owner] == 1
        low = jnp.where(ours_high, 0.0, ours) + jnp.where(theirs_high, 0.0, theirs)
        high = jnp.where(ours_high, ours, 0.0) + jnp.where(theirs_high, theirs, 0.0)
        ref[:, 0:T] = low.astype(ref.dtype)
        ref[:, T:] = high.astype(ref.dtype)


def weight_grad_kernel(place_ref, both_ref, both_pair_ref, bt_ref, x_ref, x_pair_ref, *out_refs):
    left = jnp.concatenate([both_ref[0:T, :], bt_ref[0]], axis=0)
    left_pair = jnp.concatenate([both_pair_ref[0:T, :], bt_ref[1]], axis=0)
    for ref, owner in targets(place_ref, *out_refs):
        total = dot(left, x_ref[owner]) + dot(left_pair, x_pair_ref[owner])
        ref[0:T] = total[0:T].astype(ref.dtype)
        ref[T:] = add_halves(total[T:]).astype(ref.dtype)


def fold_kernel(place_ref, one_ref, two_ref, three_ref, far_ref, own_ref, fold_ref):
    core = place_ref[0]
    mine = own_ref[...] + far_ref[...].astype(F32)
    theirs = jnp.zeros(own_ref.shape, F32)
    for ref in (one_ref, two_ref, three_ref):
        mine = mine + ref[core].astype(F32)
        theirs = theirs + ref[1 - core].astype(F32)
    fold_ref[0] = mine
    fold_ref[1] = theirs


def feature_grad_kernel(fold_ref, came_ref, both_ref, ws_ref, wn_ref, bt_ref, pay_ref, buf, sems):
    split = halves(fold_ref[0] + came_ref[1])
    bt_ref[0] = split
    bt_ref[1] = halves(fold_ref[1] + came_ref[0])
    bt = split[0:T]
    gt = both_ref[0:T, :]
    copies = []
    for part in range(pay_ref.shape[0]):
        span = slice(part * T, (part + 1) * T)
        buf[part] = (dot(ws_ref[span, :], gt) + dot(wn_ref[span, :], bt)).astype(BF16)
        copies.append(pltpu.make_async_copy(buf.at[part], pay_ref.at[part], sems.at[part]))
        copies[-1].start()
    for copy in copies:
        copy.wait()


def sum_kernel(parts_ref, out_ref):
    total = parts_ref[0].astype(F32)
    for part in range(1, parts_ref.shape[0]):
        total = total + parts_ref[part].astype(F32)
    out_ref[...] = total.T.astype(out_ref.dtype)


def last_kernel(fold_ref, came_ref, done_ref, self_ref, neigh_ref, same_ref):
    total = fold_ref[0] + came_ref[1]
    self_ref[...] = total[0:T].T
    neigh_ref[...] = total[T:].T


def call(kernel, ins, outs, in_specs=None, out_specs=None, scratch=(), limit=12, aliases=None):
    shapes = tuple(
        pltpu.HBM(shape, dtype) if spec is HBM else jax.ShapeDtypeStruct(shape, dtype)
        for (shape, dtype), spec in zip(outs, out_specs or [VMEM] * len(outs))
    )
    ins = [
        pltpu.with_memory_space_constraint(value, pltpu.HBM) if spec is HBM else value
        for value, spec in zip(ins, in_specs or [VMEM] * len(ins))
    ]
    return pl.pallas_call(
        kernel,
        out_shape=shapes,
        in_specs=in_specs or [VMEM] * len(ins),
        out_specs=tuple(out_specs or [VMEM] * len(outs)),
        scratch_shapes=list(scratch),
        input_output_aliases=aliases or {},
        compiler_params=pltpu.CompilerParams(vmem_limit_bytes=limit * MIB),
        name=kernel.__name__,
    )(*ins)


def swap(value):
    return lax.ppermute(value, "c", [(0, 1), (1, 0)])


def along(value, step):
    pairs = [(2 * chip, 2 * ((chip + step) % 8)) for chip in range(8)]
    pairs += [(2 * chip + 1, 2 * ((chip - step) % 8) + 1) for chip in range(8)]
    return lax.ppermute(value, ("z", "c"), pairs)


def exchange(one, two, three, far):
    far = along(far, 4)
    three, two, one = along(three, 3), along(two, 2), along(one, 1)
    return one, two, three, far


def exchange_shapes(shape):
    return [((2,) + shape, BF16)] * 3 + [(shape, BF16), (shape, F32)]


def per_device(features, w_self, w_neigh, out_grad, tile_count, tile_dst, tile_src, tile_weight, chips, parts):
    rows = features.shape[0]
    groups = 2 * chips
    slots = tile_weight.shape[1]
    core = lax.axis_index("c")
    place = jnp.stack([core, lax.axis_index("z"), 1 - 2 * core]).astype(jnp.int32)

    (x_pay,) = call(
        spread_kernel,
        (features,),
        [((parts, rows, T), BF16)],
        in_specs=[HBM],
        out_specs=[HBM],
        scratch=[pltpu.VMEM((rows, T), BF16), pltpu.SemaphoreType.DMA, pltpu.SemaphoreType.DMA((parts,))],
    )
    x_all = lax.all_to_all(x_pay, "f", 0, 0, tiled=True)
    (y,) = call(neighbour_kernel, (x_all, w_neigh), [((rows, T), BF16)])
    (pair,) = call(pair_kernel, (place, y, swap(y)), [((2, rows, T), BF16)], in_specs=[SMEM, VMEM, VMEM])
    y_came = exchange(pair, pair, pair, y)
    adj, inverse, sel = call(
        adjacency_kernel,
        (tile_count, tile_dst, tile_src, tile_weight[0]),
        [((groups, rows, T), BF16), ((rows, T), F32), ((groups,), jnp.int32)],
        in_specs=[SMEM, HBM, HBM, HBM],
        out_specs=[VMEM, VMEM, SMEM],
        scratch=[
            pltpu.SMEM(tile_dst.shape, jnp.int32),
            pltpu.SMEM(tile_src.shape, jnp.int32),
            pltpu.VMEM((slots, T, T), jnp.int32),
            pltpu.VMEM((groups, rows, T), jnp.int32),
            pltpu.SemaphoreType.DMA((2,)),
            pltpu.SemaphoreType.DMA((slots // CHUNK,)),
        ],
        limit=20,
    )
    adj_pair, sel_pair = swap(adj), swap(sel)
    (z_self,) = call(self_kernel, (x_all, w_self), [((rows, T), F32)])
    scalars = [SMEM] * 3
    mine, theirs = call(
        aggregate_kernel,
        (place, sel, sel_pair, adj, adj_pair, pair, *y_came),
        [((rows, T), F32)] * 2,
        in_specs=scalars + [VMEM] * 7,
    )
    output, both = call(
        activation_kernel,
        (inverse, mine, swap(theirs), z_self, out_grad),
        [((rows, T), BF16), ((3 * T, rows), BF16)],
    )
    both_pair = swap(both)

    *sends, own, x_late = call(
        transpose_kernel,
        (place, sel, sel_pair, adj, adj_pair, both, both_pair, x_all),
        exchange_shapes((T, rows)) + [(x_all.shape, BF16)],
        in_specs=scalars + [VMEM] * 4 + [ANY],
        out_specs=[VMEM] * 5 + [ANY],
        aliases={7: 5},
    )
    x_pair = swap(x_late)
    b_came = exchange(*sends)
    (fold,) = call(
        fold_kernel, (place, *b_came, own), [((2, T, rows), F32)], in_specs=[SMEM] + [VMEM] * 5
    )
    bt, p_pay = call(
        feature_grad_kernel,
        (fold, swap(fold), both, w_self, w_neigh),
        [((2, 2 * T, rows), BF16), ((parts, T, rows), BF16)],
        out_specs=[VMEM, HBM],
        scratch=[pltpu.VMEM((parts, T, rows), BF16), pltpu.SemaphoreType.DMA((parts,))],
    )
    p_all = lax.all_to_all(p_pay, "f", 0, 0, tiled=True)
    *sends, own = call(
        weight_grad_kernel,
        (place, both, both_pair, bt, x_late, x_pair),
        exchange_shapes((2 * T, T)),
        in_specs=[SMEM] + [VMEM] * 5,
    )
    w_came = exchange(*sends)
    (fold,) = call(
        fold_kernel, (place, *w_came, own), [((2, 2 * T, T), F32)], in_specs=[SMEM] + [VMEM] * 5
    )
    (grad_features,) = call(sum_kernel, (p_all,), [((rows, T), BF16)])
    grad_self, grad_neigh, grad_features = call(
        last_kernel,
        (fold, swap(fold), grad_features),
        [((T, T), F32), ((T, T), F32), ((rows, T), BF16)],
        in_specs=[VMEM, VMEM, ANY],
        out_specs=[VMEM, VMEM, ANY],
        aliases={2: 2},
    )
    return output, grad_features, grad_self, grad_neigh


def solution(mesh):
    row_count, part_count = mesh.shape["rows"], mesh.shape["feat"]
    split = Mesh(mesh.devices.reshape(row_count // 2, 2, part_count), ("z", "c", "f"))
    rows = ("z", "c")
    return jax.shard_map(
        functools.partial(per_device, chips=row_count // 2, parts=part_count),
        mesh=split,
        in_specs=(
            P(rows, "f"),
            P(None, "f"),
            P(None, "f"),
            P(rows, "f"),
            P(rows),
            P(rows, None),
            P(rows, None),
            P(rows, None, None, None),
        ),
        out_specs=(P(rows, "f"),) * 4,
        check_vma=False,
    )
```

```python
import functools

import jax
import jax.numpy as jnp
from jax import lax
from jax.experimental import pallas as pl
from jax.experimental.pallas import tpu as pltpu
from jax.sharding import Mesh, PartitionSpec as P

F32 = jnp.float32
BF16 = jnp.bfloat16
T = 128
CHUNK = 10
MIB = 1024 * 1024
VMEM = pl.BlockSpec(memory_space=pltpu.VMEM)
SMEM = pl.BlockSpec(memory_space=pltpu.SMEM)
ANY = pl.BlockSpec(memory_space=pl.ANY)
HBM = pl.BlockSpec(memory_space=pltpu.HBM)


def dot(a, b):
    return jnp.dot(a, b, preferred_element_type=F32)


def halves(block):
    high = block.astype(BF16)
    return jnp.concatenate([high, (block - high.astype(F32)).astype(BF16)], axis=0)


def add_halves(block):
    half = block.shape[0] // 2
    return block[0:half] + block[half:]


def spread_kernel(x_hbm, pay_ref, x_ref, in_sem, sems):
    copies = [
        pltpu.make_async_copy(x_ref, pay_ref.at[copy], sems.at[copy]) for copy in range(pay_ref.shape[0])
    ]
    came = pltpu.make_async_copy(x_hbm, x_ref, in_sem)
    came.start()
    came.wait()
    for copy in copies:
        copy.start()
    for copy in copies:
        copy.wait()


def neighbour_kernel(sel_ref, x_ref, w_hbm, y_ref, sel_same_ref, w_ref, sems):
    parts = x_ref.shape[0]
    chunks = sems.shape[0]
    span = parts // chunks
    copies = []
    for chunk in range(chunks):
        part = pl.ds(chunk * span * T, span * T)
        copies.append(pltpu.make_async_copy(w_hbm.at[part], w_ref.at[part], sems.at[chunk]))
        copies[-1].start()
    for owner in range(sel_ref.shape[0]):
        sel_same_ref[owner] = sel_ref[owner]
    total = jnp.zeros(y_ref.shape, F32)
    for part in range(parts):
        if part % span == 0:
            copies[part // span].wait()
        total = total + dot(x_ref[part], w_ref[part * T : (part + 1) * T, :])
    y_ref[...] = total.astype(BF16)


def self_kernel(x_ref, w_ref, z_ref):
    total = dot(x_ref[0], w_ref[0:T, :])
    for part in range(1, x_ref.shape[0]):
        total = total + dot(x_ref[part], w_ref[part * T : (part + 1) * T, :])
    z_ref[...] = total


def pair_kernel(place_ref, y_ref, y_pair_ref, pair_ref):
    core = place_ref[0]
    pair_ref[core] = y_ref[...]
    pair_ref[1 - core] = y_pair_ref[...]


def adjacency_kernel(
    count_ref, dst_hbm, src_hbm, weight_ref, adj_ref, inv_ref, sel_ref, dst_ref, src_ref, buf, acc, in_sems, sems
):
    count = count_ref[0]
    slots = weight_ref.shape[0]
    groups = acc.shape[0]

    def chunk_copy(index):
        part = pl.ds(index * CHUNK, CHUNK)
        return pltpu.make_async_copy(weight_ref.at[part], buf.at[part], sems.at[index])

    ins = [
        pltpu.make_async_copy(source, target, in_sems.at[index])
        for index, (source, target) in enumerate(((dst_hbm, dst_ref), (src_hbm, src_ref)))
    ]
    for copy in ins:
        copy.start()
    for index in range(slots // CHUNK):

        @pl.when(index * CHUNK < count)
        def _():
            chunk_copy(index).start()

    acc[...] = jnp.zeros_like(acc)
    for owner in range(groups):
        sel_ref[owner] = 0
    for copy in ins:
        copy.wait()
    for index in range(slots // CHUNK):

        @pl.when(index * CHUNK < count)
        def _():
            chunk_copy(index).wait()

            def add_tile(slot, carry):
                source = src_ref[0, slot]
                owner = source // 2
                sel_ref[owner] = source - 2 * owner
                rows = pl.ds(pl.multiple_of(dst_ref[0, slot] * T, T), T)
                acc[owner, rows, :] = acc[owner, rows, :] + buf[slot]
                return carry

            lax.fori_loop(index * CHUNK, jnp.minimum(count, (index + 1) * CHUNK), add_tile, 0)

    total = acc[0]
    for owner in range(groups):
        if owner > 0:
            total = total + acc[owner]
        adj_ref[owner] = acc[owner].astype(F32).astype(BF16)
    degree = jnp.sum(total.astype(F32), axis=1, keepdims=True)
    inv_ref[...] = jnp.broadcast_to(1.0 / jnp.maximum(degree, 1.0), inv_ref.shape)


def chip_at(place_ref, step):
    chips = 8
    return lax.rem(place_ref[1] + step + chips, chips)


def aggregate_kernel(
    place_ref, sel_ref, sel_pair_ref, adj_ref, adj_pair_ref, inv_ref, z_ref, pair_ref,
    far_ref, three_ref, two_ref, one_ref, mine_ref, theirs_ref,
):
    here, way = place_ref[1], place_ref[2]
    sources = []
    for step, ref in ((1, one_ref), (2, two_ref), (3, three_ref), (4, far_ref)):
        chip = chip_at(place_ref, -step * way)
        sources += [(ref.at[side], 2 * chip + side) for side in range(2)]
    local = [(pair_ref.at[side], 2 * here + side) for side in range(2)]

    def summed(adj, sel, tiles):
        total = jnp.zeros(mine_ref.shape, F32)
        for ref, owner in tiles:
            total = total + dot(adj[owner], ref[pl.ds(pl.multiple_of(sel[owner] * T, T), T), :])
        return total

    theirs_ref[...] = summed(adj_pair_ref, sel_pair_ref, sources)
    mine_ref[...] = z_ref[...] + inv_ref[...] * summed(adj_ref, sel_ref, sources + local)


def activation_kernel(inv_ref, mine_ref, came_ref, og_ref, out_ref, both_ref):
    inverse = inv_ref[...]
    z = mine_ref[...] + inverse * came_ref[...]
    sig = 1.0 / (1.0 + jnp.exp(-z))
    out_ref[...] = (z * sig).astype(BF16)
    grad = (og_ref[...].astype(F32) * sig * (1.0 + z * (1.0 - sig))).astype(BF16).astype(F32)
    both_ref[0:T, :] = grad.T.astype(BF16)
    both_ref[T:, :] = halves((grad * inverse).T)


def targets(place_ref, far_ref, three_ref, two_ref, one_ref, own_ref):
    core, here, way = place_ref[0], place_ref[1], place_ref[2]
    places = []
    for step, ref in ((4, far_ref), (3, three_ref), (2, two_ref), (1, one_ref)):
        chip = chip_at(place_ref, step * way)
        places += [(ref.at[side], 2 * chip + side) for side in range(2)]
    places.append((own_ref, 2 * here + core))
    return places


def transpose_kernel(
    place_ref, sel_ref, sel_pair_ref, adj_ref, adj_pair_ref, both_ref, both_pair_ref, x_ref, *out_refs
):
    left = both_ref[T:, :]
    left_pair = both_pair_ref[T:, :]
    for ref, owner in targets(place_ref, *out_refs[:-1]):
        ours = add_halves(dot(left, adj_ref[owner]))
        theirs = add_halves(dot(left_pair, adj_pair_ref[owner]))
        ours_high = sel_ref[owner] == 1
        theirs_high = sel_pair_ref[owner] == 1
        low = jnp.where(ours_high, 0.0, ours) + jnp.where(theirs_high, 0.0, theirs)
        high = jnp.where(ours_high, ours, 0.0) + jnp.where(theirs_high, theirs, 0.0)
        ref[:, 0:T] = low.astype(ref.dtype)
        ref[:, T:] = high.astype(ref.dtype)


def weight_grad_kernel(place_ref, both_ref, both_pair_ref, bt_ref, x_ref, x_pair_ref, *out_refs):
    left = jnp.concatenate([both_ref[0:T, :], bt_ref[0]], axis=0)
    left_pair = jnp.concatenate([both_pair_ref[0:T, :], bt_ref[1]], axis=0)
    for ref, owner in targets(place_ref, *out_refs):
        total = dot(left, x_ref[owner]) + dot(left_pair, x_pair_ref[owner])
        ref[0:T] = total[0:T].astype(ref.dtype)
        ref[T:] = add_halves(total[T:]).astype(ref.dtype)


def fold_kernel(place_ref, far_ref, three_ref, two_ref, one_ref, own_ref, fold_ref):
    core = place_ref[0]
    mine = own_ref[...]
    theirs = jnp.zeros(own_ref.shape, F32)
    for ref in (far_ref, three_ref, two_ref, one_ref):
        mine = mine + ref[core].astype(F32)
        theirs = theirs + ref[1 - core].astype(F32)
    fold_ref[0] = mine
    fold_ref[1] = theirs


def feature_grad_kernel(fold_ref, came_ref, both_ref, ws_ref, wn_ref, bt_ref, pay_ref, buf, sems):
    split = halves(fold_ref[0] + came_ref[1])
    bt_ref[0] = split
    bt_ref[1] = halves(fold_ref[1] + came_ref[0])
    bt = split[0:T]
    gt = both_ref[0:T, :]
    copies = []
    for part in range(pay_ref.shape[0]):
        span = slice(part * T, (part + 1) * T)
        buf[part] = (dot(ws_ref[span, :], gt) + dot(wn_ref[span, :], bt)).astype(BF16)
        copies.append(pltpu.make_async_copy(buf.at[part], pay_ref.at[part], sems.at[part]))
        copies[-1].start()
    for copy in copies:
        copy.wait()


def sum_kernel(parts_ref, out_ref):
    total = parts_ref[0].astype(F32)
    for part in range(1, parts_ref.shape[0]):
        total = total + parts_ref[part].astype(F32)
    out_ref[...] = total.T.astype(out_ref.dtype)


def last_kernel(fold_ref, came_ref, done_ref, self_ref, neigh_ref, same_ref):
    total = fold_ref[0] + came_ref[1]
    self_ref[...] = total[0:T].T
    neigh_ref[...] = total[T:].T


def call(kernel, ins, outs, in_specs=None, out_specs=None, scratch=(), limit=12, aliases=None):
    shapes = tuple(
        pltpu.HBM(shape, dtype) if spec is HBM else jax.ShapeDtypeStruct(shape, dtype)
        for (shape, dtype), spec in zip(outs, out_specs or [VMEM] * len(outs))
    )
    ins = [
        pltpu.with_memory_space_constraint(value, pltpu.HBM) if spec is HBM else value
        for value, spec in zip(ins, in_specs or [VMEM] * len(ins))
    ]
    return pl.pallas_call(
        kernel,
        out_shape=shapes,
        in_specs=in_specs or [VMEM] * len(ins),
        out_specs=tuple(out_specs or [VMEM] * len(outs)),
        scratch_shapes=list(scratch),
        input_output_aliases=aliases or {},
        compiler_params=pltpu.CompilerParams(vmem_limit_bytes=limit * MIB),
        name=kernel.__name__,
    )(*ins)


def swap(value):
    return lax.ppermute(value, "c", [(0, 1), (1, 0)])


def along(value, step):
    pairs = [(2 * chip, 2 * ((chip + step) % 8)) for chip in range(8)]
    if step < 4:
        pairs += [(2 * chip + 1, 2 * ((chip - step) % 8) + 1) for chip in range(8)]
    return lax.ppermute(value, ("z", "c"), pairs)


def exchange(far, three, two, one):
    return along(far, 4), along(three, 3), along(two, 2), along(one, 1)


def exchange_shapes(shape):
    return [((2,) + shape, BF16)] * 4 + [(shape, F32)]


def per_device(features, w_self, w_neigh, out_grad, tile_count, tile_dst, tile_src, tile_weight, chips, parts):
    rows = features.shape[0]
    groups = 2 * chips
    slots = tile_weight.shape[1]
    core = lax.axis_index("c")
    place = jnp.stack([core, lax.axis_index("z"), 1 - 2 * core]).astype(jnp.int32)

    (x_pay,) = call(
        spread_kernel,
        (features,),
        [((parts, rows, T), BF16)],
        in_specs=[HBM],
        out_specs=[HBM],
        scratch=[pltpu.VMEM((rows, T), BF16), pltpu.SemaphoreType.DMA, pltpu.SemaphoreType.DMA((parts,))],
    )
    x_all = lax.all_to_all(x_pay, "f", 0, 0, tiled=True)
    adj, inverse, sel = call(
        adjacency_kernel,
        (tile_count, tile_dst, tile_src, tile_weight[0]),
        [((groups, rows, T), BF16), ((rows, T), F32), ((groups,), jnp.int32)],
        in_specs=[SMEM, HBM, HBM, HBM],
        out_specs=[VMEM, VMEM, SMEM],
        scratch=[
            pltpu.SMEM(tile_dst.shape, jnp.int32),
            pltpu.SMEM(tile_src.shape, jnp.int32),
            pltpu.VMEM((slots, T, T), jnp.int32),
            pltpu.VMEM((groups, rows, T), jnp.int32),
            pltpu.SemaphoreType.DMA((2,)),
            pltpu.SemaphoreType.DMA((slots // CHUNK,)),
        ],
        limit=20,
    )
    sel_pair = swap(sel)
    y, sel_pair = call(
        neighbour_kernel,
        (sel_pair, x_all, w_neigh),
        [((rows, T), BF16), ((groups,), jnp.int32)],
        in_specs=[SMEM, VMEM, HBM],
        out_specs=[VMEM, SMEM],
        scratch=[pltpu.VMEM(w_neigh.shape, BF16), pltpu.SemaphoreType.DMA((4,))],
    )
    (pair,) = call(pair_kernel, (place, y, swap(y)), [((2, rows, T), BF16)], in_specs=[SMEM, VMEM, VMEM])
    y_came = exchange(pair, pair, pair, pair)
    adj_pair = swap(adj)
    (z_self,) = call(self_kernel, (x_all, w_self), [((rows, T), F32)])
    scalars = [SMEM] * 3
    mine, theirs = call(
        aggregate_kernel,
        (place, sel, sel_pair, adj, adj_pair, inverse, z_self, pair, *y_came),
        [((rows, T), F32)] * 2,
        in_specs=scalars + [VMEM] * 9,
    )
    output, both = call(
        activation_kernel,
        (inverse, mine, swap(theirs), out_grad),
        [((rows, T), BF16), ((3 * T, rows), BF16)],
    )
    both_pair = swap(both)

    *sends, own, x_late = call(
        transpose_kernel,
        (place, sel, sel_pair, adj, adj_pair, both, both_pair, x_all),
        exchange_shapes((T, rows)) + [(x_all.shape, BF16)],
        in_specs=scalars + [VMEM] * 4 + [ANY],
        out_specs=[VMEM] * 5 + [ANY],
        aliases={7: 5},
    )
    x_pair = swap(x_late)
    b_came = exchange(*sends)
    (fold,) = call(
        fold_kernel, (place, *b_came, own), [((2, T, rows), F32)], in_specs=[SMEM] + [VMEM] * 5
    )
    bt, p_pay = call(
        feature_grad_kernel,
        (fold, swap(fold), both, w_self, w_neigh),
        [((2, 2 * T, rows), BF16), ((parts, T, rows), BF16)],
        out_specs=[VMEM, HBM],
        scratch=[pltpu.VMEM((parts, T, rows), BF16), pltpu.SemaphoreType.DMA((parts,))],
    )
    p_all = lax.all_to_all(p_pay, "f", 0, 0, tiled=True)
    *sends, own = call(
        weight_grad_kernel,
        (place, both, both_pair, bt, x_late, x_pair),
        exchange_shapes((2 * T, T)),
        in_specs=[SMEM] + [VMEM] * 5,
    )
    w_came = exchange(*sends)
    (fold,) = call(
        fold_kernel, (place, *w_came, own), [((2, 2 * T, T), F32)], in_specs=[SMEM] + [VMEM] * 5
    )
    (grad_features,) = call(sum_kernel, (p_all,), [((rows, T), BF16)])
    grad_self, grad_neigh, grad_features = call(
        last_kernel,
        (fold, swap(fold), grad_features),
        [((T, T), F32), ((T, T), F32), ((rows, T), BF16)],
        in_specs=[VMEM, VMEM, ANY],
        out_specs=[VMEM, VMEM, ANY],
        aliases={2: 2},
    )
    return output, grad_features, grad_self, grad_neigh


def solution(mesh):
    row_count, part_count = mesh.shape["rows"], mesh.shape["feat"]
    split = Mesh(mesh.devices.reshape(row_count // 2, 2, part_count), ("z", "c", "f"))
    rows = ("z", "c")
    return jax.shard_map(
        functools.partial(per_device, chips=row_count // 2, parts=part_count),
        mesh=split,
        in_specs=(
            P(rows, "f"),
            P(None, "f"),
            P(None, "f"),
            P(rows, "f"),
            P(rows),
            P(rows, None),
            P(rows, None),
            P(rows, None, None, None),
        ),
        out_specs=(P(rows, "f"),) * 4,
        check_vma=False,
    )
```

```python
import functools

import jax
import jax.numpy as jnp
from jax import lax
from jax.experimental import pallas as pl
from jax.experimental.pallas import tpu as pltpu
from jax.sharding import Mesh, PartitionSpec as P

F32 = jnp.float32
BF16 = jnp.bfloat16
T = 128
CHUNK = 10
MIB = 1024 * 1024
VMEM = pl.BlockSpec(memory_space=pltpu.VMEM)
SMEM = pl.BlockSpec(memory_space=pltpu.SMEM)
ANY = pl.BlockSpec(memory_space=pl.ANY)
HBM = pl.BlockSpec(memory_space=pltpu.HBM)


def dot(a, b):
    return jnp.dot(a, b, preferred_element_type=F32)


def far_first(chips):
    return tuple(sorted(range(1, chips), key=lambda step: abs(step - chips // 2)))


def halves(block):
    high = block.astype(BF16)
    return jnp.concatenate([high, (block - high.astype(F32)).astype(BF16)], axis=0)


def setup_kernel(
    count_ref, dst_hbm, src_hbm, x_hbm, weight_ref, pay_ref, adj_ref, inv_ref, flag_ref, sel_ref,
    dst_ref, src_ref, x_ref, buf, acc, in_sems, out_sems, sems,
):
    count = count_ref[0]
    slots = weight_ref.shape[0]
    groups = acc.shape[0]

    def chunk_copy(index):
        part = pl.ds(index * CHUNK, CHUNK)
        return pltpu.make_async_copy(weight_ref.at[part], buf.at[part], sems.at[index])

    ins = [
        pltpu.make_async_copy(source, target, in_sems.at[index])
        for index, (source, target) in enumerate(((x_hbm, x_ref), (dst_hbm, dst_ref), (src_hbm, src_ref)))
    ]
    outs = [
        pltpu.make_async_copy(x_ref, pay_ref.at[copy], out_sems.at[copy]) for copy in range(pay_ref.shape[0])
    ]
    for copy in ins:
        copy.start()
    for index in range(slots // CHUNK):

        @pl.when(index * CHUNK < count)
        def _():
            chunk_copy(index).start()

    acc[...] = jnp.zeros_like(acc)
    for owner in range(groups):
        sel_ref[owner] = 0
    ins[0].wait()
    for copy in outs:
        copy.start()
    ins[1].wait()
    ins[2].wait()
    for index in range(slots // CHUNK):

        @pl.when(index * CHUNK < count)
        def _():
            chunk_copy(index).wait()

            def add_tile(slot, carry):
                source = src_ref[0, slot]
                owner = source // 2
                sel_ref[owner] = source - 2 * owner
                rows = pl.ds(pl.multiple_of(dst_ref[0, slot] * T, T), T)
                acc[owner, rows, :] = acc[owner, rows, :] + buf[slot]
                return carry

            lax.fori_loop(index * CHUNK, jnp.minimum(count, (index + 1) * CHUNK), add_tile, 0)

    total = acc[0]
    for owner in range(groups):
        if owner > 0:
            total = total + acc[owner]
        adj_ref[owner] = acc[owner].astype(F32).astype(BF16)
    degree = jnp.sum(total.astype(F32), axis=1, keepdims=True)
    inv_ref[...] = jnp.broadcast_to(1.0 / jnp.maximum(degree, 1.0), inv_ref.shape)
    row = lax.broadcasted_iota(jnp.int32, flag_ref.shape, 0)
    flags = jnp.zeros(flag_ref.shape, F32)
    for owner in range(groups):
        flags = jnp.where(row == owner, sel_ref[owner].astype(F32), flags)
    flag_ref[...] = flags.astype(BF16)
    for copy in outs:
        copy.wait()


def neighbour_product_kernel(x_ref, w_ref, flag_ref, pay_ref):
    parts = x_ref.shape[0]
    rows = x_ref.shape[1]
    total = dot(x_ref[0], w_ref[0:T, :])
    for part in range(1, parts):
        total = total + dot(x_ref[part], w_ref[part * T : (part + 1) * T, :])
    product = total.astype(BF16)
    flags = flag_ref[...]
    for copy in range(pay_ref.shape[0]):
        pay_ref[copy, 0:rows, :] = product
        pay_ref[copy, rows:, :] = flags


def chosen_tile(ref, sel_ref, chip, owner):
    return ref[chip, pl.ds(pl.multiple_of(sel_ref[owner] * T, T), T), :]


def half_kernel(sel_ref, x_ref, w_ref, adj_ref, inv_ref, own_ref, z_ref):
    core = lax.axis_index("c")
    total = dot(x_ref[0], w_ref[0:T, :])
    for part in range(1, x_ref.shape[0]):
        total = total + dot(x_ref[part], w_ref[part * T : (part + 1) * T, :])
    summed = jnp.zeros(z_ref.shape, F32)
    for chip in range(own_ref.shape[0]):
        owner = 2 * chip + core
        summed = summed + dot(adj_ref[owner], chosen_tile(own_ref, sel_ref, chip, owner))
    z_ref[...] = total + inv_ref[...] * summed


def activation_kernel(
    sel_ref, adj_ref, inv_ref, own_ref, other_ref, z_ref, og_ref,
    out_ref, gt_ref, pay_ref, mask_ref,
):
    core = lax.axis_index("c")
    me = 2 * lax.axis_index("z") + core
    rows = z_ref.shape[0]
    summed = jnp.zeros(z_ref.shape, F32)
    for chip in range(other_ref.shape[0]):
        owner = 2 * chip + 1 - core
        summed = summed + dot(adj_ref[owner], chosen_tile(other_ref, sel_ref, chip, owner))
    inverse = inv_ref[...]
    z = z_ref[...] + inverse * summed
    sig = 1.0 / (1.0 + jnp.exp(-z))
    grad = (og_ref[...].astype(F32) * sig * (1.0 + z * (1.0 - sig))).astype(BF16).astype(F32)
    scaled = halves((grad * inverse).T)
    for owner in range(pay_ref.shape[0]):
        spread = dot(scaled, adj_ref[owner])
        pay_ref[owner] = (spread[0:T] + spread[T:]).astype(BF16)
    out_ref[...] = (z * sig).astype(BF16)
    gt_ref[...] = grad.T.astype(BF16)
    row = lax.broadcasted_iota(jnp.int32, mask_ref.shape, 0)
    for chip in range(own_ref.shape[0]):
        for ref, owner in ((own_ref, 2 * chip + core), (other_ref, 2 * chip + 1 - core)):
            flags = ref[chip, rows:, :].astype(F32)
            mask_ref[pl.ds(owner, 1), :] = jnp.sum(jnp.where(row == me, flags, 0.0), axis=0, keepdims=True)


def weight_grad_kernel(came_ref, mask_ref, gt_ref, x_ref, bt_ref, keep_ref, send_ref):
    core = lax.axis_index("c")
    here = lax.axis_index("z")
    chips = keep_ref.shape[0]
    low = jnp.zeros((T, T), F32)
    high = jnp.zeros((T, T), F32)
    for sender in range(came_ref.shape[0]):
        came = came_ref[sender].astype(F32)
        is_high = mask_ref[sender : sender + 1, :] > 0.5
        low = low + jnp.where(is_high, 0.0, came)
        high = high + jnp.where(is_high, came, 0.0)
    both = halves(jnp.concatenate([low, high], axis=1))
    bt_ref[...] = both[0:T]
    left = jnp.concatenate([gt_ref[...], both], axis=0)
    for slot, step in enumerate(far_first(chips) + (0,)):
        chip = lax.rem(here + step, chips)
        kept = dot(left, x_ref[2 * chip + core])
        sent = dot(left, x_ref[2 * chip + 1 - core])
        keep_ref[slot, 0:T] = kept[0:T]
        keep_ref[slot, T:] = kept[T : 2 * T] + kept[2 * T :]
        send_ref[slot, 0:T] = sent[0:T].astype(BF16)
        send_ref[slot, T:] = (sent[T : 2 * T] + sent[2 * T :]).astype(BF16)


def feature_grad_kernel(gt_ref, bt_ref, ws_ref, wn_ref, pay_ref, buf, sems):
    gt = gt_ref[...]
    bt = bt_ref[...]
    copies = []
    for part in range(pay_ref.shape[0]):
        span = slice(part * T, (part + 1) * T)
        buf[part] = (dot(ws_ref[span, :], gt) + dot(wn_ref[span, :], bt)).astype(BF16)
        copies.append(pltpu.make_async_copy(buf.at[part], pay_ref.at[part], sems.at[part]))
        copies[-1].start()
    for copy in copies:
        copy.wait()


def pair_kernel(keep_ref, came_ref, payload_ref, *pay_refs):
    for slot, pay_ref in enumerate(pay_refs[:-1]):
        pay_ref[...] = (keep_ref[slot] + came_ref[slot].astype(F32)).astype(pay_ref.dtype)


def weight_sum_kernel(own_ref, done_ref, *refs):
    parts, (self_ref, neigh_ref, same_ref) = refs[:-3], refs[-3:]
    total = own_ref[...]
    for part in parts:
        total = total + part[...].astype(F32)
    self_ref[...] = total[0:T].T
    neigh_ref[...] = total[T:].T


def sum_kernel(parts_ref, out_ref):
    total = parts_ref[0].astype(F32)
    for part in range(1, parts_ref.shape[0]):
        total = total + parts_ref[part].astype(F32)
    out_ref[...] = total.T.astype(out_ref.dtype)


def call(kernel, ins, outs, in_specs=None, out_specs=None, scratch=(), limit=12, aliases=None):
    shapes = tuple(
        pltpu.HBM(shape, dtype) if spec is HBM else jax.ShapeDtypeStruct(shape, dtype)
        for (shape, dtype), spec in zip(outs, out_specs or [VMEM] * len(outs))
    )
    ins = [
        pltpu.with_memory_space_constraint(value, pltpu.HBM) if spec is HBM else value
        for value, spec in zip(ins, in_specs or [VMEM] * len(ins))
    ]
    return pl.pallas_call(
        kernel,
        out_shape=shapes,
        in_specs=in_specs or [VMEM] * len(ins),
        out_specs=tuple(out_specs or [VMEM] * len(outs)),
        scratch_shapes=list(scratch),
        input_output_aliases=aliases or {},
        compiler_params=pltpu.CompilerParams(vmem_limit_bytes=limit * MIB),
        name=kernel.__name__,
    )(*ins)


def per_device(features, w_self, w_neigh, out_grad, tile_count, tile_dst, tile_src, tile_weight, chips, parts):
    rows = features.shape[0]
    groups = 2 * chips
    slots = tile_weight.shape[1]
    swap = [(0, 1), (1, 0)]

    x_pay, adj, inverse, flags, sel = call(
        setup_kernel,
        (tile_count, tile_dst, tile_src, features, tile_weight[0]),
        [
            ((parts, rows, T), BF16),
            ((groups, rows, T), BF16),
            ((rows, T), F32),
            ((groups, T), BF16),
            ((groups,), jnp.int32),
        ],
        in_specs=[SMEM, HBM, HBM, HBM, HBM],
        out_specs=[HBM, VMEM, VMEM, VMEM, SMEM],
        scratch=[
            pltpu.SMEM(tile_dst.shape, jnp.int32),
            pltpu.SMEM(tile_src.shape, jnp.int32),
            pltpu.VMEM((rows, T), BF16),
            pltpu.VMEM((slots, T, T), jnp.int32),
            pltpu.VMEM((groups, rows, T), jnp.int32),
            pltpu.SemaphoreType.DMA((3,)),
            pltpu.SemaphoreType.DMA((parts,)),
            pltpu.SemaphoreType.DMA((slots // CHUNK,)),
        ],
        limit=20,
    )
    x_all = lax.all_to_all(x_pay, "f", 0, 0, tiled=True)
    (y_pay,) = call(
        neighbour_product_kernel, (x_all, w_neigh, flags), [((chips, rows + groups, T), BF16)]
    )
    y_own = lax.all_to_all(y_pay, "z", 0, 0, tiled=True)
    y_other = lax.ppermute(y_own, "c", swap)
    (z_half,) = call(
        half_kernel,
        (sel, x_all, w_self, adj, inverse, y_own),
        [((rows, T), F32)],
        in_specs=[SMEM] + [VMEM] * 5,
    )
    output, gt, c_pay, mask = call(
        activation_kernel,
        (sel, adj, inverse, y_own, y_other, z_half, out_grad),
        [((rows, T), BF16), ((T, rows), BF16), ((groups, T, T), BF16), ((groups, T), F32)],
        in_specs=[SMEM] + [VMEM] * 6,
    )
    c_all = lax.all_to_all(c_pay, ("z", "c"), 0, 0, tiled=True)
    bt, keep, send = call(
        weight_grad_kernel,
        (c_all, mask, gt, x_all),
        [((T, rows), BF16), ((chips, 2 * T, T), F32), ((chips, 2 * T, T), BF16)],
    )
    came = lax.ppermute(send, "c", swap)
    (p_pay,) = call(
        feature_grad_kernel,
        (gt, bt, w_self, w_neigh),
        [((parts, T, rows), BF16)],
        out_specs=[HBM],
        scratch=[pltpu.VMEM((parts, T, rows), BF16), pltpu.SemaphoreType.DMA((parts,))],
    )
    *w_pay, own, p_pay = call(
        pair_kernel,
        (keep, came, p_pay),
        [((2 * T, T), BF16)] * (chips - 1) + [((2 * T, T), F32), (p_pay.shape, BF16)],
        in_specs=[VMEM, VMEM, HBM],
        out_specs=[VMEM] * chips + [HBM],
        aliases={2: chips},
    )
    p_all = lax.all_to_all(p_pay, "f", 0, 0, tiled=True)
    w_came = [
        lax.ppermute(block, "z", [(chip, (chip + step) % chips) for chip in range(chips)])
        for step, block in zip(far_first(chips), w_pay)
    ]
    (grad_features,) = call(sum_kernel, (p_all,), [((rows, T), BF16)])
    grad_self, grad_neigh, grad_features = call(
        weight_sum_kernel,
        (own, grad_features, *w_came),
        [((T, T), F32), ((T, T), F32), ((rows, T), BF16)],
        in_specs=[VMEM, ANY] + [VMEM] * (chips - 1),
        out_specs=[VMEM, VMEM, ANY],
        aliases={1: 2},
    )
    return output, grad_features, grad_self, grad_neigh


def solution(mesh):
    row_count, part_count = mesh.shape["rows"], mesh.shape["feat"]
    split = Mesh(mesh.devices.reshape(row_count // 2, 2, part_count), ("z", "c", "f"))
    rows, feat = ("z", "c"), "f"
    return jax.shard_map(
        functools.partial(per_device, chips=row_count // 2, parts=part_count),
        mesh=split,
        in_specs=(
            P(rows, feat),
            P(None, feat),
            P(None, feat),
            P(rows, feat),
            P(rows),
            P(rows, None),
            P(rows, None),
            P(rows, None, None, None),
        ),
        out_specs=(P(rows, feat),) * 4,
        check_vma=False,
    )
```

```python
import functools

import jax
import jax.numpy as jnp
from jax import lax
from jax.experimental import pallas as pl
from jax.experimental.pallas import tpu as pltpu
from jax.sharding import Mesh, PartitionSpec as P

F32 = jnp.float32
BF16 = jnp.bfloat16
T = 128
CHUNK = 10
MIB = 1024 * 1024
VMEM = pl.BlockSpec(memory_space=pltpu.VMEM)
SMEM = pl.BlockSpec(memory_space=pltpu.SMEM)
ANY = pl.BlockSpec(memory_space=pl.ANY)
HBM = pl.BlockSpec(memory_space=pltpu.HBM)


def dot(a, b):
    return jnp.dot(a, b, preferred_element_type=F32)


def far_first(chips):
    return tuple(sorted(range(1, chips), key=lambda step: abs(step - chips // 2)))


def halves(block):
    high = block.astype(BF16)
    return jnp.concatenate([high, (block - high.astype(F32)).astype(BF16)], axis=0)


def spread_kernel(x_hbm, pay_ref, x_ref, in_sem, sems):
    copies = [
        pltpu.make_async_copy(x_ref, pay_ref.at[copy], sems.at[copy]) for copy in range(pay_ref.shape[0])
    ]
    came = pltpu.make_async_copy(x_hbm, x_ref, in_sem)
    came.start()
    came.wait()
    for copy in copies:
        copy.start()
    for copy in copies:
        copy.wait()


def adjacency_kernel(
    count_ref, dst_hbm, src_hbm, weight_ref, adj_ref, send_ref, inv_ref, flag_ref, sel_ref,
    dst_ref, src_ref, buf, acc, in_sems, sems,
):
    count = count_ref[0]
    slots = weight_ref.shape[0]
    groups = acc.shape[0]

    def chunk_copy(index):
        part = pl.ds(index * CHUNK, CHUNK)
        return pltpu.make_async_copy(weight_ref.at[part], buf.at[part], sems.at[index])

    ins = [
        pltpu.make_async_copy(source, target, in_sems.at[index])
        for index, (source, target) in enumerate(((dst_hbm, dst_ref), (src_hbm, src_ref)))
    ]
    for copy in ins:
        copy.start()
    for index in range(slots // CHUNK):

        @pl.when(index * CHUNK < count)
        def _():
            chunk_copy(index).start()

    acc[...] = jnp.zeros_like(acc)
    for owner in range(groups):
        sel_ref[owner] = 0
    for copy in ins:
        copy.wait()
    for index in range(slots // CHUNK):

        @pl.when(index * CHUNK < count)
        def _():
            chunk_copy(index).wait()

            def add_tile(slot, carry):
                source = src_ref[0, slot]
                owner = source // 2
                sel_ref[owner] = source - 2 * owner
                rows = pl.ds(pl.multiple_of(dst_ref[0, slot] * T, T), T)
                acc[owner, rows, :] = acc[owner, rows, :] + buf[slot]
                return carry

            lax.fori_loop(index * CHUNK, jnp.minimum(count, (index + 1) * CHUNK), add_tile, 0)

    total = acc[0]
    for owner in range(groups):
        if owner > 0:
            total = total + acc[owner]
        adj_ref[owner] = acc[owner].astype(F32).astype(BF16)
    other = 1 - lax.axis_index("c")
    for chip in range(send_ref.shape[0]):
        send_ref[chip] = adj_ref[2 * chip + other]
    degree = jnp.sum(total.astype(F32), axis=1, keepdims=True)
    inv_ref[...] = jnp.broadcast_to(1.0 / jnp.maximum(degree, 1.0), inv_ref.shape)
    row = lax.broadcasted_iota(jnp.int32, flag_ref.shape, 0)
    flags = jnp.zeros(flag_ref.shape, F32)
    for owner in range(groups):
        flags = jnp.where(row == owner, sel_ref[owner].astype(F32), flags)
    flag_ref[...] = flags.astype(BF16)


def neighbour_kernel(sel_ref, x_ref, w_ref, flag_ref, adj_ref, pay_ref, sel_same_ref, adj_same_ref):
    rows = x_ref.shape[1]
    total = dot(x_ref[0], w_ref[0:T, :])
    for part in range(1, x_ref.shape[0]):
        total = total + dot(x_ref[part], w_ref[part * T : (part + 1) * T, :])
    product = total.astype(BF16)
    flags = flag_ref[...]
    for copy in range(pay_ref.shape[0]):
        pay_ref[copy, 0:rows, :] = product
        pay_ref[copy, rows:, :] = flags
    for owner in range(sel_ref.shape[0]):
        sel_same_ref[owner] = sel_ref[owner]


def self_kernel(x_ref, w_ref, z_ref):
    total = dot(x_ref[0], w_ref[0:T, :])
    for part in range(1, x_ref.shape[0]):
        total = total + dot(x_ref[part], w_ref[part * T : (part + 1) * T, :])
    z_ref[...] = total


def aggregate_kernel(
    sel_ref, sel_pair_ref, adj_ref, adj_pair_ref, y_ref, x_ref, mine_ref, mask_ref, theirs_ref, x_same_ref
):
    core = lax.axis_index("c")
    here = 2 * lax.axis_index("z")
    chips = y_ref.shape[0]
    rows = mine_ref.shape[0]
    row = lax.broadcasted_iota(jnp.int32, (y_ref.shape[1] - rows, T), 0)

    def summed(adj, sel):
        total = jnp.zeros(mine_ref.shape, F32)
        for chip in range(chips):
            owner = 2 * chip + core
            tile = y_ref[chip, pl.ds(pl.multiple_of(sel[owner] * T, T), T), :]
            total = total + dot(adj(chip, owner), tile)
        return total

    theirs_ref[0:rows] = summed(lambda chip, owner: adj_pair_ref[chip], sel_pair_ref)
    mine_ref[...] = summed(lambda chip, owner: adj_ref[owner], sel_ref)
    for chip in range(chips):
        flags = y_ref[chip, rows:, :].astype(F32)
        mask_ref[chip : chip + 1, :] = jnp.sum(
            jnp.where(row == here + core, flags, 0.0), axis=0, keepdims=True
        )
        theirs_ref[rows + chip : rows + chip + 1, :] = jnp.sum(
            jnp.where(row == here + 1 - core, flags, 0.0), axis=0, keepdims=True
        )


def activation_kernel(
    adj_ref, inv_ref, mine_ref, own_mask_ref, came_ref, z_ref, og_ref, out_ref, gt_ref, pay_ref, mask_ref
):
    core = lax.axis_index("c")
    rows = z_ref.shape[0]
    chips = own_mask_ref.shape[0]
    mask_ref[pl.ds(pl.multiple_of(core * chips, chips), chips), :] = own_mask_ref[...]
    mask_ref[pl.ds(pl.multiple_of((1 - core) * chips, chips), chips), :] = came_ref[rows:, :]
    inverse = inv_ref[...]
    z = z_ref[...] + inverse * (mine_ref[...] + came_ref[0:rows])
    sig = 1.0 / (1.0 + jnp.exp(-z))
    grad = (og_ref[...].astype(F32) * sig * (1.0 + z * (1.0 - sig))).astype(BF16).astype(F32)
    scaled = halves((grad * inverse).T)
    for owner in range(pay_ref.shape[0]):
        spread = dot(scaled, adj_ref[owner])
        pay_ref[owner] = (spread[0:T] + spread[T:]).astype(BF16)
    out_ref[...] = (z * sig).astype(BF16)
    gt_ref[...] = grad.T.astype(BF16)


def weight_grad_kernel(came_ref, mask_ref, gt_ref, x_ref, bt_ref, keep_ref, send_ref):
    core = lax.axis_index("c")
    here = lax.axis_index("z")
    chips = keep_ref.shape[0]
    low = jnp.zeros((T, T), F32)
    high = jnp.zeros((T, T), F32)
    for sender in range(came_ref.shape[0]):
        came = came_ref[sender].astype(F32)
        place = sender % 2 * chips + sender // 2
        is_high = mask_ref[place : place + 1, :] > 0.5
        low = low + jnp.where(is_high, 0.0, came)
        high = high + jnp.where(is_high, came, 0.0)
    both = halves(jnp.concatenate([low, high], axis=1))
    bt_ref[...] = both[0:T]
    left = jnp.concatenate([gt_ref[...], both], axis=0)
    for slot, step in enumerate(far_first(chips) + (0,)):
        chip = lax.rem(here + step, chips)
        kept = dot(left, x_ref[2 * chip + core])
        sent = dot(left, x_ref[2 * chip + 1 - core])
        keep_ref[slot, 0:T] = kept[0:T]
        keep_ref[slot, T:] = kept[T : 2 * T] + kept[2 * T :]
        send_ref[slot, 0:T] = sent[0:T].astype(BF16)
        send_ref[slot, T:] = (sent[T : 2 * T] + sent[2 * T :]).astype(BF16)


def feature_grad_kernel(gt_ref, bt_ref, ws_ref, wn_ref, pay_ref, buf, sems):
    gt = gt_ref[...]
    bt = bt_ref[...]
    copies = []
    for part in range(pay_ref.shape[0]):
        span = slice(part * T, (part + 1) * T)
        buf[part] = (dot(ws_ref[span, :], gt) + dot(wn_ref[span, :], bt)).astype(BF16)
        copies.append(pltpu.make_async_copy(buf.at[part], pay_ref.at[part], sems.at[part]))
        copies[-1].start()
    for copy in copies:
        copy.wait()


def pair_kernel(keep_ref, came_ref, payload_ref, *pay_refs):
    for slot, pay_ref in enumerate(pay_refs[:-1]):
        pay_ref[...] = (keep_ref[slot] + came_ref[slot].astype(F32)).astype(pay_ref.dtype)


def weight_sum_kernel(own_ref, done_ref, *refs):
    parts, (self_ref, neigh_ref, same_ref) = refs[:-3], refs[-3:]
    total = own_ref[...]
    for part in parts:
        total = total + part[...].astype(F32)
    self_ref[...] = total[0:T].T
    neigh_ref[...] = total[T:].T


def sum_kernel(parts_ref, out_ref):
    total = parts_ref[0].astype(F32)
    for part in range(1, parts_ref.shape[0]):
        total = total + parts_ref[part].astype(F32)
    out_ref[...] = total.T.astype(out_ref.dtype)


def call(kernel, ins, outs, in_specs=None, out_specs=None, scratch=(), limit=12, aliases=None):
    shapes = tuple(
        pltpu.HBM(shape, dtype) if spec is HBM else jax.ShapeDtypeStruct(shape, dtype)
        for (shape, dtype), spec in zip(outs, out_specs or [VMEM] * len(outs))
    )
    ins = [
        pltpu.with_memory_space_constraint(value, pltpu.HBM) if spec is HBM else value
        for value, spec in zip(ins, in_specs or [VMEM] * len(ins))
    ]
    return pl.pallas_call(
        kernel,
        out_shape=shapes,
        in_specs=in_specs or [VMEM] * len(ins),
        out_specs=tuple(out_specs or [VMEM] * len(outs)),
        scratch_shapes=list(scratch),
        input_output_aliases=aliases or {},
        compiler_params=pltpu.CompilerParams(vmem_limit_bytes=limit * MIB),
        name=kernel.__name__,
    )(*ins)


def per_device(features, w_self, w_neigh, out_grad, tile_count, tile_dst, tile_src, tile_weight, chips, parts):
    rows = features.shape[0]
    groups = 2 * chips
    slots = tile_weight.shape[1]
    swap = [(0, 1), (1, 0)]

    (x_pay,) = call(
        spread_kernel,
        (features,),
        [((parts, rows, T), BF16)],
        in_specs=[HBM],
        out_specs=[HBM],
        scratch=[pltpu.VMEM((rows, T), BF16), pltpu.SemaphoreType.DMA, pltpu.SemaphoreType.DMA((parts,))],
    )
    x_all = lax.all_to_all(x_pay, "f", 0, 0, tiled=True)
    adj, adj_send, inverse, flags, sel = call(
        adjacency_kernel,
        (tile_count, tile_dst, tile_src, tile_weight[0]),
        [
            ((groups, rows, T), BF16),
            ((chips, rows, T), BF16),
            ((rows, T), F32),
            ((groups, T), BF16),
            ((groups,), jnp.int32),
        ],
        in_specs=[SMEM, HBM, HBM, HBM],
        out_specs=[VMEM, VMEM, VMEM, VMEM, SMEM],
        scratch=[
            pltpu.SMEM(tile_dst.shape, jnp.int32),
            pltpu.SMEM(tile_src.shape, jnp.int32),
            pltpu.VMEM((slots, T, T), jnp.int32),
            pltpu.VMEM((groups, rows, T), jnp.int32),
            pltpu.SemaphoreType.DMA((2,)),
            pltpu.SemaphoreType.DMA((slots // CHUNK,)),
        ],
        limit=20,
    )
    adj_pair = lax.ppermute(adj_send, "c", swap)
    y_pay, sel_pair, adj_pair = call(
        neighbour_kernel,
        (lax.ppermute(sel, "c", swap), x_all, w_neigh, flags, adj_pair),
        [((chips, rows + groups, T), BF16), ((groups,), jnp.int32), (adj_pair.shape, BF16)],
        in_specs=[SMEM] + [VMEM] * 3 + [HBM],
        out_specs=[VMEM, SMEM, HBM],
        aliases={4: 2},
    )
    y_own = lax.all_to_all(y_pay, "z", 0, 0, tiled=True)
    mine, own_mask, theirs, x_late = call(
        aggregate_kernel,
        (sel, sel_pair, adj, adj_pair, y_own, x_all),
        [((rows, T), F32), ((chips, T), F32), ((rows + chips, T), F32), (x_all.shape, BF16)],
        in_specs=[SMEM] * 2 + [VMEM] * 3 + [ANY],
        out_specs=[VMEM] * 3 + [ANY],
        aliases={5: 3},
    )
    came = lax.ppermute(theirs, "c", swap)
    (z_self,) = call(self_kernel, (x_late, w_self), [((rows, T), F32)])
    output, gt, c_pay, mask = call(
        activation_kernel,
        (adj, inverse, mine, own_mask, came, z_self, out_grad),
        [((rows, T), BF16), ((T, rows), BF16), ((groups, T, T), BF16), ((groups, T), F32)],
    )
    c_all = lax.all_to_all(c_pay, ("z", "c"), 0, 0, tiled=True)
    bt, keep, send = call(
        weight_grad_kernel,
        (c_all, mask, gt, x_late),
        [((T, rows), BF16), ((chips, 2 * T, T), F32), ((chips, 2 * T, T), BF16)],
    )
    came = lax.ppermute(send, "c", swap)
    (p_pay,) = call(
        feature_grad_kernel,
        (gt, bt, w_self, w_neigh),
        [((parts, T, rows), BF16)],
        out_specs=[HBM],
        scratch=[pltpu.VMEM((parts, T, rows), BF16), pltpu.SemaphoreType.DMA((parts,))],
    )
    *w_pay, own, p_pay = call(
        pair_kernel,
        (keep, came, p_pay),
        [((2 * T, T), BF16)] * (chips - 1) + [((2 * T, T), F32), (p_pay.shape, BF16)],
        in_specs=[VMEM, VMEM, HBM],
        out_specs=[VMEM] * chips + [HBM],
        aliases={2: chips},
    )
    p_all = lax.all_to_all(p_pay, "f", 0, 0, tiled=True)
    w_came = [
        lax.ppermute(block, "z", [(chip, (chip + step) % chips) for chip in range(chips)])
        for step, block in zip(far_first(chips), w_pay)
    ]
    (grad_features,) = call(sum_kernel, (p_all,), [((rows, T), BF16)])
    grad_self, grad_neigh, grad_features = call(
        weight_sum_kernel,
        (own, grad_features, *w_came),
        [((T, T), F32), ((T, T), F32), ((rows, T), BF16)],
        in_specs=[VMEM, ANY] + [VMEM] * (chips - 1),
        out_specs=[VMEM, VMEM, ANY],
        aliases={1: 2},
    )
    return output, grad_features, grad_self, grad_neigh


def solution(mesh):
    row_count, part_count = mesh.shape["rows"], mesh.shape["feat"]
    split = Mesh(mesh.devices.reshape(row_count // 2, 2, part_count), ("z", "c", "f"))
    rows, feat = ("z", "c"), "f"
    return jax.shard_map(
        functools.partial(per_device, chips=row_count // 2, parts=part_count),
        mesh=split,
        in_specs=(
            P(rows, feat),
            P(None, feat),
            P(None, feat),
            P(rows, feat),
            P(rows),
            P(rows, None),
            P(rows, None),
            P(rows, None, None, None),
        ),
        out_specs=(P(rows, feat),) * 4,
        check_vma=False,
    )
```

```python
import functools

import jax
import jax.numpy as jnp
from jax import lax
from jax.experimental import pallas as pl
from jax.experimental.pallas import tpu as pltpu
from jax.sharding import Mesh, PartitionSpec as P

F32 = jnp.float32
BF16 = jnp.bfloat16
T = 128
CHUNK = 10
MIB = 1024 * 1024
VMEM = pl.BlockSpec(memory_space=pltpu.VMEM)
SMEM = pl.BlockSpec(memory_space=pltpu.SMEM)
ANY = pl.BlockSpec(memory_space=pl.ANY)
HBM = pl.BlockSpec(memory_space=pltpu.HBM)


def dot(a, b):
    return jnp.dot(a, b, preferred_element_type=F32)


def owners(here, core, chips):
    way = 1 - 2 * core

    def chip(step):
        return lax.rem(here + step + chips, chips)

    far = 2 * chip(chips // 2) + core
    three, two, one = (2 * chip(step * way) for step in (3, 2, 1))
    return [three, three + 1, far, two, two + 1, one, one + 1, 2 * here + core]


def halves(block):
    high = block.astype(BF16)
    return jnp.concatenate([high, (block - high.astype(F32)).astype(BF16)], axis=0)


def spread_kernel(x_hbm, pay_ref, x_ref, in_sem, sems):
    copies = [
        pltpu.make_async_copy(x_ref, pay_ref.at[copy], sems.at[copy]) for copy in range(pay_ref.shape[0])
    ]
    came = pltpu.make_async_copy(x_hbm, x_ref, in_sem)
    came.start()
    came.wait()
    for copy in copies:
        copy.start()
    for copy in copies:
        copy.wait()


def adjacency_kernel(
    count_ref, dst_hbm, src_hbm, weight_ref, adj_ref, send_ref, inv_ref, flag_ref, sel_ref,
    dst_ref, src_ref, buf, acc, in_sems, sems,
):
    count = count_ref[0]
    slots = weight_ref.shape[0]
    groups = acc.shape[0]

    def chunk_copy(index):
        part = pl.ds(index * CHUNK, CHUNK)
        return pltpu.make_async_copy(weight_ref.at[part], buf.at[part], sems.at[index])

    ins = [
        pltpu.make_async_copy(source, target, in_sems.at[index])
        for index, (source, target) in enumerate(((dst_hbm, dst_ref), (src_hbm, src_ref)))
    ]
    for copy in ins:
        copy.start()
    for index in range(slots // CHUNK):

        @pl.when(index * CHUNK < count)
        def _():
            chunk_copy(index).start()

    acc[...] = jnp.zeros_like(acc)
    for owner in range(groups):
        sel_ref[owner] = 0
    for copy in ins:
        copy.wait()
    for index in range(slots // CHUNK):

        @pl.when(index * CHUNK < count)
        def _():
            chunk_copy(index).wait()

            def add_tile(slot, carry):
                source = src_ref[0, slot]
                owner = source // 2
                sel_ref[owner] = source - 2 * owner
                rows = pl.ds(pl.multiple_of(dst_ref[0, slot] * T, T), T)
                acc[owner, rows, :] = acc[owner, rows, :] + buf[slot]
                return carry

            lax.fori_loop(index * CHUNK, jnp.minimum(count, (index + 1) * CHUNK), add_tile, 0)

    total = acc[0]
    for owner in range(groups):
        if owner > 0:
            total = total + acc[owner]
        adj_ref[owner] = acc[owner].astype(F32).astype(BF16)
    other = 1 - lax.axis_index("c")
    for chip in range(send_ref.shape[0]):
        send_ref[chip] = adj_ref[2 * chip + other]
    degree = jnp.sum(total.astype(F32), axis=1, keepdims=True)
    inv_ref[...] = jnp.broadcast_to(1.0 / jnp.maximum(degree, 1.0), inv_ref.shape)
    row = lax.broadcasted_iota(jnp.int32, flag_ref.shape, 0)
    flags = jnp.zeros(flag_ref.shape, F32)
    for owner in range(groups):
        flags = jnp.where(row == owner, sel_ref[owner].astype(F32), flags)
    flag_ref[...] = flags.astype(BF16)


def neighbour_kernel(x_ref, w_ref, flag_ref, sel_ref, adj_ref, pay_ref, sel_same_ref, adj_same_ref):
    rows = x_ref.shape[1]
    total = dot(x_ref[0], w_ref[0:T, :])
    for part in range(1, x_ref.shape[0]):
        total = total + dot(x_ref[part], w_ref[part * T : (part + 1) * T, :])
    product = total.astype(BF16)
    flags = flag_ref[...]
    for copy in range(pay_ref.shape[0]):
        pay_ref[copy, 0:rows, :] = product
        pay_ref[copy, rows:, :] = flags


def self_kernel(x_ref, w_ref, z_ref):
    total = dot(x_ref[0], w_ref[0:T, :])
    for part in range(1, x_ref.shape[0]):
        total = total + dot(x_ref[part], w_ref[part * T : (part + 1) * T, :])
    z_ref[...] = total


def aggregate_kernel(
    sel_ref, sel_pair_ref, adj_ref, adj_pair_ref, y_ref, x_ref, mine_ref, mask_ref, theirs_ref, x_same_ref
):
    core = lax.axis_index("c")
    here = 2 * lax.axis_index("z")
    chips = y_ref.shape[0]
    rows = mine_ref.shape[0]
    row = lax.broadcasted_iota(jnp.int32, (y_ref.shape[1] - rows, T), 0)

    def summed(adj, sel):
        total = jnp.zeros(mine_ref.shape, F32)
        for chip in range(chips):
            owner = 2 * chip + core
            tile = y_ref[chip, pl.ds(pl.multiple_of(sel[owner] * T, T), T), :]
            total = total + dot(adj(chip, owner), tile)
        return total

    theirs_ref[0:rows] = summed(lambda chip, owner: adj_pair_ref[chip], sel_pair_ref)
    mine_ref[...] = summed(lambda chip, owner: adj_ref[owner], sel_ref)
    for chip in range(chips):
        flags = y_ref[chip, rows:, :].astype(F32)
        mask_ref[chip : chip + 1, :] = jnp.sum(
            jnp.where(row == here + core, flags, 0.0), axis=0, keepdims=True
        )
        theirs_ref[rows + chip : rows + chip + 1, :] = jnp.sum(
            jnp.where(row == here + 1 - core, flags, 0.0), axis=0, keepdims=True
        )


def activation_kernel(
    adj_ref, inv_ref, mine_ref, own_mask_ref, came_ref, z_ref, og_ref, out_ref, gt_ref, pay_ref, mask_ref
):
    core = lax.axis_index("c")
    rows = z_ref.shape[0]
    chips = own_mask_ref.shape[0]
    mask_ref[pl.ds(pl.multiple_of(core * chips, chips), chips), :] = own_mask_ref[...]
    mask_ref[pl.ds(pl.multiple_of((1 - core) * chips, chips), chips), :] = came_ref[rows:, :]
    inverse = inv_ref[...]
    z = z_ref[...] + inverse * (mine_ref[...] + came_ref[0:rows])
    sig = 1.0 / (1.0 + jnp.exp(-z))
    grad = (og_ref[...].astype(F32) * sig * (1.0 + z * (1.0 - sig))).astype(BF16).astype(F32)
    scaled = halves((grad * inverse).T)
    for owner in range(pay_ref.shape[0]):
        spread = dot(scaled, adj_ref[owner])
        pay_ref[owner] = (spread[0:T] + spread[T:]).astype(BF16)
    out_ref[...] = (z * sig).astype(BF16)
    gt_ref[...] = grad.T.astype(BF16)


def weight_grad_kernel(came_ref, mask_ref, gt_ref, x_ref, bt_ref, keep_ref, send_ref):
    core = lax.axis_index("c")
    here = lax.axis_index("z")
    chips = keep_ref.shape[0]
    low = jnp.zeros((T, T), F32)
    high = jnp.zeros((T, T), F32)
    for sender in range(came_ref.shape[0]):
        came = came_ref[sender].astype(F32)
        place = sender % 2 * chips + sender // 2
        is_high = mask_ref[place : place + 1, :] > 0.5
        low = low + jnp.where(is_high, 0.0, came)
        high = high + jnp.where(is_high, came, 0.0)
    both = halves(jnp.concatenate([low, high], axis=1))
    bt_ref[...] = both[0:T]
    left = jnp.concatenate([gt_ref[...], both], axis=0)
    slots = zip(owners(here, core, chips), owners(here, 1 - core, chips))
    for slot, (ours, theirs) in enumerate(slots):
        kept = dot(left, x_ref[ours])
        sent = dot(left, x_ref[theirs])
        keep_ref[slot, 0:T] = kept[0:T]
        keep_ref[slot, T:] = kept[T : 2 * T] + kept[2 * T :]
        send_ref[slot, 0:T] = sent[0:T].astype(BF16)
        send_ref[slot, T:] = (sent[T : 2 * T] + sent[2 * T :]).astype(BF16)


def feature_grad_kernel(gt_ref, bt_ref, ws_ref, wn_ref, pay_ref, buf, sems):
    gt = gt_ref[...]
    bt = bt_ref[...]
    copies = []
    for part in range(pay_ref.shape[0]):
        span = slice(part * T, (part + 1) * T)
        buf[part] = (dot(ws_ref[span, :], gt) + dot(wn_ref[span, :], bt)).astype(BF16)
        copies.append(pltpu.make_async_copy(buf.at[part], pay_ref.at[part], sems.at[part]))
        copies[-1].start()
    for copy in copies:
        copy.wait()


def pair_kernel(keep_ref, came_ref, payload_ref, three_ref, two_ref, one_ref, own_ref, same_ref):
    def pair(slot):
        return keep_ref[slot] + came_ref[slot].astype(F32)

    for place in range(3):
        three_ref[place] = pair(place).astype(BF16)
    for place in range(2):
        two_ref[place] = pair(3 + place).astype(BF16)
        one_ref[place] = pair(5 + place)
    own_ref[...] = pair(7)


def relay_kernel(part_ref, own_ref, three_ref, two_ref, one_ref, fold_ref):
    core = lax.axis_index("c")
    one_ref[core] = (part_ref[core] + three_ref[2].astype(F32)).astype(BF16)
    one_ref[1 - core] = part_ref[1 - core].astype(BF16)
    fold_ref[0] = own_ref[...] + three_ref[core].astype(F32) + two_ref[core].astype(F32)
    fold_ref[1] = three_ref[1 - core].astype(F32) + two_ref[1 - core].astype(F32)


def fold_kernel(fold_ref, one_ref, mine_ref, theirs_ref):
    core = lax.axis_index("c")
    theirs_ref[...] = fold_ref[1] + one_ref[1 - core].astype(F32)
    mine_ref[...] = fold_ref[0] + one_ref[core].astype(F32)


def last_kernel(mine_ref, came_ref, done_ref, self_ref, neigh_ref, same_ref):
    total = mine_ref[...] + came_ref[...]
    self_ref[...] = total[0:T].T
    neigh_ref[...] = total[T:].T


def sum_kernel(parts_ref, out_ref):
    total = parts_ref[0].astype(F32)
    for part in range(1, parts_ref.shape[0]):
        total = total + parts_ref[part].astype(F32)
    out_ref[...] = total.T.astype(out_ref.dtype)


def call(kernel, ins, outs, in_specs=None, out_specs=None, scratch=(), limit=12, aliases=None):
    shapes = tuple(
        pltpu.HBM(shape, dtype) if spec is HBM else jax.ShapeDtypeStruct(shape, dtype)
        for (shape, dtype), spec in zip(outs, out_specs or [VMEM] * len(outs))
    )
    ins = [
        pltpu.with_memory_space_constraint(value, pltpu.HBM) if spec is HBM else value
        for value, spec in zip(ins, in_specs or [VMEM] * len(ins))
    ]
    return pl.pallas_call(
        kernel,
        out_shape=shapes,
        in_specs=in_specs or [VMEM] * len(ins),
        out_specs=tuple(out_specs or [VMEM] * len(outs)),
        scratch_shapes=list(scratch),
        input_output_aliases=aliases or {},
        compiler_params=pltpu.CompilerParams(vmem_limit_bytes=limit * MIB),
        name=kernel.__name__,
    )(*ins)


def along(value, step, chips):
    pairs = [(2 * chip, 2 * ((chip + step) % chips)) for chip in range(chips)]
    pairs += [(2 * chip + 1, 2 * ((chip - step) % chips) + 1) for chip in range(chips)]
    return lax.ppermute(value, ("z", "c"), pairs)


def per_device(features, w_self, w_neigh, out_grad, tile_count, tile_dst, tile_src, tile_weight, chips, parts):
    rows = features.shape[0]
    groups = 2 * chips
    slots = tile_weight.shape[1]
    swap = [(0, 1), (1, 0)]

    (x_pay,) = call(
        spread_kernel,
        (features,),
        [((parts, rows, T), BF16)],
        in_specs=[HBM],
        out_specs=[HBM],
        scratch=[pltpu.VMEM((rows, T), BF16), pltpu.SemaphoreType.DMA, pltpu.SemaphoreType.DMA((parts,))],
    )
    x_all = lax.all_to_all(x_pay, "f", 0, 0, tiled=True)
    adj, adj_send, inverse, flags, sel = call(
        adjacency_kernel,
        (tile_count, tile_dst, tile_src, tile_weight[0]),
        [
            ((groups, rows, T), BF16),
            ((chips, rows, T), BF16),
            ((rows, T), F32),
            ((groups, T), BF16),
            ((groups,), jnp.int32),
        ],
        in_specs=[SMEM, HBM, HBM, HBM],
        out_specs=[VMEM, VMEM, VMEM, VMEM, SMEM],
        scratch=[
            pltpu.SMEM(tile_dst.shape, jnp.int32),
            pltpu.SMEM(tile_src.shape, jnp.int32),
            pltpu.VMEM((slots, T, T), jnp.int32),
            pltpu.VMEM((groups, rows, T), jnp.int32),
            pltpu.SemaphoreType.DMA((2,)),
            pltpu.SemaphoreType.DMA((slots // CHUNK,)),
        ],
        limit=20,
    )
    adj_pair = lax.ppermute(adj_send, "c", swap)
    y_pay, sel_pair, adj_pair = call(
        neighbour_kernel,
        (x_all, w_neigh, flags, lax.ppermute(sel, "c", swap), adj_pair),
        [((chips, rows + groups, T), BF16), ((groups,), jnp.int32), (adj_pair.shape, BF16)],
        in_specs=[VMEM] * 3 + [ANY, HBM],
        out_specs=[VMEM, ANY, HBM],
        aliases={3: 1, 4: 2},
    )
    y_own = lax.all_to_all(y_pay, "z", 0, 0, tiled=True)
    mine, own_mask, theirs, x_late = call(
        aggregate_kernel,
        (sel, sel_pair, adj, adj_pair, y_own, x_all),
        [((rows, T), F32), ((chips, T), F32), ((rows + chips, T), F32), (x_all.shape, BF16)],
        in_specs=[SMEM] * 2 + [VMEM] * 3 + [ANY],
        out_specs=[VMEM] * 3 + [ANY],
        aliases={5: 3},
    )
    came = lax.ppermute(theirs, "c", swap)
    (z_self,) = call(self_kernel, (x_late, w_self), [((rows, T), F32)])
    output, gt, c_pay, mask = call(
        activation_kernel,
        (adj, inverse, mine, own_mask, came, z_self, out_grad),
        [((rows, T), BF16), ((T, rows), BF16), ((groups, T, T), BF16), ((groups, T), F32)],
    )
    c_all = lax.all_to_all(c_pay, ("z", "c"), 0, 0, tiled=True)
    bt, keep, send = call(
        weight_grad_kernel,
        (c_all, mask, gt, x_late),
        [((T, rows), BF16), ((chips, 2 * T, T), F32), ((chips, 2 * T, T), BF16)],
    )
    came = lax.ppermute(send, "c", swap)
    (p_pay,) = call(
        feature_grad_kernel,
        (gt, bt, w_self, w_neigh),
        [((parts, T, rows), BF16)],
        out_specs=[HBM],
        scratch=[pltpu.VMEM((parts, T, rows), BF16), pltpu.SemaphoreType.DMA((parts,))],
    )
    block = (2 * T, T)
    three, two, part, own, p_pay = call(
        pair_kernel,
        (keep, came, p_pay),
        [((3,) + block, BF16), ((2,) + block, BF16), ((2,) + block, F32), (block, F32), (p_pay.shape, BF16)],
        in_specs=[VMEM, VMEM, HBM],
        out_specs=[VMEM] * 4 + [HBM],
        aliases={2: 4},
    )
    p_all = lax.all_to_all(p_pay, "f", 0, 0, tiled=True)
    one, fold = call(
        relay_kernel,
        (part, own, along(three, 3, chips), along(two, 2, chips)),
        [((2,) + block, BF16), ((2,) + block, F32)],
    )
    mine, theirs = call(fold_kernel, (fold, along(one, 1, chips)), [(block, F32)] * 2)
    (grad_features,) = call(sum_kernel, (p_all,), [((rows, T), BF16)])
    grad_self, grad_neigh, grad_features = call(
        last_kernel,
        (mine, lax.ppermute(theirs, "c", swap), grad_features),
        [((T, T), F32), ((T, T), F32), ((rows, T), BF16)],
        in_specs=[VMEM, VMEM, ANY],
        out_specs=[VMEM, VMEM, ANY],
        aliases={2: 2},
    )
    return output, grad_features, grad_self, grad_neigh


def solution(mesh):
    row_count, part_count = mesh.shape["rows"], mesh.shape["feat"]
    split = Mesh(mesh.devices.reshape(row_count // 2, 2, part_count), ("z", "c", "f"))
    rows, feat = ("z", "c"), "f"
    return jax.shard_map(
        functools.partial(per_device, chips=row_count // 2, parts=part_count),
        mesh=split,
        in_specs=(
            P(rows, feat),
            P(None, feat),
            P(None, feat),
            P(rows, feat),
            P(rows),
            P(rows, None),
            P(rows, None),
            P(rows, None, None, None),
        ),
        out_specs=(P(rows, feat),) * 4,
        check_vma=False,
    )
```

```python
import functools

import jax
import jax.numpy as jnp
from jax import lax
from jax.experimental import pallas as pl
from jax.experimental.pallas import tpu as pltpu
from jax.sharding import Mesh, PartitionSpec as P

F32 = jnp.float32
BF16 = jnp.bfloat16
T = 128
CHUNK = 10
MIB = 1024 * 1024
VMEM = pl.BlockSpec(memory_space=pltpu.VMEM)
SMEM = pl.BlockSpec(memory_space=pltpu.SMEM)
ANY = pl.BlockSpec(memory_space=pl.ANY)
HBM = pl.BlockSpec(memory_space=pltpu.HBM)


def dot(a, b):
    return jnp.dot(a, b, preferred_element_type=F32)


def far_first(chips):
    return tuple(sorted(range(1, chips), key=lambda step: abs(step - chips // 2)))


def halves(block):
    high = block.astype(BF16)
    return jnp.concatenate([high, (block - high.astype(F32)).astype(BF16)], axis=0)


def spread_kernel(x_hbm, pay_ref, x_ref, in_sem, sems):
    copies = [
        pltpu.make_async_copy(x_ref, pay_ref.at[copy], sems.at[copy]) for copy in range(pay_ref.shape[0])
    ]
    came = pltpu.make_async_copy(x_hbm, x_ref, in_sem)
    came.start()
    came.wait()
    for copy in copies:
        copy.start()
    for copy in copies:
        copy.wait()


def adjacency_kernel(
    count_ref, dst_hbm, src_hbm, weight_ref, adj_ref, send_ref, inv_ref, flag_ref,
    dst_ref, src_ref, buf, acc, sel_ref, in_sems, sems,
):
    count = count_ref[0]
    slots = weight_ref.shape[0]
    groups = acc.shape[0]

    def chunk_copy(index):
        part = pl.ds(index * CHUNK, CHUNK)
        return pltpu.make_async_copy(weight_ref.at[part], buf.at[part], sems.at[index])

    ins = [
        pltpu.make_async_copy(source, target, in_sems.at[index])
        for index, (source, target) in enumerate(((dst_hbm, dst_ref), (src_hbm, src_ref)))
    ]
    for copy in ins:
        copy.start()
    for index in range(slots // CHUNK):

        @pl.when(index * CHUNK < count)
        def _():
            chunk_copy(index).start()

    acc[...] = jnp.zeros_like(acc)
    for owner in range(groups):
        sel_ref[owner] = 0
    for copy in ins:
        copy.wait()
    for index in range(slots // CHUNK):

        @pl.when(index * CHUNK < count)
        def _():
            chunk_copy(index).wait()

            def add_tile(slot, carry):
                source = src_ref[0, slot]
                owner = source // 2
                sel_ref[owner] = source - 2 * owner
                rows = pl.ds(pl.multiple_of(dst_ref[0, slot] * T, T), T)
                acc[owner, rows, :] = acc[owner, rows, :] + buf[slot]
                return carry

            lax.fori_loop(index * CHUNK, jnp.minimum(count, (index + 1) * CHUNK), add_tile, 0)

    total = acc[0]
    for owner in range(groups):
        if owner > 0:
            total = total + acc[owner]
        adj_ref[owner] = acc[owner].astype(F32).astype(BF16)
    other = 1 - lax.axis_index("c")
    for chip in range(send_ref.shape[0]):
        send_ref[chip] = adj_ref[2 * chip + other]
    degree = jnp.sum(total.astype(F32), axis=1, keepdims=True)
    inv_ref[...] = jnp.broadcast_to(1.0 / jnp.maximum(degree, 1.0), inv_ref.shape)
    row = lax.broadcasted_iota(jnp.int32, flag_ref.shape, 0)
    flags = jnp.zeros(flag_ref.shape, F32)
    for owner in range(groups):
        flags = jnp.where(row == owner, sel_ref[owner].astype(F32), flags)
    flag_ref[...] = flags


def wide_dot(x_ref, w_ref):
    total = None
    for part in range(0, x_ref.shape[0], 2):
        pair = jnp.concatenate([x_ref[part], x_ref[part + 1]], axis=1)
        product = dot(pair, w_ref[part * T : (part + 2) * T, :])
        total = product if total is None else total + product
    return total


def neighbour_kernel(x_ref, w_ref, flag_ref, pair_flag_ref, adj_ref, pay_ref, flag_same_ref, adj_same_ref):
    rows = x_ref.shape[1]
    product = wide_dot(x_ref, w_ref).astype(BF16)
    flags = flag_ref[...].astype(BF16)
    for copy in range(pay_ref.shape[0]):
        pay_ref[copy, 0:rows, :] = product
        pay_ref[copy, rows:, :] = flags


def self_kernel(x_ref, w_ref, z_ref):
    z_ref[...] = wide_dot(x_ref, w_ref)


def aggregate_kernel(
    flag_ref, flag_pair_ref, adj_ref, adj_pair_ref, y_ref, x_ref, mine_ref, mask_ref, theirs_ref, x_same_ref
):
    core = lax.axis_index("c")
    here = 2 * lax.axis_index("z")
    chips = y_ref.shape[0]
    rows = mine_ref.shape[0]
    row = lax.broadcasted_iota(jnp.int32, (y_ref.shape[1] - rows, T), 0)

    def summed(adj, flag):
        total = jnp.zeros(mine_ref.shape, F32)
        for first in range(0, chips, 2):
            blocks, tiles = [], []
            for chip in (first, first + 1):
                high = flag[pl.ds(2 * chip + core, 1), :] > 0.5
                blocks.append(adj(chip))
                low_tile = y_ref[chip, 0:T, :].astype(F32)
                high_tile = y_ref[chip, T : 2 * T, :].astype(F32)
                tiles.append(jnp.where(high, high_tile, low_tile).astype(BF16))
            total = total + dot(jnp.concatenate(blocks, axis=1), jnp.concatenate(tiles, axis=0))
        return total

    theirs_ref[0:rows] = summed(lambda chip: adj_pair_ref[chip], flag_pair_ref)
    mine_ref[...] = summed(lambda chip: adj_ref[2 * chip + core], flag_ref)
    for chip in range(chips):
        flags = y_ref[chip, rows:, :].astype(F32)
        mask_ref[chip : chip + 1, :] = jnp.sum(
            jnp.where(row == here + core, flags, 0.0), axis=0, keepdims=True
        )
        theirs_ref[rows + chip : rows + chip + 1, :] = jnp.sum(
            jnp.where(row == here + 1 - core, flags, 0.0), axis=0, keepdims=True
        )


def activation_kernel(
    adj_ref, inv_ref, mine_ref, own_mask_ref, came_ref, z_ref, og_ref, out_ref, gt_ref, pay_ref, mask_ref
):
    core = lax.axis_index("c")
    rows = z_ref.shape[0]
    chips = own_mask_ref.shape[0]
    mask_ref[pl.ds(pl.multiple_of(core * chips, chips), chips), :] = own_mask_ref[...]
    mask_ref[pl.ds(pl.multiple_of((1 - core) * chips, chips), chips), :] = came_ref[rows:, :]
    inverse = inv_ref[...]
    z = z_ref[...] + inverse * (mine_ref[...] + came_ref[0:rows])
    sig = 1.0 / (1.0 + jnp.exp(-z))
    grad = (og_ref[...].astype(F32) * sig * (1.0 + z * (1.0 - sig))).astype(BF16).astype(F32)
    scaled = halves((grad * inverse).T)
    for owner in range(0, pay_ref.shape[0], 2):
        spread = dot(scaled, jnp.concatenate([adj_ref[owner], adj_ref[owner + 1]], axis=1))
        spread = (spread[0:T] + spread[T:]).astype(BF16)
        pay_ref[owner] = spread[:, 0:T]
        pay_ref[owner + 1] = spread[:, T:]
    out_ref[...] = (z * sig).astype(BF16)
    gt_ref[...] = grad.T.astype(BF16)


def weight_grad_kernel(came_ref, mask_ref, gt_ref, x_ref, bt_ref, keep_ref, send_ref):
    core = lax.axis_index("c")
    here = lax.axis_index("z")
    chips = keep_ref.shape[0]
    low = jnp.zeros((T, T), F32)
    high = jnp.zeros((T, T), F32)
    for sender in range(came_ref.shape[0]):
        came = came_ref[sender].astype(F32)
        place = sender % 2 * chips + sender // 2
        is_high = mask_ref[place : place + 1, :] > 0.5
        low = low + jnp.where(is_high, 0.0, came)
        high = high + jnp.where(is_high, came, 0.0)
    both = halves(jnp.concatenate([low, high], axis=1))
    bt_ref[...] = both[0:T]
    left = jnp.concatenate([gt_ref[...], both], axis=0)
    for slot, step in enumerate(far_first(chips) + (0,)):
        chip = lax.rem(here + step, chips)
        pair = jnp.concatenate([x_ref[2 * chip + core], x_ref[2 * chip + 1 - core]], axis=1)
        total = dot(left, pair)
        kept, sent = total[:, 0:T], total[:, T:]
        keep_ref[slot, 0:T] = kept[0:T]
        keep_ref[slot, T:] = kept[T : 2 * T] + kept[2 * T :]
        send_ref[slot, 0:T] = sent[0:T].astype(BF16)
        send_ref[slot, T:] = (sent[T : 2 * T] + sent[2 * T :]).astype(BF16)


def feature_grad_kernel(gt_ref, bt_ref, ws_ref, wn_ref, pay_ref, buf, sems):
    right = jnp.concatenate([gt_ref[...], bt_ref[...]], axis=0)
    copies = []
    for part in range(pay_ref.shape[0]):
        span = slice(part * T, (part + 1) * T)
        left = jnp.concatenate([ws_ref[span, :], wn_ref[span, :]], axis=1)
        buf[part] = dot(left, right).astype(BF16)
        copies.append(pltpu.make_async_copy(buf.at[part], pay_ref.at[part], sems.at[part]))
        copies[-1].start()
    for copy in copies:
        copy.wait()


def pair_kernel(keep_ref, came_ref, payload_ref, *pay_refs):
    for slot, pay_ref in enumerate(pay_refs[:-1]):
        pay_ref[...] = (keep_ref[slot] + came_ref[slot].astype(F32)).astype(pay_ref.dtype)


def weight_sum_kernel(own_ref, done_ref, *refs):
    parts, (self_ref, neigh_ref, same_ref) = refs[:-3], refs[-3:]
    total = own_ref[...]
    for part in parts:
        total = total + part[...].astype(F32)
    self_ref[...] = total[0:T].T
    neigh_ref[...] = total[T:].T


def sum_kernel(parts_ref, out_ref):
    total = parts_ref[0].astype(F32)
    for part in range(1, parts_ref.shape[0]):
        total = total + parts_ref[part].astype(F32)
    out_ref[...] = total.T.astype(out_ref.dtype)


def call(kernel, ins, outs, in_specs=None, out_specs=None, scratch=(), limit=12, aliases=None):
    shapes = tuple(
        pltpu.HBM(shape, dtype) if spec is HBM else jax.ShapeDtypeStruct(shape, dtype)
        for (shape, dtype), spec in zip(outs, out_specs or [VMEM] * len(outs))
    )
    ins = [
        pltpu.with_memory_space_constraint(value, pltpu.HBM) if spec is HBM else value
        for value, spec in zip(ins, in_specs or [VMEM] * len(ins))
    ]
    return pl.pallas_call(
        kernel,
        out_shape=shapes,
        in_specs=in_specs or [VMEM] * len(ins),
        out_specs=tuple(out_specs or [VMEM] * len(outs)),
        scratch_shapes=list(scratch),
        input_output_aliases=aliases or {},
        compiler_params=pltpu.CompilerParams(vmem_limit_bytes=limit * MIB),
        name=kernel.__name__,
    )(*ins)


def per_device(features, w_self, w_neigh, out_grad, tile_count, tile_dst, tile_src, tile_weight, chips, parts):
    rows = features.shape[0]
    groups = 2 * chips
    slots = tile_weight.shape[1]
    swap = [(0, 1), (1, 0)]

    (x_pay,) = call(
        spread_kernel,
        (features,),
        [((parts, rows, T), BF16)],
        in_specs=[HBM],
        out_specs=[HBM],
        scratch=[pltpu.VMEM((rows, T), BF16), pltpu.SemaphoreType.DMA, pltpu.SemaphoreType.DMA((parts,))],
    )
    x_all = lax.all_to_all(x_pay, "f", 0, 0, tiled=True)
    adj, adj_send, inverse, flags = call(
        adjacency_kernel,
        (tile_count, tile_dst, tile_src, tile_weight[0]),
        [
            ((groups, rows, T), BF16),
            ((chips, rows, T), BF16),
            ((rows, T), F32),
            ((groups, T), F32),
        ],
        in_specs=[SMEM, HBM, HBM, HBM],
        scratch=[
            pltpu.SMEM(tile_dst.shape, jnp.int32),
            pltpu.SMEM(tile_src.shape, jnp.int32),
            pltpu.VMEM((slots, T, T), jnp.int32),
            pltpu.VMEM((groups, rows, T), jnp.int32),
            pltpu.SMEM((groups,), jnp.int32),
            pltpu.SemaphoreType.DMA((2,)),
            pltpu.SemaphoreType.DMA((slots // CHUNK,)),
        ],
        limit=20,
    )
    adj_pair = lax.ppermute(adj_send, "c", swap)
    y_pay, flags_pair, adj_pair = call(
        neighbour_kernel,
        (x_all, w_neigh, flags, lax.ppermute(flags, "c", swap), adj_pair),
        [((chips, rows + groups, T), BF16), (flags.shape, F32), (adj_pair.shape, BF16)],
        in_specs=[VMEM] * 3 + [ANY, HBM],
        out_specs=[VMEM, ANY, HBM],
        aliases={3: 1, 4: 2},
    )
    y_own = lax.all_to_all(y_pay, "z", 0, 0, tiled=True)
    mine, own_mask, theirs, x_late = call(
        aggregate_kernel,
        (flags, flags_pair, adj, adj_pair, y_own, x_all),
        [((rows, T), F32), ((chips, T), F32), ((rows + chips, T), F32), (x_all.shape, BF16)],
        in_specs=[VMEM] * 5 + [ANY],
        out_specs=[VMEM] * 3 + [ANY],
        aliases={5: 3},
    )
    came = lax.ppermute(theirs, "c", swap)
    (z_self,) = call(self_kernel, (x_late, w_self), [((rows, T), F32)])
    output, gt, c_pay, mask = call(
        activation_kernel,
        (adj, inverse, mine, own_mask, came, z_self, out_grad),
        [((rows, T), BF16), ((T, rows), BF16), ((groups, T, T), BF16), ((groups, T), F32)],
    )
    c_all = lax.all_to_all(c_pay, ("z", "c"), 0, 0, tiled=True)
    bt, keep, send = call(
        weight_grad_kernel,
        (c_all, mask, gt, x_late),
        [((T, rows), BF16), ((chips, 2 * T, T), F32), ((chips, 2 * T, T), BF16)],
    )
    came = lax.ppermute(send, "c", swap)
    (p_pay,) = call(
        feature_grad_kernel,
        (gt, bt, w_self, w_neigh),
        [((parts, T, rows), BF16)],
        out_specs=[HBM],
        scratch=[pltpu.VMEM((parts, T, rows), BF16), pltpu.SemaphoreType.DMA((parts,))],
    )
    *w_pay, own, p_pay = call(
        pair_kernel,
        (keep, came, p_pay),
        [((2 * T, T), BF16)] * (chips - 1) + [((2 * T, T), F32), (p_pay.shape, BF16)],
        in_specs=[VMEM, VMEM, HBM],
        out_specs=[VMEM] * chips + [HBM],
        aliases={2: chips},
    )
    p_all = lax.all_to_all(p_pay, "f", 0, 0, tiled=True)
    w_came = [
        lax.ppermute(block, "z", [(chip, (chip + step) % chips) for chip in range(chips)])
        for step, block in zip(far_first(chips), w_pay)
    ]
    (grad_features,) = call(sum_kernel, (p_all,), [((rows, T), BF16)])
    grad_self, grad_neigh, grad_features = call(
        weight_sum_kernel,
        (own, grad_features, *w_came),
        [((T, T), F32), ((T, T), F32), ((rows, T), BF16)],
        in_specs=[VMEM, ANY] + [VMEM] * (chips - 1),
        out_specs=[VMEM, VMEM, ANY],
        aliases={1: 2},
    )
    return output, grad_features, grad_self, grad_neigh


def solution(mesh):
    row_count, part_count = mesh.shape["rows"], mesh.shape["feat"]
    split = Mesh(mesh.devices.reshape(row_count // 2, 2, part_count), ("z", "c", "f"))
    rows, feat = ("z", "c"), "f"
    return jax.shard_map(
        functools.partial(per_device, chips=row_count // 2, parts=part_count),
        mesh=split,
        in_specs=(
            P(rows, feat),
            P(None, feat),
            P(None, feat),
            P(rows, feat),
            P(rows),
            P(rows, None),
            P(rows, None),
            P(rows, None, None, None),
        ),
        out_specs=(P(rows, feat),) * 4,
        check_vma=False,
    )
```

```python
import functools

import jax
import jax.numpy as jnp
from jax import lax
from jax.experimental import pallas as pl
from jax.experimental.pallas import tpu as pltpu
from jax.sharding import Mesh, PartitionSpec as P

F32 = jnp.float32
BF16 = jnp.bfloat16
T = 128
CHUNK = 10
MIB = 1024 * 1024
VMEM = pl.BlockSpec(memory_space=pltpu.VMEM)
SMEM = pl.BlockSpec(memory_space=pltpu.SMEM)
ANY = pl.BlockSpec(memory_space=pl.ANY)
HBM = pl.BlockSpec(memory_space=pltpu.HBM)


def dot(a, b):
    return jnp.dot(a, b, preferred_element_type=F32)


def owners(here, core, chips):
    way = 1 - 2 * core

    def chip(step):
        return lax.rem(here + step + chips, chips)

    far = 2 * chip(chips // 2) + 1 - core
    three, two, one = (2 * chip(step * way) for step in (3, 2, 1))
    return [far, three, three + 1, two, two + 1, one, one + 1, 2 * here + core]


def halves(block):
    high = block.astype(BF16)
    return jnp.concatenate([high, (block - high.astype(F32)).astype(BF16)], axis=0)


def spread_kernel(x_hbm, pay_ref, x_ref, in_sem, sems):
    copies = [
        pltpu.make_async_copy(x_ref, pay_ref.at[copy], sems.at[copy]) for copy in range(pay_ref.shape[0])
    ]
    came = pltpu.make_async_copy(x_hbm, x_ref, in_sem)
    came.start()
    came.wait()
    for copy in copies:
        copy.start()
    for copy in copies:
        copy.wait()


def adjacency_kernel(
    count_ref, dst_hbm, src_hbm, weight_ref, adj_ref, send_ref, inv_ref, flag_ref,
    dst_ref, src_ref, buf, acc, sel_ref, in_sems, sems,
):
    count = count_ref[0]
    slots = weight_ref.shape[0]
    groups = acc.shape[0]

    def chunk_copy(index):
        part = pl.ds(index * CHUNK, CHUNK)
        return pltpu.make_async_copy(weight_ref.at[part], buf.at[part], sems.at[index])

    ins = [
        pltpu.make_async_copy(source, target, in_sems.at[index])
        for index, (source, target) in enumerate(((dst_hbm, dst_ref), (src_hbm, src_ref)))
    ]
    for copy in ins:
        copy.start()
    for index in range(slots // CHUNK):

        @pl.when(index * CHUNK < count)
        def _():
            chunk_copy(index).start()

    acc[...] = jnp.zeros_like(acc)
    for owner in range(groups):
        sel_ref[owner] = 0
    for copy in ins:
        copy.wait()
    for index in range(slots // CHUNK):

        @pl.when(index * CHUNK < count)
        def _():
            chunk_copy(index).wait()

            def add_tile(slot, carry):
                source = src_ref[0, slot]
                owner = source // 2
                sel_ref[owner] = source - 2 * owner
                rows = pl.ds(pl.multiple_of(dst_ref[0, slot] * T, T), T)
                acc[owner, rows, :] = acc[owner, rows, :] + buf[slot]
                return carry

            lax.fori_loop(index * CHUNK, jnp.minimum(count, (index + 1) * CHUNK), add_tile, 0)

    total = acc[0]
    for owner in range(groups):
        if owner > 0:
            total = total + acc[owner]
        adj_ref[owner] = acc[owner].astype(F32).astype(BF16)
    other = 1 - lax.axis_index("c")
    for chip in range(send_ref.shape[0]):
        send_ref[chip] = adj_ref[2 * chip + other]
    degree = jnp.sum(total.astype(F32), axis=1, keepdims=True)
    inv_ref[...] = jnp.broadcast_to(1.0 / jnp.maximum(degree, 1.0), inv_ref.shape)
    row = lax.broadcasted_iota(jnp.int32, flag_ref.shape, 0)
    flags = jnp.zeros(flag_ref.shape, F32)
    for owner in range(groups):
        flags = jnp.where(row == owner, sel_ref[owner].astype(F32), flags)
    flag_ref[...] = flags


def wide_dot(x_ref, w_ref):
    total = None
    for part in range(0, x_ref.shape[0], 2):
        pair = jnp.concatenate([x_ref[part], x_ref[part + 1]], axis=1)
        product = dot(pair, w_ref[part * T : (part + 2) * T, :])
        total = product if total is None else total + product
    return total


def neighbour_kernel(x_ref, w_ref, flag_ref, pair_flag_ref, adj_ref, pay_ref, flag_same_ref, adj_same_ref):
    rows = x_ref.shape[1]
    product = wide_dot(x_ref, w_ref).astype(BF16)
    flags = flag_ref[...].astype(BF16)
    for copy in range(pay_ref.shape[0]):
        pay_ref[copy, 0:rows, :] = product
        pay_ref[copy, rows:, :] = flags


def self_kernel(x_ref, w_ref, z_ref):
    z_ref[...] = wide_dot(x_ref, w_ref)


def aggregate_kernel(
    flag_ref, flag_pair_ref, adj_ref, adj_pair_ref, y_ref, x_ref, mine_ref, mask_ref, theirs_ref, x_same_ref
):
    core = lax.axis_index("c")
    here = 2 * lax.axis_index("z")
    chips = y_ref.shape[0]
    rows = mine_ref.shape[0]
    row = lax.broadcasted_iota(jnp.int32, (y_ref.shape[1] - rows, T), 0)

    def summed(adj, flag):
        total = jnp.zeros(mine_ref.shape, F32)
        for first in range(0, chips, 2):
            blocks, tiles = [], []
            for chip in (first, first + 1):
                high = flag[pl.ds(2 * chip + core, 1), :] > 0.5
                blocks.append(adj(chip))
                low_tile = y_ref[chip, 0:T, :].astype(F32)
                high_tile = y_ref[chip, T : 2 * T, :].astype(F32)
                tiles.append(jnp.where(high, high_tile, low_tile).astype(BF16))
            total = total + dot(jnp.concatenate(blocks, axis=1), jnp.concatenate(tiles, axis=0))
        return total

    theirs_ref[0:rows] = summed(lambda chip: adj_pair_ref[chip], flag_pair_ref)
    mine_ref[...] = summed(lambda chip: adj_ref[2 * chip + core], flag_ref)
    for chip in range(chips):
        flags = y_ref[chip, rows:, :].astype(F32)
        mask_ref[chip : chip + 1, :] = jnp.sum(
            jnp.where(row == here + core, flags, 0.0), axis=0, keepdims=True
        )
        theirs_ref[rows + chip : rows + chip + 1, :] = jnp.sum(
            jnp.where(row == here + 1 - core, flags, 0.0), axis=0, keepdims=True
        )


def activation_kernel(
    adj_ref, inv_ref, mine_ref, own_mask_ref, came_ref, z_ref, og_ref, out_ref, gt_ref, pay_ref, mask_ref
):
    core = lax.axis_index("c")
    rows = z_ref.shape[0]
    chips = own_mask_ref.shape[0]
    mask_ref[pl.ds(pl.multiple_of(core * chips, chips), chips), :] = own_mask_ref[...]
    mask_ref[pl.ds(pl.multiple_of((1 - core) * chips, chips), chips), :] = came_ref[rows:, :]
    inverse = inv_ref[...]
    z = z_ref[...] + inverse * (mine_ref[...] + came_ref[0:rows])
    sig = 1.0 / (1.0 + jnp.exp(-z))
    grad = (og_ref[...].astype(F32) * sig * (1.0 + z * (1.0 - sig))).astype(BF16).astype(F32)
    scaled = halves((grad * inverse).T)
    for owner in range(0, pay_ref.shape[0], 2):
        spread = dot(scaled, jnp.concatenate([adj_ref[owner], adj_ref[owner + 1]], axis=1))
        spread = (spread[0:T] + spread[T:]).astype(BF16)
        pay_ref[owner] = spread[:, 0:T]
        pay_ref[owner + 1] = spread[:, T:]
    out_ref[...] = (z * sig).astype(BF16)
    gt_ref[...] = grad.T.astype(BF16)


def weight_grad_kernel(came_ref, mask_ref, gt_ref, x_ref, bt_ref, keep_ref, send_ref):
    core = lax.axis_index("c")
    here = lax.axis_index("z")
    chips = keep_ref.shape[0]
    low = jnp.zeros((T, T), F32)
    high = jnp.zeros((T, T), F32)
    for sender in range(came_ref.shape[0]):
        came = came_ref[sender].astype(F32)
        place = sender % 2 * chips + sender // 2
        is_high = mask_ref[place : place + 1, :] > 0.5
        low = low + jnp.where(is_high, 0.0, came)
        high = high + jnp.where(is_high, came, 0.0)
    both = halves(jnp.concatenate([low, high], axis=1))
    bt_ref[...] = both[0:T]
    left = jnp.concatenate([gt_ref[...], both], axis=0)
    slots = zip(owners(here, core, chips), owners(here, 1 - core, chips))
    for slot, (ours, theirs) in enumerate(slots):
        total = dot(left, jnp.concatenate([x_ref[ours], x_ref[theirs]], axis=1))
        kept, sent = total[:, 0:T], total[:, T:]
        keep_ref[slot, 0:T] = kept[0:T]
        keep_ref[slot, T:] = kept[T : 2 * T] + kept[2 * T :]
        send_ref[slot, 0:T] = sent[0:T].astype(BF16)
        send_ref[slot, T:] = (sent[T : 2 * T] + sent[2 * T :]).astype(BF16)


def feature_grad_kernel(gt_ref, bt_ref, ws_ref, wn_ref, pay_ref, buf, sems):
    right = jnp.concatenate([gt_ref[...], bt_ref[...]], axis=0)
    copies = []
    for part in range(pay_ref.shape[0]):
        span = slice(part * T, (part + 1) * T)
        left = jnp.concatenate([ws_ref[span, :], wn_ref[span, :]], axis=1)
        buf[part] = dot(left, right).astype(BF16)
        copies.append(pltpu.make_async_copy(buf.at[part], pay_ref.at[part], sems.at[part]))
        copies[-1].start()
    for copy in copies:
        copy.wait()


def pair_kernel(keep_ref, came_ref, payload_ref, far_ref, three_ref, two_ref, one_ref, own_ref, same_ref):
    def pair(slot):
        return keep_ref[slot] + came_ref[slot].astype(F32)

    far_ref[...] = pair(0).astype(BF16)
    for index, ref in enumerate((three_ref, two_ref, one_ref)):
        for place in range(2):
            ref[place] = pair(1 + 2 * index + place).astype(BF16)
    own_ref[...] = pair(7)


def fold_kernel(own_ref, far_ref, three_ref, two_ref, one_ref, mine_ref, theirs_ref):
    core = lax.axis_index("c")
    mine, theirs = own_ref[...] + far_ref[...].astype(F32), jnp.zeros(own_ref.shape, F32)
    for ref in (three_ref, two_ref, one_ref):
        mine = mine + ref[core].astype(F32)
        theirs = theirs + ref[1 - core].astype(F32)
    theirs_ref[...] = theirs
    mine_ref[...] = mine


def last_kernel(mine_ref, came_ref, done_ref, self_ref, neigh_ref, same_ref):
    total = mine_ref[...] + came_ref[...]
    self_ref[...] = total[0:T].T
    neigh_ref[...] = total[T:].T


def sum_kernel(parts_ref, out_ref):
    total = parts_ref[0].astype(F32)
    for part in range(1, parts_ref.shape[0]):
        total = total + parts_ref[part].astype(F32)
    out_ref[...] = total.T.astype(out_ref.dtype)


def call(kernel, ins, outs, in_specs=None, out_specs=None, scratch=(), limit=12, aliases=None):
    shapes = tuple(
        pltpu.HBM(shape, dtype) if spec is HBM else jax.ShapeDtypeStruct(shape, dtype)
        for (shape, dtype), spec in zip(outs, out_specs or [VMEM] * len(outs))
    )
    ins = [
        pltpu.with_memory_space_constraint(value, pltpu.HBM) if spec is HBM else value
        for value, spec in zip(ins, in_specs or [VMEM] * len(ins))
    ]
    return pl.pallas_call(
        kernel,
        out_shape=shapes,
        in_specs=in_specs or [VMEM] * len(ins),
        out_specs=tuple(out_specs or [VMEM] * len(outs)),
        scratch_shapes=list(scratch),
        input_output_aliases=aliases or {},
        compiler_params=pltpu.CompilerParams(vmem_limit_bytes=limit * MIB),
        name=kernel.__name__,
    )(*ins)


def along(value, step, chips):
    pairs = [(2 * chip, 2 * ((chip + step) % chips)) for chip in range(chips)]
    pairs += [(2 * chip + 1, 2 * ((chip - step) % chips) + 1) for chip in range(chips)]
    return lax.ppermute(value, ("z", "c"), pairs)


def per_device(features, w_self, w_neigh, out_grad, tile_count, tile_dst, tile_src, tile_weight, chips, parts):
    rows = features.shape[0]
    groups = 2 * chips
    slots = tile_weight.shape[1]
    swap = [(0, 1), (1, 0)]

    (x_pay,) = call(
        spread_kernel,
        (features,),
        [((parts, rows, T), BF16)],
        in_specs=[HBM],
        out_specs=[HBM],
        scratch=[pltpu.VMEM((rows, T), BF16), pltpu.SemaphoreType.DMA, pltpu.SemaphoreType.DMA((parts,))],
    )
    x_all = lax.all_to_all(x_pay, "f", 0, 0, tiled=True)
    adj, adj_send, inverse, flags = call(
        adjacency_kernel,
        (tile_count, tile_dst, tile_src, tile_weight[0]),
        [
            ((groups, rows, T), BF16),
            ((chips, rows, T), BF16),
            ((rows, T), F32),
            ((groups, T), F32),
        ],
        in_specs=[SMEM, HBM, HBM, HBM],
        scratch=[
            pltpu.SMEM(tile_dst.shape, jnp.int32),
            pltpu.SMEM(tile_src.shape, jnp.int32),
            pltpu.VMEM((slots, T, T), jnp.int32),
            pltpu.VMEM((groups, rows, T), jnp.int32),
            pltpu.SMEM((groups,), jnp.int32),
            pltpu.SemaphoreType.DMA((2,)),
            pltpu.SemaphoreType.DMA((slots // CHUNK,)),
        ],
        limit=20,
    )
    adj_pair = lax.ppermute(adj_send, "c", swap)
    y_pay, flags_pair, adj_pair = call(
        neighbour_kernel,
        (x_all, w_neigh, flags, lax.ppermute(flags, "c", swap), adj_pair),
        [((chips, rows + groups, T), BF16), (flags.shape, F32), (adj_pair.shape, BF16)],
        in_specs=[VMEM] * 3 + [ANY, HBM],
        out_specs=[VMEM, ANY, HBM],
        aliases={3: 1, 4: 2},
    )
    y_own = lax.all_to_all(y_pay, "z", 0, 0, tiled=True)
    mine, own_mask, theirs, x_late = call(
        aggregate_kernel,
        (flags, flags_pair, adj, adj_pair, y_own, x_all),
        [((rows, T), F32), ((chips, T), F32), ((rows + chips, T), F32), (x_all.shape, BF16)],
        in_specs=[VMEM] * 5 + [ANY],
        out_specs=[VMEM] * 3 + [ANY],
        aliases={5: 3},
    )
    came = lax.ppermute(theirs, "c", swap)
    (z_self,) = call(self_kernel, (x_late, w_self), [((rows, T), F32)])
    output, gt, c_pay, mask = call(
        activation_kernel,
        (adj, inverse, mine, own_mask, came, z_self, out_grad),
        [((rows, T), BF16), ((T, rows), BF16), ((groups, T, T), BF16), ((groups, T), F32)],
    )
    c_all = lax.all_to_all(c_pay, ("z", "c"), 0, 0, tiled=True)
    bt, keep, send = call(
        weight_grad_kernel,
        (c_all, mask, gt, x_late),
        [((T, rows), BF16), ((chips, 2 * T, T), F32), ((chips, 2 * T, T), BF16)],
    )
    came = lax.ppermute(send, "c", swap)
    (p_pay,) = call(
        feature_grad_kernel,
        (gt, bt, w_self, w_neigh),
        [((parts, T, rows), BF16)],
        out_specs=[HBM],
        scratch=[pltpu.VMEM((parts, T, rows), BF16), pltpu.SemaphoreType.DMA((parts,))],
    )
    block = (2 * T, T)
    far, three, two, one, own, p_pay = call(
        pair_kernel,
        (keep, came, p_pay),
        [(block, BF16)] + [((2,) + block, BF16)] * 3 + [(block, F32), (p_pay.shape, BF16)],
        in_specs=[VMEM, VMEM, HBM],
        out_specs=[VMEM] * 5 + [HBM],
        aliases={2: 5},
    )
    p_all = lax.all_to_all(p_pay, "f", 0, 0, tiled=True)
    across = [(chip, (chip + chips // 2) % chips) for chip in range(chips)]
    far = lax.ppermute(lax.ppermute(far, "z", across), "c", swap)
    three, two, one = along(three, 3, chips), along(two, 2, chips), along(one, 1, chips)
    mine, theirs = call(fold_kernel, (own, far, three, two, one), [(block, F32)] * 2)
    (grad_features,) = call(sum_kernel, (p_all,), [((rows, T), BF16)])
    grad_self, grad_neigh, grad_features = call(
        last_kernel,
        (mine, lax.ppermute(theirs, "c", swap), grad_features),
        [((T, T), F32), ((T, T), F32), ((rows, T), BF16)],
        in_specs=[VMEM] * 2 + [ANY],
        out_specs=[VMEM, VMEM, ANY],
        aliases={2: 2},
    )
    return output, grad_features, grad_self, grad_neigh


def solution(mesh):
    row_count, part_count = mesh.shape["rows"], mesh.shape["feat"]
    split = Mesh(mesh.devices.reshape(row_count // 2, 2, part_count), ("z", "c", "f"))
    rows, feat = ("z", "c"), "f"
    return jax.shard_map(
        functools.partial(per_device, chips=row_count // 2, parts=part_count),
        mesh=split,
        in_specs=(
            P(rows, feat),
            P(None, feat),
            P(None, feat),
            P(rows, feat),
            P(rows),
            P(rows, None),
            P(rows, None),
            P(rows, None, None, None),
        ),
        out_specs=(P(rows, feat),) * 4,
        check_vma=False,
    )
```

```python
import functools

import jax
import jax.numpy as jnp
from jax import lax
from jax.experimental import pallas as pl
from jax.experimental.pallas import tpu as pltpu
from jax.sharding import Mesh, PartitionSpec as P

F32 = jnp.float32
BF16 = jnp.bfloat16
T = 128
CHUNK = 10
MIB = 1024 * 1024
VMEM = pl.BlockSpec(memory_space=pltpu.VMEM)
SMEM = pl.BlockSpec(memory_space=pltpu.SMEM)
ANY = pl.BlockSpec(memory_space=pl.ANY)
HBM = pl.BlockSpec(memory_space=pltpu.HBM)


def dot(a, b):
    return jnp.dot(a, b, preferred_element_type=F32)


def far_first(chips):
    return tuple(sorted(range(1, chips), key=lambda step: abs(step - chips // 2)))


def sources(here, core, chips):
    way = 1 - 2 * core
    found = []
    for step in (1, 2, 3):
        chip = lax.rem(here - step * way + chips, chips)
        found += [2 * chip, 2 * chip + 1]
    return found + [2 * lax.rem(here + chips // 2, chips) + core]


def halves(block):
    high = block.astype(BF16)
    return jnp.concatenate([high, (block - high.astype(F32)).astype(BF16)], axis=0)


def spread_kernel(x_hbm, pay_ref, x_ref, in_sem, sems):
    copies = [
        pltpu.make_async_copy(x_ref, pay_ref.at[copy], sems.at[copy]) for copy in range(pay_ref.shape[0])
    ]
    came = pltpu.make_async_copy(x_hbm, x_ref, in_sem)
    came.start()
    came.wait()
    for copy in copies:
        copy.start()
    for copy in copies:
        copy.wait()


def adjacency_kernel(
    count_ref, dst_hbm, src_hbm, weight_ref, adj_ref, send_ref, inv_ref, flag_ref,
    dst_ref, src_ref, buf, acc, sel_ref, in_sems, sems,
):
    count = count_ref[0]
    slots = weight_ref.shape[0]
    groups = acc.shape[0]

    def chunk_copy(index):
        part = pl.ds(index * CHUNK, CHUNK)
        return pltpu.make_async_copy(weight_ref.at[part], buf.at[part], sems.at[index])

    ins = [
        pltpu.make_async_copy(source, target, in_sems.at[index])
        for index, (source, target) in enumerate(((dst_hbm, dst_ref), (src_hbm, src_ref)))
    ]
    for copy in ins:
        copy.start()
    for index in range(slots // CHUNK):

        @pl.when(index * CHUNK < count)
        def _():
            chunk_copy(index).start()

    acc[...] = jnp.zeros_like(acc)
    for owner in range(groups):
        sel_ref[owner] = 0
    for copy in ins:
        copy.wait()
    for index in range(slots // CHUNK):

        @pl.when(index * CHUNK < count)
        def _():
            chunk_copy(index).wait()

            def add_tile(slot, carry):
                source = src_ref[0, slot]
                owner = source // 2
                sel_ref[owner] = source - 2 * owner
                rows = pl.ds(pl.multiple_of(dst_ref[0, slot] * T, T), T)
                acc[owner, rows, :] = acc[owner, rows, :] + buf[slot]
                return carry

            lax.fori_loop(index * CHUNK, jnp.minimum(count, (index + 1) * CHUNK), add_tile, 0)

    total = acc[0]
    for owner in range(groups):
        if owner > 0:
            total = total + acc[owner]
        adj_ref[owner] = acc[owner].astype(F32).astype(BF16)
    for slot, owner in enumerate(sources(lax.axis_index("z"), 1 - lax.axis_index("c"), groups // 2)):
        send_ref[slot] = adj_ref[owner]
    degree = jnp.sum(total.astype(F32), axis=1, keepdims=True)
    inv_ref[...] = jnp.broadcast_to(1.0 / jnp.maximum(degree, 1.0), inv_ref.shape)
    row = lax.broadcasted_iota(jnp.int32, flag_ref.shape, 0)
    flags = jnp.zeros(flag_ref.shape, F32)
    for owner in range(groups):
        flags = jnp.where(row == owner, sel_ref[owner].astype(F32), flags)
    flag_ref[...] = flags


def wide_dot(x_ref, w_ref):
    total = None
    for part in range(0, x_ref.shape[0], 2):
        pair = jnp.concatenate([x_ref[part], x_ref[part + 1]], axis=1)
        product = dot(pair, w_ref[part * T : (part + 2) * T, :])
        total = product if total is None else total + product
    return total


def neighbour_kernel(x_ref, w_ref, flag_ref, pair_flag_ref, adj_ref, pay_ref, flag_same_ref, adj_same_ref):
    rows = x_ref.shape[1]
    product = wide_dot(x_ref, w_ref).astype(BF16)
    flags = flag_ref[...].astype(BF16)
    pay_ref[0:rows, :] = product
    pay_ref[rows:, :] = flags


def join_kernel(y_ref, y_pair_ref, pair_ref):
    core = lax.axis_index("c")
    pair_ref[core] = y_ref[...]
    pair_ref[1 - core] = y_pair_ref[...]


def half_kernel(pair_ref, half_ref):
    half_ref[...] = pair_ref[lax.axis_index("c")]


def self_kernel(x_ref, w_ref, z_ref):
    z_ref[...] = wide_dot(x_ref, w_ref)


def aggregate_kernel(
    flag_ref, flag_pair_ref, adj_ref, adj_pair_ref, pair_ref, one_ref, two_ref, three_ref, far_ref,
    mine_ref, mask_ref, theirs_ref,
):
    core = lax.axis_index("c")
    here = lax.axis_index("z")
    rows = mine_ref.shape[0]
    row = lax.broadcasted_iota(jnp.int32, (far_ref.shape[0] - rows, T), 0)
    blocks = [ref.at[side] for ref in (one_ref, two_ref, three_ref) for side in range(2)] + [far_ref]
    found = sources(here, core, flag_ref.shape[0] // 2)

    def summed(adj, flag, blocks, found):
        tiles = []
        for block, owner in zip(blocks, found):
            high = flag[pl.ds(owner, 1), :] > 0.5
            low_tile = block[0:T, :].astype(F32)
            high_tile = block[T : 2 * T, :].astype(F32)
            tiles.append(jnp.where(high, high_tile, low_tile).astype(BF16))
        return dot(jnp.concatenate(adj, axis=1), jnp.concatenate(tiles, axis=0))

    def mask_row(block, reader):
        return jnp.sum(jnp.where(row == reader, block[rows:, :].astype(F32), 0.0), axis=0, keepdims=True)

    adj_pair = [adj_pair_ref[slot] for slot in range(len(found))]
    theirs_ref[0:rows] = summed(adj_pair, flag_pair_ref, blocks, found)
    theirs_ref[rows:] = jnp.zeros((theirs_ref.shape[0] - rows, T), F32)
    for slot, block in enumerate(blocks):
        theirs_ref[rows + slot : rows + slot + 1, :] = mask_row(block, 2 * here + 1 - core)
    blocks = blocks + [pair_ref.at[0], pair_ref.at[1]]
    found = found + [2 * here, 2 * here + 1]
    mine_ref[...] = summed([adj_ref[owner] for owner in found], flag_ref, blocks, found)
    mask_ref[...] = jnp.zeros_like(mask_ref)
    for block, owner in zip(blocks, found):
        mask_ref[pl.ds(owner, 1), :] = mask_row(block, 2 * here + core)


def activation_kernel(
    adj_ref, inv_ref, mine_ref, own_mask_ref, came_ref, z_ref, og_ref, out_ref, gt_ref, pay_ref, mask_ref
):
    rows = z_ref.shape[0]
    mask_ref[...] = own_mask_ref[...]
    found = sources(lax.axis_index("z"), 1 - lax.axis_index("c"), mask_ref.shape[0] // 2)
    for slot, owner in enumerate(found):
        mask_ref[pl.ds(owner, 1), :] = came_ref[rows + slot : rows + slot + 1, :]
    inverse = inv_ref[...]
    z = z_ref[...] + inverse * (mine_ref[...] + came_ref[0:rows])
    sig = 1.0 / (1.0 + jnp.exp(-z))
    grad = (og_ref[...].astype(F32) * sig * (1.0 + z * (1.0 - sig))).astype(BF16).astype(F32)
    scaled = halves((grad * inverse).T)
    for owner in range(0, pay_ref.shape[0], 2):
        spread = dot(scaled, jnp.concatenate([adj_ref[owner], adj_ref[owner + 1]], axis=1))
        spread = (spread[0:T] + spread[T:]).astype(BF16)
        pay_ref[owner] = spread[:, 0:T]
        pay_ref[owner + 1] = spread[:, T:]
    out_ref[...] = (z * sig).astype(BF16)
    gt_ref[...] = grad.T.astype(BF16)


def weight_grad_kernel(came_ref, mask_ref, gt_ref, x_ref, bt_ref, keep_ref, send_ref):
    core = lax.axis_index("c")
    here = lax.axis_index("z")
    chips = keep_ref.shape[0]
    low = jnp.zeros((T, T), F32)
    high = jnp.zeros((T, T), F32)
    for sender in range(came_ref.shape[0]):
        came = came_ref[sender].astype(F32)
        is_high = mask_ref[sender : sender + 1, :] > 0.5
        low = low + jnp.where(is_high, 0.0, came)
        high = high + jnp.where(is_high, came, 0.0)
    both = halves(jnp.concatenate([low, high], axis=1))
    bt_ref[...] = both[0:T]
    left = jnp.concatenate([gt_ref[...], both], axis=0)
    for slot, step in enumerate(far_first(chips) + (0,)):
        chip = lax.rem(here + step, chips)
        pair = jnp.concatenate([x_ref[2 * chip + core], x_ref[2 * chip + 1 - core]], axis=1)
        total = dot(left, pair)
        kept, sent = total[:, 0:T], total[:, T:]
        keep_ref[slot, 0:T] = kept[0:T]
        keep_ref[slot, T:] = kept[T : 2 * T] + kept[2 * T :]
        send_ref[slot, 0:T] = sent[0:T].astype(BF16)
        send_ref[slot, T:] = (sent[T : 2 * T] + sent[2 * T :]).astype(BF16)


def feature_grad_kernel(gt_ref, bt_ref, ws_ref, wn_ref, pay_ref, buf, sems):
    right = jnp.concatenate([gt_ref[...], bt_ref[...]], axis=0)
    copies = []
    for part in range(pay_ref.shape[0]):
        span = slice(part * T, (part + 1) * T)
        left = jnp.concatenate([ws_ref[span, :], wn_ref[span, :]], axis=1)
        buf[part] = dot(left, right).astype(BF16)
        copies.append(pltpu.make_async_copy(buf.at[part], pay_ref.at[part], sems.at[part]))
        copies[-1].start()
    for copy in copies:
        copy.wait()


def pair_kernel(keep_ref, came_ref, payload_ref, *pay_refs):
    for slot, pay_ref in enumerate(pay_refs[:-1]):
        pay_ref[...] = (keep_ref[slot] + came_ref[slot].astype(F32)).astype(pay_ref.dtype)


def weight_sum_kernel(own_ref, done_ref, *refs):
    parts, (self_ref, neigh_ref, same_ref) = refs[:-3], refs[-3:]
    total = own_ref[...]
    for part in parts:
        total = total + part[...].astype(F32)
    self_ref[...] = total[0:T].T
    neigh_ref[...] = total[T:].T


def sum_kernel(parts_ref, out_ref):
    total = parts_ref[0].astype(F32)
    for part in range(1, parts_ref.shape[0]):
        total = total + parts_ref[part].astype(F32)
    out_ref[...] = total.T.astype(out_ref.dtype)


def call(kernel, ins, outs, in_specs=None, out_specs=None, scratch=(), limit=12, aliases=None):
    shapes = tuple(
        pltpu.HBM(shape, dtype) if spec is HBM else jax.ShapeDtypeStruct(shape, dtype)
        for (shape, dtype), spec in zip(outs, out_specs or [VMEM] * len(outs))
    )
    ins = [
        pltpu.with_memory_space_constraint(value, pltpu.HBM) if spec is HBM else value
        for value, spec in zip(ins, in_specs or [VMEM] * len(ins))
    ]
    return pl.pallas_call(
        kernel,
        out_shape=shapes,
        in_specs=in_specs or [VMEM] * len(ins),
        out_specs=tuple(out_specs or [VMEM] * len(outs)),
        scratch_shapes=list(scratch),
        input_output_aliases=aliases or {},
        compiler_params=pltpu.CompilerParams(vmem_limit_bytes=limit * MIB),
        name=kernel.__name__,
    )(*ins)


def along(value, step, chips):
    pairs = [(2 * chip, 2 * ((chip + step) % chips)) for chip in range(chips)]
    pairs += [(2 * chip + 1, 2 * ((chip - step) % chips) + 1) for chip in range(chips)]
    return lax.ppermute(value, ("z", "c"), pairs)


def per_device(features, w_self, w_neigh, out_grad, tile_count, tile_dst, tile_src, tile_weight, chips, parts):
    rows = features.shape[0]
    groups = 2 * chips
    slots = tile_weight.shape[1]
    swap = [(0, 1), (1, 0)]

    (x_pay,) = call(
        spread_kernel,
        (features,),
        [((parts, rows, T), BF16)],
        in_specs=[HBM],
        out_specs=[HBM],
        scratch=[pltpu.VMEM((rows, T), BF16), pltpu.SemaphoreType.DMA, pltpu.SemaphoreType.DMA((parts,))],
    )
    x_all = lax.all_to_all(x_pay, "f", 0, 0, tiled=True)
    adj, adj_send, inverse, flags = call(
        adjacency_kernel,
        (tile_count, tile_dst, tile_src, tile_weight[0]),
        [
            ((groups, rows, T), BF16),
            ((chips - 1, rows, T), BF16),
            ((rows, T), F32),
            ((groups, T), F32),
        ],
        in_specs=[SMEM, HBM, HBM, HBM],
        scratch=[
            pltpu.SMEM(tile_dst.shape, jnp.int32),
            pltpu.SMEM(tile_src.shape, jnp.int32),
            pltpu.VMEM((slots, T, T), jnp.int32),
            pltpu.VMEM((groups, rows, T), jnp.int32),
            pltpu.SMEM((groups,), jnp.int32),
            pltpu.SemaphoreType.DMA((2,)),
            pltpu.SemaphoreType.DMA((slots // CHUNK,)),
        ],
        limit=20,
    )
    adj_pair = lax.ppermute(adj_send, "c", swap)
    y, flags_pair, adj_pair = call(
        neighbour_kernel,
        (x_all, w_neigh, flags, lax.ppermute(flags, "c", swap), adj_pair),
        [((rows + groups, T), BF16), (flags.shape, F32), (adj_pair.shape, BF16)],
        in_specs=[VMEM] * 3 + [ANY, HBM],
        out_specs=[VMEM, ANY, HBM],
        aliases={3: 1, 4: 2},
    )
    (pair,) = call(join_kernel, (y, lax.ppermute(y, "c", swap)), [((2,) + y.shape, BF16)])
    two, one = along(pair, 2, chips), along(pair, 1, chips)
    (half,) = call(half_kernel, (two,), [(y.shape, BF16)])
    three, far = along(two, 1, chips), along(half, 2, chips)
    mine, own_mask, theirs = call(
        aggregate_kernel,
        (flags, flags_pair, adj, adj_pair, pair, one, two, three, far),
        [((rows, T), F32), ((groups, T), F32), ((rows + chips, T), F32)],
    )
    came = lax.ppermute(theirs, "c", swap)
    (z_self,) = call(self_kernel, (x_all, w_self), [((rows, T), F32)])
    output, gt, c_pay, mask = call(
        activation_kernel,
        (adj, inverse, mine, own_mask, came, z_self, out_grad),
        [((rows, T), BF16), ((T, rows), BF16), ((groups, T, T), BF16), ((groups, T), F32)],
    )
    c_all = lax.all_to_all(c_pay, ("z", "c"), 0, 0, tiled=True)
    bt, keep, send = call(
        weight_grad_kernel,
        (c_all, mask, gt, x_all),
        [((T, rows), BF16), ((chips, 2 * T, T), F32), ((chips, 2 * T, T), BF16)],
    )
    came = lax.ppermute(send, "c", swap)
    (p_pay,) = call(
        feature_grad_kernel,
        (gt, bt, w_self, w_neigh),
        [((parts, T, rows), BF16)],
        out_specs=[HBM],
        scratch=[pltpu.VMEM((parts, T, rows), BF16), pltpu.SemaphoreType.DMA((parts,))],
    )
    *w_pay, own, p_pay = call(
        pair_kernel,
        (keep, came, p_pay),
        [((2 * T, T), BF16)] * (chips - 1) + [((2 * T, T), F32), (p_pay.shape, BF16)],
        in_specs=[VMEM, VMEM, HBM],
        out_specs=[VMEM] * chips + [HBM],
        aliases={2: chips},
    )
    p_all = lax.all_to_all(p_pay, "f", 0, 0, tiled=True)
    w_came = [
        lax.ppermute(block, "z", [(chip, (chip + step) % chips) for chip in range(chips)])
        for step, block in zip(far_first(chips), w_pay)
    ]
    (grad_features,) = call(sum_kernel, (p_all,), [((rows, T), BF16)])
    grad_self, grad_neigh, grad_features = call(
        weight_sum_kernel,
        (own, grad_features, *w_came),
        [((T, T), F32), ((T, T), F32), ((rows, T), BF16)],
        in_specs=[VMEM, ANY] + [VMEM] * (chips - 1),
        out_specs=[VMEM, VMEM, ANY],
        aliases={1: 2},
    )
    return output, grad_features, grad_self, grad_neigh


def solution(mesh):
    row_count, part_count = mesh.shape["rows"], mesh.shape["feat"]
    split = Mesh(mesh.devices.reshape(row_count // 2, 2, part_count), ("z", "c", "f"))
    rows, feat = ("z", "c"), "f"
    return jax.shard_map(
        functools.partial(per_device, chips=row_count // 2, parts=part_count),
        mesh=split,
        in_specs=(
            P(rows, feat),
            P(None, feat),
            P(None, feat),
            P(rows, feat),
            P(rows),
            P(rows, None),
            P(rows, None),
            P(rows, None, None, None),
        ),
        out_specs=(P(rows, feat),) * 4,
        check_vma=False,
    )
```

```python
import functools

import jax
import jax.numpy as jnp
from jax import lax
from jax.experimental import pallas as pl
from jax.experimental.pallas import tpu as pltpu
from jax.sharding import Mesh, PartitionSpec as P

F32 = jnp.float32
BF16 = jnp.bfloat16
T = 128
CHUNK = 10
MIB = 1024 * 1024
VMEM = pl.BlockSpec(memory_space=pltpu.VMEM)
SMEM = pl.BlockSpec(memory_space=pltpu.SMEM)
ANY = pl.BlockSpec(memory_space=pl.ANY)
HBM = pl.BlockSpec(memory_space=pltpu.HBM)


def dot(a, b):
    return jnp.dot(a, b, preferred_element_type=F32)


def owners(here, core, chips):
    way = 1 - 2 * core

    def chip(step):
        return lax.rem(here + step + chips, chips)

    far = 2 * chip(chips // 2) + core
    three, two, one = (2 * chip(step * way) for step in (3, 2, 1))
    return [far, three, three + 1, two, two + 1, one, one + 1, 2 * here + core]


def sources(here, core, chips):
    way = 1 - 2 * core
    found = []
    for step in (1, 2, 3):
        chip = lax.rem(here - step * way + chips, chips)
        found += [2 * chip, 2 * chip + 1]
    return found + [2 * lax.rem(here + chips // 2, chips) + core]


def halves(block):
    high = block.astype(BF16)
    return jnp.concatenate([high, (block - high.astype(F32)).astype(BF16)], axis=0)


def spread_kernel(x_hbm, pay_ref, x_ref, in_sem, sems):
    copies = [
        pltpu.make_async_copy(x_ref, pay_ref.at[copy], sems.at[copy]) for copy in range(pay_ref.shape[0])
    ]
    came = pltpu.make_async_copy(x_hbm, x_ref, in_sem)
    came.start()
    came.wait()
    for copy in copies:
        copy.start()
    for copy in copies:
        copy.wait()


def adjacency_kernel(
    count_ref, dst_hbm, src_hbm, weight_ref, adj_ref, send_ref, inv_ref, flag_ref,
    dst_ref, src_ref, buf, acc, sel_ref, in_sems, sems,
):
    count = count_ref[0]
    slots = weight_ref.shape[0]
    groups = acc.shape[0]

    def chunk_copy(index):
        part = pl.ds(index * CHUNK, CHUNK)
        return pltpu.make_async_copy(weight_ref.at[part], buf.at[part], sems.at[index])

    ins = [
        pltpu.make_async_copy(source, target, in_sems.at[index])
        for index, (source, target) in enumerate(((dst_hbm, dst_ref), (src_hbm, src_ref)))
    ]
    for copy in ins:
        copy.start()
    for index in range(slots // CHUNK):

        @pl.when(index * CHUNK < count)
        def _():
            chunk_copy(index).start()

    acc[...] = jnp.zeros_like(acc)
    for owner in range(groups):
        sel_ref[owner] = 0
    for copy in ins:
        copy.wait()
    for index in range(slots // CHUNK):

        @pl.when(index * CHUNK < count)
        def _():
            chunk_copy(index).wait()

            def add_tile(slot, carry):
                source = src_ref[0, slot]
                owner = source // 2
                sel_ref[owner] = source - 2 * owner
                rows = pl.ds(pl.multiple_of(dst_ref[0, slot] * T, T), T)
                acc[owner, rows, :] = acc[owner, rows, :] + buf[slot]
                return carry

            lax.fori_loop(index * CHUNK, jnp.minimum(count, (index + 1) * CHUNK), add_tile, 0)

    total = acc[0]
    for owner in range(groups):
        if owner > 0:
            total = total + acc[owner]
        adj_ref[owner] = acc[owner].astype(F32).astype(BF16)
    for slot, owner in enumerate(sources(lax.axis_index("z"), 1 - lax.axis_index("c"), groups // 2)):
        send_ref[slot] = adj_ref[owner]
    degree = jnp.sum(total.astype(F32), axis=1, keepdims=True)
    inv_ref[...] = jnp.broadcast_to(1.0 / jnp.maximum(degree, 1.0), inv_ref.shape)
    row = lax.broadcasted_iota(jnp.int32, flag_ref.shape, 0)
    flags = jnp.zeros(flag_ref.shape, F32)
    for owner in range(groups):
        flags = jnp.where(row == owner, sel_ref[owner].astype(F32), flags)
    flag_ref[...] = flags


def wide_dot(x_ref, w_ref):
    total = None
    for part in range(0, x_ref.shape[0], 2):
        pair = jnp.concatenate([x_ref[part], x_ref[part + 1]], axis=1)
        product = dot(pair, w_ref[part * T : (part + 2) * T, :])
        total = product if total is None else total + product
    return total


def neighbour_kernel(x_ref, w_ref, flag_ref, pair_flag_ref, adj_ref, pay_ref, flag_same_ref, adj_same_ref):
    rows = x_ref.shape[1]
    product = wide_dot(x_ref, w_ref).astype(BF16)
    flags = flag_ref[...].astype(BF16)
    pay_ref[0:rows, :] = product
    pay_ref[rows:, :] = flags


def join_kernel(y_ref, y_pair_ref, pair_ref):
    core = lax.axis_index("c")
    pair_ref[core] = y_ref[...]
    pair_ref[1 - core] = y_pair_ref[...]


def half_kernel(pair_ref, half_ref):
    half_ref[...] = pair_ref[lax.axis_index("c")]


def self_kernel(x_ref, w_ref, z_ref):
    z_ref[...] = wide_dot(x_ref, w_ref)


def aggregate_kernel(
    flag_ref, flag_pair_ref, adj_ref, adj_pair_ref, pair_ref, one_ref, two_ref, three_ref, far_ref,
    mine_ref, mask_ref, theirs_ref,
):
    core = lax.axis_index("c")
    here = lax.axis_index("z")
    rows = mine_ref.shape[0]
    row = lax.broadcasted_iota(jnp.int32, (far_ref.shape[0] - rows, T), 0)
    blocks = [ref.at[side] for ref in (one_ref, two_ref, three_ref) for side in range(2)] + [far_ref]
    found = sources(here, core, flag_ref.shape[0] // 2)

    def summed(adj, flag, blocks, found):
        tiles = []
        for block, owner in zip(blocks, found):
            high = flag[pl.ds(owner, 1), :] > 0.5
            low_tile = block[0:T, :].astype(F32)
            high_tile = block[T : 2 * T, :].astype(F32)
            tiles.append(jnp.where(high, high_tile, low_tile).astype(BF16))
        return dot(jnp.concatenate(adj, axis=1), jnp.concatenate(tiles, axis=0))

    def mask_row(block, reader):
        return jnp.sum(jnp.where(row == reader, block[rows:, :].astype(F32), 0.0), axis=0, keepdims=True)

    adj_pair = [adj_pair_ref[slot] for slot in range(len(found))]
    theirs_ref[0:rows] = summed(adj_pair, flag_pair_ref, blocks, found)
    theirs_ref[rows:] = jnp.zeros((theirs_ref.shape[0] - rows, T), F32)
    for slot, block in enumerate(blocks):
        theirs_ref[rows + slot : rows + slot + 1, :] = mask_row(block, 2 * here + 1 - core)
    blocks = blocks + [pair_ref.at[0], pair_ref.at[1]]
    found = found + [2 * here, 2 * here + 1]
    mine_ref[...] = summed([adj_ref[owner] for owner in found], flag_ref, blocks, found)
    mask_ref[...] = jnp.zeros_like(mask_ref)
    for block, owner in zip(blocks, found):
        mask_ref[pl.ds(owner, 1), :] = mask_row(block, 2 * here + core)


def activation_kernel(
    adj_ref, inv_ref, mine_ref, own_mask_ref, came_ref, z_ref, og_ref, out_ref, gt_ref, pay_ref, mask_ref
):
    rows = z_ref.shape[0]
    mask_ref[...] = own_mask_ref[...]
    found = sources(lax.axis_index("z"), 1 - lax.axis_index("c"), mask_ref.shape[0] // 2)
    for slot, owner in enumerate(found):
        mask_ref[pl.ds(owner, 1), :] = came_ref[rows + slot : rows + slot + 1, :]
    inverse = inv_ref[...]
    z = z_ref[...] + inverse * (mine_ref[...] + came_ref[0:rows])
    sig = 1.0 / (1.0 + jnp.exp(-z))
    grad = (og_ref[...].astype(F32) * sig * (1.0 + z * (1.0 - sig))).astype(BF16).astype(F32)
    scaled = halves((grad * inverse).T)
    for owner in range(0, pay_ref.shape[0], 2):
        spread = dot(scaled, jnp.concatenate([adj_ref[owner], adj_ref[owner + 1]], axis=1))
        spread = (spread[0:T] + spread[T:]).astype(BF16)
        pay_ref[owner] = spread[:, 0:T]
        pay_ref[owner + 1] = spread[:, T:]
    out_ref[...] = (z * sig).astype(BF16)
    gt_ref[...] = grad.T.astype(BF16)


def weight_grad_kernel(came_ref, mask_ref, gt_ref, x_ref, bt_ref, keep_ref, send_ref):
    core = lax.axis_index("c")
    here = lax.axis_index("z")
    chips = keep_ref.shape[0]
    low = jnp.zeros((T, T), F32)
    high = jnp.zeros((T, T), F32)
    for sender in range(came_ref.shape[0]):
        came = came_ref[sender].astype(F32)
        is_high = mask_ref[sender : sender + 1, :] > 0.5
        low = low + jnp.where(is_high, 0.0, came)
        high = high + jnp.where(is_high, came, 0.0)
    both = halves(jnp.concatenate([low, high], axis=1))
    bt_ref[...] = both[0:T]
    left = jnp.concatenate([gt_ref[...], both], axis=0)
    slots = zip(owners(here, core, chips), owners(here, 1 - core, chips))
    for slot, (ours, theirs) in enumerate(slots):
        total = dot(left, jnp.concatenate([x_ref[ours], x_ref[theirs]], axis=1))
        kept, sent = total[:, 0:T], total[:, T:]
        keep_ref[slot, 0:T] = kept[0:T]
        keep_ref[slot, T:] = kept[T : 2 * T] + kept[2 * T :]
        send_ref[slot, 0:T] = sent[0:T].astype(BF16)
        send_ref[slot, T:] = (sent[T : 2 * T] + sent[2 * T :]).astype(BF16)


def feature_grad_kernel(gt_ref, bt_ref, ws_ref, wn_ref, pay_ref, buf, sems):
    right = jnp.concatenate([gt_ref[...], bt_ref[...]], axis=0)
    copies = []
    for part in range(pay_ref.shape[0]):
        span = slice(part * T, (part + 1) * T)
        left = jnp.concatenate([ws_ref[span, :], wn_ref[span, :]], axis=1)
        buf[part] = dot(left, right).astype(BF16)
        copies.append(pltpu.make_async_copy(buf.at[part], pay_ref.at[part], sems.at[part]))
        copies[-1].start()
    for copy in copies:
        copy.wait()


def pair_kernel(keep_ref, came_ref, payload_ref, far_ref, three_ref, one_ref, two_ref, own_ref, same_ref):
    def pair(slot):
        return keep_ref[slot] + came_ref[slot].astype(F32)

    far_ref[...] = pair(0).astype(BF16)
    for place in range(2):
        three_ref[place] = pair(1 + place).astype(BF16)
        two_ref[place] = pair(3 + place)
        one_ref[place] = pair(5 + place).astype(BF16)
    own_ref[...] = pair(7)


def relay_kernel(two_ref, three_ref, far_ref, out_ref):
    core = lax.axis_index("c")
    far = far_ref[...].astype(F32)
    out_ref[core] = (two_ref[core] + three_ref[core].astype(F32) + far).astype(BF16)
    out_ref[1 - core] = (two_ref[1 - core] + three_ref[1 - core].astype(F32)).astype(BF16)


def fold_kernel(own_ref, two_ref, one_ref, mine_ref, theirs_ref):
    core = lax.axis_index("c")
    theirs_ref[...] = two_ref[1 - core].astype(F32) + one_ref[1 - core].astype(F32)
    mine_ref[...] = own_ref[...] + two_ref[core].astype(F32) + one_ref[core].astype(F32)


def last_kernel(mine_ref, came_ref, done_ref, self_ref, neigh_ref, same_ref):
    total = mine_ref[...] + came_ref[...]
    self_ref[...] = total[0:T].T
    neigh_ref[...] = total[T:].T


def sum_kernel(parts_ref, out_ref):
    total = parts_ref[0].astype(F32)
    for part in range(1, parts_ref.shape[0]):
        total = total + parts_ref[part].astype(F32)
    out_ref[...] = total.T.astype(out_ref.dtype)


def call(kernel, ins, outs, in_specs=None, out_specs=None, scratch=(), limit=12, aliases=None):
    shapes = tuple(
        pltpu.HBM(shape, dtype) if spec is HBM else jax.ShapeDtypeStruct(shape, dtype)
        for (shape, dtype), spec in zip(outs, out_specs or [VMEM] * len(outs))
    )
    ins = [
        pltpu.with_memory_space_constraint(value, pltpu.HBM) if spec is HBM else value
        for value, spec in zip(ins, in_specs or [VMEM] * len(ins))
    ]
    return pl.pallas_call(
        kernel,
        out_shape=shapes,
        in_specs=in_specs or [VMEM] * len(ins),
        out_specs=tuple(out_specs or [VMEM] * len(outs)),
        scratch_shapes=list(scratch),
        input_output_aliases=aliases or {},
        compiler_params=pltpu.CompilerParams(vmem_limit_bytes=limit * MIB),
        name=kernel.__name__,
    )(*ins)


def along(value, step, chips):
    pairs = [(2 * chip, 2 * ((chip + step) % chips)) for chip in range(chips)]
    pairs += [(2 * chip + 1, 2 * ((chip - step) % chips) + 1) for chip in range(chips)]
    return lax.ppermute(value, ("z", "c"), pairs)


def per_device(features, w_self, w_neigh, out_grad, tile_count, tile_dst, tile_src, tile_weight, chips, parts):
    rows = features.shape[0]
    groups = 2 * chips
    slots = tile_weight.shape[1]
    swap = [(0, 1), (1, 0)]

    (x_pay,) = call(
        spread_kernel,
        (features,),
        [((parts, rows, T), BF16)],
        in_specs=[HBM],
        out_specs=[HBM],
        scratch=[pltpu.VMEM((rows, T), BF16), pltpu.SemaphoreType.DMA, pltpu.SemaphoreType.DMA((parts,))],
    )
    x_all = lax.all_to_all(x_pay, "f", 0, 0, tiled=True)
    adj, adj_send, inverse, flags = call(
        adjacency_kernel,
        (tile_count, tile_dst, tile_src, tile_weight[0]),
        [
            ((groups, rows, T), BF16),
            ((chips - 1, rows, T), BF16),
            ((rows, T), F32),
            ((groups, T), F32),
        ],
        in_specs=[SMEM, HBM, HBM, HBM],
        scratch=[
            pltpu.SMEM(tile_dst.shape, jnp.int32),
            pltpu.SMEM(tile_src.shape, jnp.int32),
            pltpu.VMEM((slots, T, T), jnp.int32),
            pltpu.VMEM((groups, rows, T), jnp.int32),
            pltpu.SMEM((groups,), jnp.int32),
            pltpu.SemaphoreType.DMA((2,)),
            pltpu.SemaphoreType.DMA((slots // CHUNK,)),
        ],
        limit=20,
    )
    adj_pair = lax.ppermute(adj_send, "c", swap)
    y, flags_pair, adj_pair = call(
        neighbour_kernel,
        (x_all, w_neigh, flags, lax.ppermute(flags, "c", swap), adj_pair),
        [((rows + groups, T), BF16), (flags.shape, F32), (adj_pair.shape, BF16)],
        in_specs=[VMEM] * 3 + [ANY, HBM],
        out_specs=[VMEM, ANY, HBM],
        aliases={3: 1, 4: 2},
    )
    (pair,) = call(join_kernel, (y, lax.ppermute(y, "c", swap)), [((2,) + y.shape, BF16)])
    two, one = along(pair, 2, chips), along(pair, 1, chips)
    (half,) = call(half_kernel, (two,), [(y.shape, BF16)])
    three, far = along(two, 1, chips), along(half, 2, chips)
    mine, own_mask, theirs = call(
        aggregate_kernel,
        (flags, flags_pair, adj, adj_pair, pair, one, two, three, far),
        [((rows, T), F32), ((groups, T), F32), ((rows + chips, T), F32)],
    )
    came = lax.ppermute(theirs, "c", swap)
    (z_self,) = call(self_kernel, (x_all, w_self), [((rows, T), F32)])
    output, gt, c_pay, mask = call(
        activation_kernel,
        (adj, inverse, mine, own_mask, came, z_self, out_grad),
        [((rows, T), BF16), ((T, rows), BF16), ((groups, T, T), BF16), ((groups, T), F32)],
    )
    c_all = lax.all_to_all(c_pay, ("z", "c"), 0, 0, tiled=True)
    bt, keep, send = call(
        weight_grad_kernel,
        (c_all, mask, gt, x_all),
        [((T, rows), BF16), ((chips, 2 * T, T), F32), ((chips, 2 * T, T), BF16)],
    )
    came = lax.ppermute(send, "c", swap)
    (p_pay,) = call(
        feature_grad_kernel,
        (gt, bt, w_self, w_neigh),
        [((parts, T, rows), BF16)],
        out_specs=[HBM],
        scratch=[pltpu.VMEM((parts, T, rows), BF16), pltpu.SemaphoreType.DMA((parts,))],
    )
    block = (2 * T, T)
    far, three, one, two, own, p_pay = call(
        pair_kernel,
        (keep, came, p_pay),
        [
            (block, BF16),
            ((2,) + block, BF16),
            ((2,) + block, BF16),
            ((2,) + block, F32),
            (block, F32),
            (p_pay.shape, BF16),
        ],
        in_specs=[VMEM, VMEM, HBM],
        out_specs=[VMEM] * 5 + [HBM],
        aliases={2: 5},
    )
    p_all = lax.all_to_all(p_pay, "f", 0, 0, tiled=True)
    (two,) = call(
        relay_kernel, (two, along(three, 1, chips), along(far, 2, chips)), [((2,) + block, BF16)]
    )
    two, one = along(two, 2, chips), along(one, 1, chips)
    mine, theirs = call(fold_kernel, (own, two, one), [(block, F32)] * 2)
    (grad_features,) = call(sum_kernel, (p_all,), [((rows, T), BF16)])
    grad_self, grad_neigh, grad_features = call(
        last_kernel,
        (mine, lax.ppermute(theirs, "c", swap), grad_features),
        [((T, T), F32), ((T, T), F32), ((rows, T), BF16)],
        in_specs=[VMEM] * 2 + [ANY],
        out_specs=[VMEM, VMEM, ANY],
        aliases={2: 2},
    )
    return output, grad_features, grad_self, grad_neigh


def solution(mesh):
    row_count, part_count = mesh.shape["rows"], mesh.shape["feat"]
    split = Mesh(mesh.devices.reshape(row_count // 2, 2, part_count), ("z", "c", "f"))
    rows, feat = ("z", "c"), "f"
    return jax.shard_map(
        functools.partial(per_device, chips=row_count // 2, parts=part_count),
        mesh=split,
        in_specs=(
            P(rows, feat),
            P(None, feat),
            P(None, feat),
            P(rows, feat),
            P(rows),
            P(rows, None),
            P(rows, None),
            P(rows, None, None, None),
        ),
        out_specs=(P(rows, feat),) * 4,
        check_vma=False,
    )
```

```python
import functools

import jax
import jax.numpy as jnp
from jax import lax
from jax.experimental import pallas as pl
from jax.experimental.pallas import tpu as pltpu
from jax.sharding import Mesh, PartitionSpec as P

F32 = jnp.float32
BF16 = jnp.bfloat16
T = 128
CHUNK = 10
MIB = 1024 * 1024
VMEM = pl.BlockSpec(memory_space=pltpu.VMEM)
SMEM = pl.BlockSpec(memory_space=pltpu.SMEM)
ANY = pl.BlockSpec(memory_space=pl.ANY)
HBM = pl.BlockSpec(memory_space=pltpu.HBM)


def dot(a, b):
    return jnp.dot(a, b, preferred_element_type=F32)


def owners(here, core, chips):
    way = 1 - 2 * core

    def chip(step):
        return lax.rem(here + step + chips, chips)

    far = 2 * chip(chips // 2) + core
    three, two, one = (2 * chip(step * way) for step in (3, 2, 1))
    return [far, three, three + 1, two, two + 1, one, one + 1, 2 * here + core]


def sources(here, core, chips):
    way = 1 - 2 * core
    found = []
    for step in (1, 2, 3):
        chip = lax.rem(here - step * way + chips, chips)
        found += [2 * chip, 2 * chip + 1]
    return found + [2 * lax.rem(here + chips // 2, chips) + core]


def halves(block):
    high = block.astype(BF16)
    return jnp.concatenate([high, (block - high.astype(F32)).astype(BF16)], axis=0)


def spread_kernel(x_hbm, pay_ref, x_ref, in_sem, sems):
    copies = [
        pltpu.make_async_copy(x_ref, pay_ref.at[copy], sems.at[copy]) for copy in range(pay_ref.shape[0])
    ]
    came = pltpu.make_async_copy(x_hbm, x_ref, in_sem)
    came.start()
    came.wait()
    for copy in copies:
        copy.start()
    for copy in copies:
        copy.wait()


def adjacency_kernel(
    count_ref, dst_hbm, src_hbm, weight_ref, adj_ref, send_ref, back_ref, inv_ref, flag_ref,
    dst_ref, src_ref, buf, acc, sel_ref, in_sems, sems,
):
    count = count_ref[0]
    slots = weight_ref.shape[0]
    groups = acc.shape[0]

    def chunk_copy(index):
        part = pl.ds(index * CHUNK, CHUNK)
        return pltpu.make_async_copy(weight_ref.at[part], buf.at[part], sems.at[index])

    ins = [
        pltpu.make_async_copy(source, target, in_sems.at[index])
        for index, (source, target) in enumerate(((dst_hbm, dst_ref), (src_hbm, src_ref)))
    ]
    for copy in ins:
        copy.start()
    for index in range(slots // CHUNK):

        @pl.when(index * CHUNK < count)
        def _():
            chunk_copy(index).start()

    acc[...] = jnp.zeros_like(acc)
    for owner in range(groups):
        sel_ref[owner] = 0
    for copy in ins:
        copy.wait()
    for index in range(slots // CHUNK):

        @pl.when(index * CHUNK < count)
        def _():
            chunk_copy(index).wait()

            def add_tile(slot, carry):
                source = src_ref[0, slot]
                owner = source // 2
                sel_ref[owner] = source - 2 * owner
                rows = pl.ds(pl.multiple_of(dst_ref[0, slot] * T, T), T)
                acc[owner, rows, :] = acc[owner, rows, :] + buf[slot]
                return carry

            lax.fori_loop(index * CHUNK, jnp.minimum(count, (index + 1) * CHUNK), add_tile, 0)

    total = acc[0]
    for owner in range(groups):
        if owner > 0:
            total = total + acc[owner]
        adj_ref[owner] = acc[owner].astype(F32).astype(BF16)
    for slot, owner in enumerate(sources(lax.axis_index("z"), 1 - lax.axis_index("c"), groups // 2)):
        send_ref[slot] = adj_ref[owner]
    for slot, owner in enumerate(owners(lax.axis_index("z"), 1 - lax.axis_index("c"), groups // 2)[1:]):
        back_ref[slot] = adj_ref[owner]
    degree = jnp.sum(total.astype(F32), axis=1, keepdims=True)
    inv_ref[...] = jnp.broadcast_to(1.0 / jnp.maximum(degree, 1.0), inv_ref.shape)
    row = lax.broadcasted_iota(jnp.int32, flag_ref.shape, 0)
    flags = jnp.zeros(flag_ref.shape, F32)
    for owner in range(groups):
        flags = jnp.where(row == owner, sel_ref[owner].astype(F32), flags)
    flag_ref[...] = flags


def wide_dot(x_ref, w_ref):
    total = None
    for part in range(0, x_ref.shape[0], 2):
        pair = jnp.concatenate([x_ref[part], x_ref[part + 1]], axis=1)
        product = dot(pair, w_ref[part * T : (part + 2) * T, :])
        total = product if total is None else total + product
    return total


def neighbour_kernel(x_ref, w_ref, pair_flag_ref, adj_ref, pay_ref, flag_same_ref, adj_same_ref):
    pay_ref[...] = wide_dot(x_ref, w_ref).astype(BF16)


def join_kernel(y_ref, y_pair_ref, pair_ref):
    core = lax.axis_index("c")
    pair_ref[core] = y_ref[...]
    pair_ref[1 - core] = y_pair_ref[...]


def half_kernel(pair_ref, half_ref):
    half_ref[...] = pair_ref[lax.axis_index("c")]


def self_kernel(x_ref, w_ref, z_ref):
    z_ref[...] = wide_dot(x_ref, w_ref)


def aggregate_kernel(
    flag_ref, flag_pair_ref, adj_ref, adj_pair_ref, pair_ref, one_ref, two_ref, three_ref, far_ref,
    mine_ref, theirs_ref,
):
    core = lax.axis_index("c")
    here = lax.axis_index("z")
    blocks = [ref.at[side] for ref in (one_ref, two_ref, three_ref) for side in range(2)] + [far_ref]
    found = sources(here, core, flag_ref.shape[0] // 2)

    def summed(adj, flag, blocks, found):
        tiles = []
        for block, owner in zip(blocks, found):
            high = flag[pl.ds(owner, 1), :] > 0.5
            low_tile = block[0:T, :].astype(F32)
            high_tile = block[T : 2 * T, :].astype(F32)
            tiles.append(jnp.where(high, high_tile, low_tile).astype(BF16))
        return dot(jnp.concatenate(adj, axis=1), jnp.concatenate(tiles, axis=0))

    adj_pair = [adj_pair_ref[slot] for slot in range(len(found))]
    theirs_ref[...] = summed(adj_pair, flag_pair_ref, blocks, found)
    blocks = blocks + [pair_ref.at[0], pair_ref.at[1]]
    found = found + [2 * here, 2 * here + 1]
    mine_ref[...] = summed([adj_ref[owner] for owner in found], flag_ref, blocks, found)


def activation_kernel(inv_ref, mine_ref, came_ref, z_ref, og_ref, out_ref, both_ref):
    inverse = inv_ref[...]
    z = z_ref[...] + inverse * (mine_ref[...] + came_ref[...])
    sig = 1.0 / (1.0 + jnp.exp(-z))
    grad = (og_ref[...].astype(F32) * sig * (1.0 + z * (1.0 - sig))).astype(BF16).astype(F32)
    both_ref[0:T, :] = grad.T.astype(BF16)
    both_ref[T:, :] = halves((grad * inverse).T)
    out_ref[...] = (z * sig).astype(BF16)


def transpose_kernel(
    flag_ref, flag_pair_ref, adj_ref, adj_pair_ref, adj_back_ref, both_ref, both_pair_ref,
    far_ref, three_ref, one_ref, two_ref, own_ref,
):
    found = owners(lax.axis_index("z"), lax.axis_index("c"), flag_ref.shape[0] // 2)
    adj_pair = [adj_pair_ref[len(found) - 2]] + [adj_back_ref[slot] for slot in range(len(found) - 1)]
    left = jnp.concatenate([both_ref[T:, :], both_pair_ref[T:, :]], axis=1)

    def block(slot):
        parts = []
        for adj, flag in ((adj_ref[found[slot]], flag_ref), (adj_pair[slot], flag_pair_ref)):
            high = flag[pl.ds(found[slot], 1), :]
            parts.append(jnp.concatenate([adj * (1.0 - high).astype(BF16), adj * high.astype(BF16)], axis=1))
        product = dot(left, jnp.concatenate(parts, axis=0))
        return product[0:T] + product[T:]

    far_ref[...] = block(0).astype(BF16)
    for place in range(2):
        three_ref[place] = block(1 + place).astype(BF16)
        two_ref[place] = block(3 + place)
        one_ref[place] = block(5 + place).astype(BF16)
    own_ref[...] = block(7)


def weight_grad_kernel(mine_ref, came_ref, both_ref, x_ref, bt_ref, keep_ref, send_ref):
    core = lax.axis_index("c")
    here = lax.axis_index("z")
    chips = keep_ref.shape[0]
    split = halves(mine_ref[...] + came_ref[...])
    bt_ref[...] = split[0:T]
    left = jnp.concatenate([both_ref[0:T, :], split], axis=0)
    slots = zip(owners(here, core, chips), owners(here, 1 - core, chips))
    for slot, (ours, theirs) in enumerate(slots):
        total = dot(left, jnp.concatenate([x_ref[ours], x_ref[theirs]], axis=1))
        kept, sent = total[:, 0:T], total[:, T:]
        keep_ref[slot, 0:T] = kept[0:T]
        keep_ref[slot, T:] = kept[T : 2 * T] + kept[2 * T :]
        send_ref[slot, 0:T] = sent[0:T].astype(BF16)
        send_ref[slot, T:] = (sent[T : 2 * T] + sent[2 * T :]).astype(BF16)


def feature_grad_kernel(both_ref, bt_ref, ws_ref, wn_ref, pay_ref, buf, sems):
    right = jnp.concatenate([both_ref[0:T, :], bt_ref[...]], axis=0)
    copies = []
    for part in range(pay_ref.shape[0]):
        span = slice(part * T, (part + 1) * T)
        left = jnp.concatenate([ws_ref[span, :], wn_ref[span, :]], axis=1)
        buf[part] = dot(left, right).astype(BF16)
        copies.append(pltpu.make_async_copy(buf.at[part], pay_ref.at[part], sems.at[part]))
        copies[-1].start()
    for copy in copies:
        copy.wait()


def pair_kernel(keep_ref, came_ref, payload_ref, far_ref, three_ref, one_ref, two_ref, own_ref, same_ref):
    def pair(slot):
        return keep_ref[slot] + came_ref[slot].astype(F32)

    far_ref[...] = pair(0).astype(BF16)
    for place in range(2):
        three_ref[place] = pair(1 + place).astype(BF16)
        two_ref[place] = pair(3 + place)
        one_ref[place] = pair(5 + place).astype(BF16)
    own_ref[...] = pair(7)


def relay_kernel(two_ref, three_ref, far_ref, out_ref):
    core = lax.axis_index("c")
    far = far_ref[...].astype(F32)
    out_ref[core] = (two_ref[core] + three_ref[core].astype(F32) + far).astype(BF16)
    out_ref[1 - core] = (two_ref[1 - core] + three_ref[1 - core].astype(F32)).astype(BF16)


def fold_kernel(own_ref, two_ref, one_ref, mine_ref, theirs_ref):
    core = lax.axis_index("c")
    theirs_ref[...] = two_ref[1 - core].astype(F32) + one_ref[1 - core].astype(F32)
    mine_ref[...] = own_ref[...] + two_ref[core].astype(F32) + one_ref[core].astype(F32)


def last_kernel(mine_ref, came_ref, done_ref, self_ref, neigh_ref, same_ref):
    total = mine_ref[...] + came_ref[...]
    self_ref[...] = total[0:T].T
    neigh_ref[...] = total[T:].T


def sum_kernel(parts_ref, out_ref):
    total = parts_ref[0].astype(F32)
    for part in range(1, parts_ref.shape[0]):
        total = total + parts_ref[part].astype(F32)
    out_ref[...] = total.T.astype(out_ref.dtype)


def call(kernel, ins, outs, in_specs=None, out_specs=None, scratch=(), limit=12, aliases=None):
    shapes = tuple(
        pltpu.HBM(shape, dtype) if spec is HBM else jax.ShapeDtypeStruct(shape, dtype)
        for (shape, dtype), spec in zip(outs, out_specs or [VMEM] * len(outs))
    )
    ins = [
        pltpu.with_memory_space_constraint(value, pltpu.HBM) if spec is HBM else value
        for value, spec in zip(ins, in_specs or [VMEM] * len(ins))
    ]
    return pl.pallas_call(
        kernel,
        out_shape=shapes,
        in_specs=in_specs or [VMEM] * len(ins),
        out_specs=tuple(out_specs or [VMEM] * len(outs)),
        scratch_shapes=list(scratch),
        input_output_aliases=aliases or {},
        compiler_params=pltpu.CompilerParams(vmem_limit_bytes=limit * MIB),
        name=kernel.__name__,
    )(*ins)


def along(value, step, chips):
    pairs = [(2 * chip, 2 * ((chip + step) % chips)) for chip in range(chips)]
    pairs += [(2 * chip + 1, 2 * ((chip - step) % chips) + 1) for chip in range(chips)]
    return lax.ppermute(value, ("z", "c"), pairs)


def per_device(features, w_self, w_neigh, out_grad, tile_count, tile_dst, tile_src, tile_weight, chips, parts):
    rows = features.shape[0]
    groups = 2 * chips
    slots = tile_weight.shape[1]
    swap = [(0, 1), (1, 0)]

    (x_pay,) = call(
        spread_kernel,
        (features,),
        [((parts, rows, T), BF16)],
        in_specs=[HBM],
        out_specs=[HBM],
        scratch=[pltpu.VMEM((rows, T), BF16), pltpu.SemaphoreType.DMA, pltpu.SemaphoreType.DMA((parts,))],
    )
    x_all = lax.all_to_all(x_pay, "f", 0, 0, tiled=True)
    adj, adj_send, adj_back, inverse, flags = call(
        adjacency_kernel,
        (tile_count, tile_dst, tile_src, tile_weight[0]),
        [
            ((groups, rows, T), BF16),
            ((chips - 1, rows, T), BF16),
            ((chips - 1, rows, T), BF16),
            ((rows, T), F32),
            ((groups, T), F32),
        ],
        in_specs=[SMEM, HBM, HBM, HBM],
        scratch=[
            pltpu.SMEM(tile_dst.shape, jnp.int32),
            pltpu.SMEM(tile_src.shape, jnp.int32),
            pltpu.VMEM((slots, T, T), jnp.int32),
            pltpu.VMEM((groups, rows, T), jnp.int32),
            pltpu.SMEM((groups,), jnp.int32),
            pltpu.SemaphoreType.DMA((2,)),
            pltpu.SemaphoreType.DMA((slots // CHUNK,)),
        ],
        limit=20,
    )
    adj_pair, adj_back = lax.ppermute(adj_send, "c", swap), lax.ppermute(adj_back, "c", swap)
    y, flags_pair, adj_pair = call(
        neighbour_kernel,
        (x_all, w_neigh, lax.ppermute(flags, "c", swap), adj_pair),
        [((rows, T), BF16), (flags.shape, F32), (adj_pair.shape, BF16)],
        in_specs=[VMEM] * 2 + [ANY, HBM],
        out_specs=[VMEM, ANY, HBM],
        aliases={2: 1, 3: 2},
    )
    (pair,) = call(join_kernel, (y, lax.ppermute(y, "c", swap)), [((2,) + y.shape, BF16)])
    two, one = along(pair, 2, chips), along(pair, 1, chips)
    (half,) = call(half_kernel, (two,), [(y.shape, BF16)])
    three, far = along(two, 1, chips), along(half, 2, chips)
    mine, theirs = call(
        aggregate_kernel,
        (flags, flags_pair, adj, adj_pair, pair, one, two, three, far),
        [((rows, T), F32)] * 2,
    )
    came = lax.ppermute(theirs, "c", swap)
    (z_self,) = call(self_kernel, (x_all, w_self), [((rows, T), F32)])
    output, both = call(
        activation_kernel,
        (inverse, mine, came, z_self, out_grad),
        [((rows, T), BF16), ((3 * T, rows), BF16)],
    )

    def sends(block):
        pair = (2,) + block
        return [(block, BF16), (pair, BF16), (pair, BF16), (pair, F32), (block, F32)]

    def reduce(far, three, one, two, own):
        block = own.shape
        (two,) = call(
            relay_kernel, (two, along(three, 1, chips), along(far, 2, chips)), [((2,) + block, BF16)]
        )
        two, one = along(two, 2, chips), along(one, 1, chips)
        mine, theirs = call(fold_kernel, (own, two, one), [(block, F32)] * 2)
        return mine, lax.ppermute(theirs, "c", swap)

    parts_sent = call(
        transpose_kernel,
        (flags, flags_pair, adj, adj_pair, adj_back, both, lax.ppermute(both, "c", swap)),
        sends((T, rows)),
    )
    mine, came = reduce(*parts_sent)
    bt, keep, send = call(
        weight_grad_kernel,
        (mine, came, both, x_all),
        [((T, rows), BF16), ((chips, 2 * T, T), F32), ((chips, 2 * T, T), BF16)],
    )
    came = lax.ppermute(send, "c", swap)
    (p_pay,) = call(
        feature_grad_kernel,
        (both, bt, w_self, w_neigh),
        [((parts, T, rows), BF16)],
        out_specs=[HBM],
        scratch=[pltpu.VMEM((parts, T, rows), BF16), pltpu.SemaphoreType.DMA((parts,))],
    )
    *parts_sent, p_pay = call(
        pair_kernel,
        (keep, came, p_pay),
        sends((2 * T, T)) + [(p_pay.shape, BF16)],
        in_specs=[VMEM, VMEM, HBM],
        out_specs=[VMEM] * 5 + [HBM],
        aliases={2: 5},
    )
    p_all = lax.all_to_all(p_pay, "f", 0, 0, tiled=True)
    mine, came = reduce(*parts_sent)
    (grad_features,) = call(sum_kernel, (p_all,), [((rows, T), BF16)])
    grad_self, grad_neigh, grad_features = call(
        last_kernel,
        (mine, came, grad_features),
        [((T, T), F32), ((T, T), F32), ((rows, T), BF16)],
        in_specs=[VMEM] * 2 + [ANY],
        out_specs=[VMEM, VMEM, ANY],
        aliases={2: 2},
    )
    return output, grad_features, grad_self, grad_neigh


def solution(mesh):
    row_count, part_count = mesh.shape["rows"], mesh.shape["feat"]
    split = Mesh(mesh.devices.reshape(row_count // 2, 2, part_count), ("z", "c", "f"))
    rows, feat = ("z", "c"), "f"
    return jax.shard_map(
        functools.partial(per_device, chips=row_count // 2, parts=part_count),
        mesh=split,
        in_specs=(
            P(rows, feat),
            P(None, feat),
            P(None, feat),
            P(rows, feat),
            P(rows),
            P(rows, None),
            P(rows, None),
            P(rows, None, None, None),
        ),
        out_specs=(P(rows, feat),) * 4,
        check_vma=False,
    )
```

```python
import functools

import jax
import jax.numpy as jnp
from jax import lax
from jax.experimental import pallas as pl
from jax.experimental.pallas import tpu as pltpu
from jax.sharding import Mesh, PartitionSpec as P

F32 = jnp.float32
BF16 = jnp.bfloat16
T = 128
CHUNK = 10
MIB = 1024 * 1024
VMEM = pl.BlockSpec(memory_space=pltpu.VMEM)
SMEM = pl.BlockSpec(memory_space=pltpu.SMEM)
ANY = pl.BlockSpec(memory_space=pl.ANY)
HBM = pl.BlockSpec(memory_space=pltpu.HBM)


def dot(a, b):
    return jnp.dot(a, b, preferred_element_type=F32)


def owners(here, core, chips):
    way = 1 - 2 * core

    def chip(step):
        return lax.rem(here + step + chips, chips)

    far = 2 * chip(chips // 2) + core
    three, two, one = (2 * chip(step * way) for step in (3, 2, 1))
    return [far, three, three + 1, two, two + 1, one, one + 1, 2 * here + core]


def sources(here, core, chips):
    way = 1 - 2 * core
    found = []
    for step in (1, 2, 3):
        chip = lax.rem(here - step * way + chips, chips)
        found += [2 * chip, 2 * chip + 1]
    return found + [2 * lax.rem(here + chips // 2, chips) + core]


def halves(block):
    high = block.astype(BF16)
    return jnp.concatenate([high, (block - high.astype(F32)).astype(BF16)], axis=0)


def spread_kernel(x_hbm, pay_ref, x_ref, in_sem, sems):
    copies = [
        pltpu.make_async_copy(x_ref, pay_ref.at[copy], sems.at[copy]) for copy in range(pay_ref.shape[0])
    ]
    came = pltpu.make_async_copy(x_hbm, x_ref, in_sem)
    came.start()
    came.wait()
    for copy in copies:
        copy.start()
    for copy in copies:
        copy.wait()


def adjacency_kernel(
    count_ref, dst_hbm, src_hbm, weight_ref, adj_ref, send_ref, back_ref, inv_ref, flag_ref,
    dst_ref, src_ref, buf, acc, sel_ref, send_buf, back_buf, in_sems, out_sems, sems,
):
    count = count_ref[0]
    slots = weight_ref.shape[0]
    groups = acc.shape[0]

    def chunk_copy(index):
        part = pl.ds(index * CHUNK, CHUNK)
        return pltpu.make_async_copy(weight_ref.at[part], buf.at[part], sems.at[index])

    ins = [
        pltpu.make_async_copy(source, target, in_sems.at[index])
        for index, (source, target) in enumerate(((dst_hbm, dst_ref), (src_hbm, src_ref)))
    ]
    for copy in ins:
        copy.start()
    for index in range(slots // CHUNK):

        @pl.when(index * CHUNK < count)
        def _():
            chunk_copy(index).start()

    acc[...] = jnp.zeros_like(acc)
    for owner in range(groups):
        sel_ref[owner] = 0
    for copy in ins:
        copy.wait()
    for index in range(slots // CHUNK):

        @pl.when(index * CHUNK < count)
        def _():
            chunk_copy(index).wait()

            def add_tile(slot, carry):
                source = src_ref[0, slot]
                owner = source // 2
                sel_ref[owner] = source - 2 * owner
                rows = pl.ds(pl.multiple_of(dst_ref[0, slot] * T, T), T)
                acc[owner, rows, :] = acc[owner, rows, :] + buf[slot]
                return carry

            lax.fori_loop(index * CHUNK, jnp.minimum(count, (index + 1) * CHUNK), add_tile, 0)

    total = acc[0]
    for owner in range(groups):
        if owner > 0:
            total = total + acc[owner]
        adj_ref[owner] = acc[owner].astype(F32).astype(BF16)
    for slot, owner in enumerate(sources(lax.axis_index("z"), 1 - lax.axis_index("c"), groups // 2)):
        send_buf[slot] = adj_ref[owner]
    for slot, owner in enumerate(owners(lax.axis_index("z"), 1 - lax.axis_index("c"), groups // 2)[1:]):
        back_buf[slot] = adj_ref[owner]
    outs = [
        pltpu.make_async_copy(send_buf, send_ref, out_sems.at[0]),
        pltpu.make_async_copy(back_buf, back_ref, out_sems.at[1]),
    ]
    for copy in outs:
        copy.start()
    degree = jnp.sum(total.astype(F32), axis=1, keepdims=True)
    inv_ref[...] = jnp.broadcast_to(1.0 / jnp.maximum(degree, 1.0), inv_ref.shape)
    row = lax.broadcasted_iota(jnp.int32, flag_ref.shape, 0)
    flags = jnp.zeros(flag_ref.shape, F32)
    for owner in range(groups):
        flags = jnp.where(row == owner, sel_ref[owner].astype(F32), flags)
    flag_ref[...] = flags
    for copy in outs:
        copy.wait()


def wide_dot(x_ref, w_ref):
    total = None
    for part in range(0, x_ref.shape[0], 2):
        pair = jnp.concatenate([x_ref[part], x_ref[part + 1]], axis=1)
        product = dot(pair, w_ref[part * T : (part + 2) * T, :])
        total = product if total is None else total + product
    return total


def neighbour_kernel(x_ref, w_ref, pair_flag_ref, adj_ref, pay_ref, flag_same_ref, adj_same_ref):
    pay_ref[...] = wide_dot(x_ref, w_ref).astype(BF16)


def join_kernel(y_ref, y_pair_ref, pair_ref):
    core = lax.axis_index("c")
    pair_ref[core] = y_ref[...]
    pair_ref[1 - core] = y_pair_ref[...]


def half_kernel(pair_ref, half_ref):
    half_ref[...] = pair_ref[lax.axis_index("c")]


def fetch_kernel(one_ref, pair_hbm, back_hbm, one_same_ref, pair_ref, back_ref, sems):
    copies = [
        pltpu.make_async_copy(pair_hbm, pair_ref, sems.at[0]),
        pltpu.make_async_copy(back_hbm, back_ref, sems.at[1]),
    ]
    for copy in copies:
        copy.start()
    for copy in copies:
        copy.wait()


def self_kernel(x_ref, w_ref, z_ref):
    z_ref[...] = wide_dot(x_ref, w_ref)


def aggregate_kernel(
    flag_ref, flag_pair_ref, adj_ref, adj_pair_ref, pair_ref, one_ref, two_ref, three_ref, far_ref,
    mine_ref, theirs_ref,
):
    core = lax.axis_index("c")
    here = lax.axis_index("z")
    blocks = [ref.at[side] for ref in (one_ref, two_ref, three_ref) for side in range(2)] + [far_ref]
    found = sources(here, core, flag_ref.shape[0] // 2)

    def summed(adj, flag, blocks, found):
        tiles = []
        for block, owner in zip(blocks, found):
            high = flag[pl.ds(owner, 1), :] > 0.5
            low_tile = block[0:T, :].astype(F32)
            high_tile = block[T : 2 * T, :].astype(F32)
            tiles.append(jnp.where(high, high_tile, low_tile).astype(BF16))
        return dot(jnp.concatenate(adj, axis=1), jnp.concatenate(tiles, axis=0))

    adj_pair = [adj_pair_ref[slot] for slot in range(len(found))]
    theirs_ref[...] = summed(adj_pair, flag_pair_ref, blocks, found)
    blocks = blocks + [pair_ref.at[0], pair_ref.at[1]]
    found = found + [2 * here, 2 * here + 1]
    mine_ref[...] = summed([adj_ref[owner] for owner in found], flag_ref, blocks, found)


def activation_kernel(inv_ref, mine_ref, came_ref, z_ref, og_ref, out_ref, both_ref):
    inverse = inv_ref[...]
    z = z_ref[...] + inverse * (mine_ref[...] + came_ref[...])
    sig = 1.0 / (1.0 + jnp.exp(-z))
    grad = (og_ref[...].astype(F32) * sig * (1.0 + z * (1.0 - sig))).astype(BF16).astype(F32)
    both_ref[0:T, :] = grad.T.astype(BF16)
    both_ref[T:, :] = halves((grad * inverse).T)
    out_ref[...] = (z * sig).astype(BF16)


def transpose_kernel(
    flag_ref, flag_pair_ref, adj_ref, adj_pair_ref, adj_back_ref, both_ref, both_pair_ref,
    far_ref, three_ref, one_ref, two_ref, own_ref,
):
    found = owners(lax.axis_index("z"), lax.axis_index("c"), flag_ref.shape[0] // 2)
    adj_pair = [adj_pair_ref[len(found) - 2]] + [adj_back_ref[slot] for slot in range(len(found) - 1)]
    left = jnp.concatenate([both_ref[T:, :], both_pair_ref[T:, :]], axis=1)

    def block(slot):
        parts = []
        for adj, flag in ((adj_ref[found[slot]], flag_ref), (adj_pair[slot], flag_pair_ref)):
            high = flag[pl.ds(found[slot], 1), :]
            parts.append(jnp.concatenate([adj * (1.0 - high).astype(BF16), adj * high.astype(BF16)], axis=1))
        product = dot(left, jnp.concatenate(parts, axis=0))
        return product[0:T] + product[T:]

    far_ref[...] = block(0).astype(BF16)
    for place in range(2):
        three_ref[place] = block(1 + place).astype(BF16)
        two_ref[place] = block(3 + place)
        one_ref[place] = block(5 + place).astype(BF16)
    own_ref[...] = block(7)


def weight_grad_kernel(mine_ref, came_ref, both_ref, x_ref, bt_ref, keep_ref, send_ref):
    core = lax.axis_index("c")
    here = lax.axis_index("z")
    chips = keep_ref.shape[0]
    split = halves(mine_ref[...] + came_ref[...])
    bt_ref[...] = split[0:T]
    left = jnp.concatenate([both_ref[0:T, :], split], axis=0)
    slots = zip(owners(here, core, chips), owners(here, 1 - core, chips))
    for slot, (ours, theirs) in enumerate(slots):
        total = dot(left, jnp.concatenate([x_ref[ours], x_ref[theirs]], axis=1))
        kept, sent = total[:, 0:T], total[:, T:]
        keep_ref[slot, 0:T] = kept[0:T]
        keep_ref[slot, T:] = kept[T : 2 * T] + kept[2 * T :]
        send_ref[slot, 0:T] = sent[0:T].astype(BF16)
        send_ref[slot, T:] = (sent[T : 2 * T] + sent[2 * T :]).astype(BF16)


def feature_grad_kernel(both_ref, bt_ref, ws_ref, wn_ref, pay_ref, buf, sems):
    right = jnp.concatenate([both_ref[0:T, :], bt_ref[...]], axis=0)
    copies = []
    for part in range(pay_ref.shape[0]):
        span = slice(part * T, (part + 1) * T)
        left = jnp.concatenate([ws_ref[span, :], wn_ref[span, :]], axis=1)
        buf[part] = dot(left, right).astype(BF16)
        copies.append(pltpu.make_async_copy(buf.at[part], pay_ref.at[part], sems.at[part]))
        copies[-1].start()
    for copy in copies:
        copy.wait()


def pair_kernel(keep_ref, came_ref, payload_ref, far_ref, three_ref, one_ref, two_ref, own_ref, same_ref):
    def pair(slot):
        return keep_ref[slot] + came_ref[slot].astype(F32)

    far_ref[...] = pair(0).astype(BF16)
    for place in range(2):
        three_ref[place] = pair(1 + place).astype(BF16)
        two_ref[place] = pair(3 + place)
        one_ref[place] = pair(5 + place).astype(BF16)
    own_ref[...] = pair(7)


def relay_kernel(two_ref, three_ref, far_ref, out_ref):
    core = lax.axis_index("c")
    far = far_ref[...].astype(F32)
    out_ref[core] = (two_ref[core] + three_ref[core].astype(F32) + far).astype(BF16)
    out_ref[1 - core] = (two_ref[1 - core] + three_ref[1 - core].astype(F32)).astype(BF16)


def fold_kernel(own_ref, two_ref, one_ref, mine_ref, theirs_ref):
    core = lax.axis_index("c")
    theirs_ref[...] = two_ref[1 - core].astype(F32) + one_ref[1 - core].astype(F32)
    mine_ref[...] = own_ref[...] + two_ref[core].astype(F32) + one_ref[core].astype(F32)


def last_kernel(mine_ref, came_ref, done_ref, self_ref, neigh_ref, same_ref):
    total = mine_ref[...] + came_ref[...]
    self_ref[...] = total[0:T].T
    neigh_ref[...] = total[T:].T


def sum_kernel(parts_ref, out_ref):
    total = parts_ref[0].astype(F32)
    for part in range(1, parts_ref.shape[0]):
        total = total + parts_ref[part].astype(F32)
    out_ref[...] = total.T.astype(out_ref.dtype)


def call(kernel, ins, outs, in_specs=None, out_specs=None, scratch=(), limit=12, aliases=None):
    shapes = tuple(
        pltpu.HBM(shape, dtype) if spec is HBM else jax.ShapeDtypeStruct(shape, dtype)
        for (shape, dtype), spec in zip(outs, out_specs or [VMEM] * len(outs))
    )
    ins = [
        pltpu.with_memory_space_constraint(value, pltpu.HBM) if spec is HBM else value
        for value, spec in zip(ins, in_specs or [VMEM] * len(ins))
    ]
    return pl.pallas_call(
        kernel,
        out_shape=shapes,
        in_specs=in_specs or [VMEM] * len(ins),
        out_specs=tuple(out_specs or [VMEM] * len(outs)),
        scratch_shapes=list(scratch),
        input_output_aliases=aliases or {},
        compiler_params=pltpu.CompilerParams(vmem_limit_bytes=limit * MIB),
        name=kernel.__name__,
    )(*ins)


def along(value, step, chips):
    pairs = [(2 * chip, 2 * ((chip + step) % chips)) for chip in range(chips)]
    pairs += [(2 * chip + 1, 2 * ((chip - step) % chips) + 1) for chip in range(chips)]
    return lax.ppermute(value, ("z", "c"), pairs)


def per_device(features, w_self, w_neigh, out_grad, tile_count, tile_dst, tile_src, tile_weight, chips, parts):
    rows = features.shape[0]
    groups = 2 * chips
    slots = tile_weight.shape[1]
    swap = [(0, 1), (1, 0)]

    (x_pay,) = call(
        spread_kernel,
        (features,),
        [((parts, rows, T), BF16)],
        in_specs=[HBM],
        out_specs=[HBM],
        scratch=[pltpu.VMEM((rows, T), BF16), pltpu.SemaphoreType.DMA, pltpu.SemaphoreType.DMA((parts,))],
    )
    x_all = lax.all_to_all(x_pay, "f", 0, 0, tiled=True)
    adj, adj_send, adj_back, inverse, flags = call(
        adjacency_kernel,
        (tile_count, tile_dst, tile_src, tile_weight[0]),
        [
            ((groups, rows, T), BF16),
            ((chips - 1, rows, T), BF16),
            ((chips - 1, rows, T), BF16),
            ((rows, T), F32),
            ((groups, T), F32),
        ],
        in_specs=[SMEM, HBM, HBM, HBM],
        out_specs=[VMEM, HBM, HBM, VMEM, VMEM],
        scratch=[
            pltpu.SMEM(tile_dst.shape, jnp.int32),
            pltpu.SMEM(tile_src.shape, jnp.int32),
            pltpu.VMEM((slots, T, T), jnp.int32),
            pltpu.VMEM((groups, rows, T), jnp.int32),
            pltpu.SMEM((groups,), jnp.int32),
            pltpu.VMEM((chips - 1, rows, T), BF16),
            pltpu.VMEM((chips - 1, rows, T), BF16),
            pltpu.SemaphoreType.DMA((2,)),
            pltpu.SemaphoreType.DMA((2,)),
            pltpu.SemaphoreType.DMA((slots // CHUNK,)),
        ],
        limit=20,
    )
    adj_pair, adj_back = lax.ppermute(adj_send, "c", swap), lax.ppermute(adj_back, "c", swap)
    y, flags_pair, adj_pair = call(
        neighbour_kernel,
        (x_all, w_neigh, lax.ppermute(flags, "c", swap), adj_pair),
        [((rows, T), BF16), (flags.shape, F32), (adj_pair.shape, BF16)],
        in_specs=[VMEM] * 2 + [ANY, HBM],
        out_specs=[VMEM, ANY, HBM],
        aliases={2: 1, 3: 2},
    )
    (pair,) = call(join_kernel, (y, lax.ppermute(y, "c", swap)), [((2,) + y.shape, BF16)])
    two, one = along(pair, 2, chips), along(pair, 1, chips)
    (half,) = call(half_kernel, (two,), [(y.shape, BF16)])
    three, far = along(two, 1, chips), along(half, 2, chips)
    one, adj_pair, adj_back = call(
        fetch_kernel,
        (one, adj_pair, adj_back),
        [(one.shape, BF16), (adj_pair.shape, BF16), (adj_back.shape, BF16)],
        in_specs=[ANY, HBM, HBM],
        out_specs=[ANY, VMEM, VMEM],
        scratch=[pltpu.SemaphoreType.DMA((2,))],
        aliases={0: 0},
    )
    mine, theirs = call(
        aggregate_kernel,
        (flags, flags_pair, adj, adj_pair, pair, one, two, three, far),
        [((rows, T), F32)] * 2,
    )
    came = lax.ppermute(theirs, "c", swap)
    (z_self,) = call(self_kernel, (x_all, w_self), [((rows, T), F32)])
    output, both = call(
        activation_kernel,
        (inverse, mine, came, z_self, out_grad),
        [((rows, T), BF16), ((3 * T, rows), BF16)],
    )

    def sends(block):
        pair = (2,) + block
        return [(block, BF16), (pair, BF16), (pair, BF16), (pair, F32), (block, F32)]

    def reduce(far, three, one, two, own):
        block = own.shape
        (two,) = call(
            relay_kernel, (two, along(three, 1, chips), along(far, 2, chips)), [((2,) + block, BF16)]
        )
        two, one = along(two, 2, chips), along(one, 1, chips)
        mine, theirs = call(fold_kernel, (own, two, one), [(block, F32)] * 2)
        return mine, lax.ppermute(theirs, "c", swap)

    parts_sent = call(
        transpose_kernel,
        (flags, flags_pair, adj, adj_pair, adj_back, both, lax.ppermute(both, "c", swap)),
        sends((T, rows)),
    )
    mine, came = reduce(*parts_sent)
    bt, keep, send = call(
        weight_grad_kernel,
        (mine, came, both, x_all),
        [((T, rows), BF16), ((chips, 2 * T, T), F32), ((chips, 2 * T, T), BF16)],
    )
    came = lax.ppermute(send, "c", swap)
    (p_pay,) = call(
        feature_grad_kernel,
        (both, bt, w_self, w_neigh),
        [((parts, T, rows), BF16)],
        out_specs=[HBM],
        scratch=[pltpu.VMEM((parts, T, rows), BF16), pltpu.SemaphoreType.DMA((parts,))],
    )
    *parts_sent, p_pay = call(
        pair_kernel,
        (keep, came, p_pay),
        sends((2 * T, T)) + [(p_pay.shape, BF16)],
        in_specs=[VMEM, VMEM, HBM],
        out_specs=[VMEM] * 5 + [HBM],
        aliases={2: 5},
    )
    p_all = lax.all_to_all(p_pay, "f", 0, 0, tiled=True)
    mine, came = reduce(*parts_sent)
    (grad_features,) = call(sum_kernel, (p_all,), [((rows, T), BF16)])
    grad_self, grad_neigh, grad_features = call(
        last_kernel,
        (mine, came, grad_features),
        [((T, T), F32), ((T, T), F32), ((rows, T), BF16)],
        in_specs=[VMEM] * 2 + [ANY],
        out_specs=[VMEM, VMEM, ANY],
        aliases={2: 2},
    )
    return output, grad_features, grad_self, grad_neigh


def solution(mesh):
    row_count, part_count = mesh.shape["rows"], mesh.shape["feat"]
    split = Mesh(mesh.devices.reshape(row_count // 2, 2, part_count), ("z", "c", "f"))
    rows, feat = ("z", "c"), "f"
    return jax.shard_map(
        functools.partial(per_device, chips=row_count // 2, parts=part_count),
        mesh=split,
        in_specs=(
            P(rows, feat),
            P(None, feat),
            P(None, feat),
            P(rows, feat),
            P(rows),
            P(rows, None),
            P(rows, None),
            P(rows, None, None, None),
        ),
        out_specs=(P(rows, feat),) * 4,
        check_vma=False,
    )
```

```python
import functools

import jax
import jax.numpy as jnp
from jax import lax
from jax.experimental import pallas as pl
from jax.experimental.pallas import tpu as pltpu
from jax.sharding import Mesh, PartitionSpec as P

F32 = jnp.float32
BF16 = jnp.bfloat16
T = 128
CHUNK = 10
MIB = 1024 * 1024
VMEM = pl.BlockSpec(memory_space=pltpu.VMEM)
SMEM = pl.BlockSpec(memory_space=pltpu.SMEM)
ANY = pl.BlockSpec(memory_space=pl.ANY)
HBM = pl.BlockSpec(memory_space=pltpu.HBM)


def dot(a, b):
    return jnp.dot(a, b, preferred_element_type=F32)


def owners(here, core, chips):
    way = 1 - 2 * core

    def chip(step):
        return lax.rem(here + step + chips, chips)

    far = 2 * chip(chips // 2) + core
    three, two, one = (2 * chip(step * way) for step in (3, 2, 1))
    return [far, three, three + 1, two, two + 1, one, one + 1, 2 * here + core]


def sources(here, core, chips):
    way = 1 - 2 * core
    found = []
    for step in (1, 2, 3):
        chip = lax.rem(here - step * way + chips, chips)
        found += [2 * chip, 2 * chip + 1]
    return found + [2 * lax.rem(here + chips // 2, chips) + core]


def halves(block):
    high = block.astype(BF16)
    return jnp.concatenate([high, (block - high.astype(F32)).astype(BF16)], axis=0)


def spread_kernel(x_hbm, pay_ref, x_ref, in_sem, sems):
    copies = [
        pltpu.make_async_copy(x_ref, pay_ref.at[copy], sems.at[copy]) for copy in range(pay_ref.shape[0])
    ]
    came = pltpu.make_async_copy(x_hbm, x_ref, in_sem)
    came.start()
    came.wait()
    for copy in copies:
        copy.start()
    for copy in copies:
        copy.wait()


def adjacency_kernel(
    count_ref, dst_hbm, src_hbm, weight_ref, adj_ref, send_ref, back_ref, inv_ref, flag_ref,
    dst_ref, src_ref, buf, acc, sel_ref, send_buf, back_buf, in_sems, out_sems, sems,
):
    count = count_ref[0]
    slots = weight_ref.shape[0]
    groups = acc.shape[0]

    def chunk_copy(index):
        part = pl.ds(index * CHUNK, CHUNK)
        return pltpu.make_async_copy(weight_ref.at[part], buf.at[part], sems.at[index])

    ins = [
        pltpu.make_async_copy(source, target, in_sems.at[index])
        for index, (source, target) in enumerate(((dst_hbm, dst_ref), (src_hbm, src_ref)))
    ]
    for copy in ins:
        copy.start()
    for index in range(slots // CHUNK):

        @pl.when(index * CHUNK < count)
        def _():
            chunk_copy(index).start()

    acc[...] = jnp.zeros_like(acc)
    for owner in range(groups):
        sel_ref[owner] = 0
    for copy in ins:
        copy.wait()
    for index in range(slots // CHUNK):

        @pl.when(index * CHUNK < count)
        def _():
            chunk_copy(index).wait()

            def add_tile(slot, carry):
                source = src_ref[0, slot]
                owner = source // 2
                sel_ref[owner] = source - 2 * owner
                rows = pl.ds(pl.multiple_of(dst_ref[0, slot] * T, T), T)
                acc[owner, rows, :] = acc[owner, rows, :] + buf[slot]
                return carry

            lax.fori_loop(index * CHUNK, jnp.minimum(count, (index + 1) * CHUNK), add_tile, 0)

    total = acc[0]
    for owner in range(groups):
        if owner > 0:
            total = total + acc[owner]
        adj_ref[owner] = acc[owner].astype(F32).astype(BF16)
    for slot, owner in enumerate(sources(lax.axis_index("z"), 1 - lax.axis_index("c"), groups // 2)):
        send_buf[slot] = adj_ref[owner]
    for slot, owner in enumerate(owners(lax.axis_index("z"), 1 - lax.axis_index("c"), groups // 2)[1:]):
        back_buf[slot] = adj_ref[owner]
    outs = [
        pltpu.make_async_copy(send_buf, send_ref, out_sems.at[0]),
        pltpu.make_async_copy(back_buf, back_ref, out_sems.at[1]),
    ]
    for copy in outs:
        copy.start()
    degree = jnp.sum(total.astype(F32), axis=1, keepdims=True)
    inv_ref[...] = jnp.broadcast_to(1.0 / jnp.maximum(degree, 1.0), inv_ref.shape)
    row = lax.broadcasted_iota(jnp.int32, flag_ref.shape, 0)
    flags = jnp.zeros(flag_ref.shape, F32)
    for owner in range(groups):
        flags = jnp.where(row == owner, sel_ref[owner].astype(F32), flags)
    flag_ref[...] = flags
    for copy in outs:
        copy.wait()


def wide_dot(x_ref, w_ref):
    total = None
    for part in range(0, x_ref.shape[0], 2):
        pair = jnp.concatenate([x_ref[part], x_ref[part + 1]], axis=1)
        product = dot(pair, w_ref[part * T : (part + 2) * T, :])
        total = product if total is None else total + product
    return total


def neighbour_kernel(x_ref, w_ref, pair_flag_ref, adj_ref, pay_ref, flag_same_ref, adj_same_ref):
    pay_ref[...] = wide_dot(x_ref, w_ref).astype(BF16)


def join_kernel(y_ref, y_pair_ref, pair_ref):
    core = lax.axis_index("c")
    pair_ref[core] = y_ref[...]
    pair_ref[1 - core] = y_pair_ref[...]


def half_kernel(pair_ref, half_ref):
    half_ref[...] = pair_ref[lax.axis_index("c")]


def fetch_kernel(one_ref, pair_hbm, back_hbm, one_same_ref, pair_ref, back_ref, sems):
    copies = [
        pltpu.make_async_copy(pair_hbm, pair_ref, sems.at[0]),
        pltpu.make_async_copy(back_hbm, back_ref, sems.at[1]),
    ]
    for copy in copies:
        copy.start()
    for copy in copies:
        copy.wait()


def self_kernel(x_ref, w_ref, z_ref):
    z_ref[...] = wide_dot(x_ref, w_ref)


def aggregate_kernel(
    flag_ref, flag_pair_ref, adj_ref, adj_pair_ref, pair_ref, one_ref, two_ref, three_ref, far_ref,
    mine_ref, theirs_ref,
):
    core = lax.axis_index("c")
    here = lax.axis_index("z")
    blocks = [ref.at[side] for ref in (one_ref, two_ref, three_ref) for side in range(2)] + [far_ref]
    found = sources(here, core, flag_ref.shape[0] // 2)

    def summed(adj, flag, blocks, found):
        tiles = []
        for block, owner in zip(blocks, found):
            high = flag[pl.ds(owner, 1), :] > 0.5
            low_tile = block[0:T, :].astype(F32)
            high_tile = block[T : 2 * T, :].astype(F32)
            tiles.append(jnp.where(high, high_tile, low_tile).astype(BF16))
        return dot(jnp.concatenate(adj, axis=1), jnp.concatenate(tiles, axis=0))

    adj_pair = [adj_pair_ref[slot] for slot in range(len(found))]
    theirs_ref[...] = summed(adj_pair, flag_pair_ref, blocks, found)
    blocks = blocks + [pair_ref.at[0], pair_ref.at[1]]
    found = found + [2 * here, 2 * here + 1]
    mine_ref[...] = summed([adj_ref[owner] for owner in found], flag_ref, blocks, found)


def activation_kernel(inv_ref, mine_ref, came_ref, z_ref, og_ref, out_ref, gt_ref, scaled_ref):
    inverse = inv_ref[...]
    z = z_ref[...] + inverse * (mine_ref[...] + came_ref[...])
    sig = 1.0 / (1.0 + jnp.exp(-z))
    grad = (og_ref[...].astype(F32) * sig * (1.0 + z * (1.0 - sig))).astype(BF16).astype(F32)
    scaled_ref[...] = halves((grad * inverse).T)
    gt_ref[...] = grad.T.astype(BF16)
    out_ref[...] = (z * sig).astype(BF16)


def transpose_kernel(
    flag_ref, flag_pair_ref, adj_ref, adj_pair_ref, adj_back_ref, scaled_ref, scaled_pair_ref,
    far_ref, three_ref, one_ref, two_ref, own_ref,
):
    found = owners(lax.axis_index("z"), lax.axis_index("c"), flag_ref.shape[0] // 2)
    adj_pair = [adj_pair_ref[len(found) - 2]] + [adj_back_ref[slot] for slot in range(len(found) - 1)]
    left = jnp.concatenate([scaled_ref[...], scaled_pair_ref[...]], axis=1)

    def block(slot):
        parts = []
        for adj, flag in ((adj_ref[found[slot]], flag_ref), (adj_pair[slot], flag_pair_ref)):
            high = flag[pl.ds(found[slot], 1), :]
            parts.append(jnp.concatenate([adj * (1.0 - high).astype(BF16), adj * high.astype(BF16)], axis=1))
        product = dot(left, jnp.concatenate(parts, axis=0))
        return product[0:T] + product[T:]

    far_ref[...] = block(0).astype(BF16)
    for place in range(2):
        three_ref[place] = block(1 + place).astype(BF16)
        two_ref[place] = block(3 + place)
        one_ref[place] = block(5 + place).astype(BF16)
    own_ref[...] = block(7)


def weight_grad_kernel(mine_ref, came_ref, gt_ref, x_ref, bt_ref, keep_ref, send_ref):
    core = lax.axis_index("c")
    here = lax.axis_index("z")
    chips = keep_ref.shape[0]
    split = halves(mine_ref[...] + came_ref[...])
    bt_ref[...] = split[0:T]
    left = jnp.concatenate([gt_ref[...], split], axis=0)
    slots = zip(owners(here, core, chips), owners(here, 1 - core, chips))
    for slot, (ours, theirs) in enumerate(slots):
        total = dot(left, jnp.concatenate([x_ref[ours], x_ref[theirs]], axis=1))
        kept, sent = total[:, 0:T], total[:, T:]
        keep_ref[slot, 0:T] = kept[0:T]
        keep_ref[slot, T:] = kept[T : 2 * T] + kept[2 * T :]
        send_ref[slot, 0:T] = sent[0:T].astype(BF16)
        send_ref[slot, T:] = (sent[T : 2 * T] + sent[2 * T :]).astype(BF16)


def feature_grad_kernel(gt_ref, bt_ref, ws_ref, wn_ref, pay_ref, buf, sems):
    right = jnp.concatenate([gt_ref[...], bt_ref[...]], axis=0)
    copies = []
    for part in range(pay_ref.shape[0]):
        span = slice(part * T, (part + 1) * T)
        left = jnp.concatenate([ws_ref[span, :], wn_ref[span, :]], axis=1)
        buf[part] = dot(left, right).astype(BF16)
        copies.append(pltpu.make_async_copy(buf.at[part], pay_ref.at[part], sems.at[part]))
        copies[-1].start()
    for copy in copies:
        copy.wait()


def pair_kernel(keep_ref, came_ref, payload_ref, far_ref, three_ref, one_ref, two_ref, own_ref, same_ref):
    def pair(slot):
        return keep_ref[slot] + came_ref[slot].astype(F32)

    far_ref[...] = pair(0).astype(BF16)
    for place in range(2):
        three_ref[place] = pair(1 + place).astype(BF16)
        two_ref[place] = pair(3 + place)
        one_ref[place] = pair(5 + place).astype(BF16)
    own_ref[...] = pair(7)


def relay_kernel(two_ref, three_ref, far_ref, out_ref):
    core = lax.axis_index("c")
    far = far_ref[...].astype(F32)
    out_ref[core] = (two_ref[core] + three_ref[core].astype(F32) + far).astype(BF16)
    out_ref[1 - core] = (two_ref[1 - core] + three_ref[1 - core].astype(F32)).astype(BF16)


def fold_kernel(own_ref, two_ref, one_ref, mine_ref, theirs_ref):
    core = lax.axis_index("c")
    theirs_ref[...] = two_ref[1 - core].astype(F32) + one_ref[1 - core].astype(F32)
    mine_ref[...] = own_ref[...] + two_ref[core].astype(F32) + one_ref[core].astype(F32)


def last_kernel(mine_ref, came_ref, done_ref, self_ref, neigh_ref, same_ref):
    total = mine_ref[...] + came_ref[...]
    self_ref[...] = total[0:T].T
    neigh_ref[...] = total[T:].T


def sum_kernel(parts_ref, out_ref):
    total = parts_ref[0].astype(F32)
    for part in range(1, parts_ref.shape[0]):
        total = total + parts_ref[part].astype(F32)
    out_ref[...] = total.T.astype(out_ref.dtype)


def call(kernel, ins, outs, in_specs=None, out_specs=None, scratch=(), limit=12, aliases=None):
    shapes = tuple(
        pltpu.HBM(shape, dtype) if spec is HBM else jax.ShapeDtypeStruct(shape, dtype)
        for (shape, dtype), spec in zip(outs, out_specs or [VMEM] * len(outs))
    )
    ins = [
        pltpu.with_memory_space_constraint(value, pltpu.HBM) if spec is HBM else value
        for value, spec in zip(ins, in_specs or [VMEM] * len(ins))
    ]
    return pl.pallas_call(
        kernel,
        out_shape=shapes,
        in_specs=in_specs or [VMEM] * len(ins),
        out_specs=tuple(out_specs or [VMEM] * len(outs)),
        scratch_shapes=list(scratch),
        input_output_aliases=aliases or {},
        compiler_params=pltpu.CompilerParams(vmem_limit_bytes=limit * MIB),
        name=kernel.__name__,
    )(*ins)


def along(value, step, chips):
    pairs = [(2 * chip, 2 * ((chip + step) % chips)) for chip in range(chips)]
    pairs += [(2 * chip + 1, 2 * ((chip - step) % chips) + 1) for chip in range(chips)]
    return lax.ppermute(value, ("z", "c"), pairs)


def per_device(features, w_self, w_neigh, out_grad, tile_count, tile_dst, tile_src, tile_weight, chips, parts):
    rows = features.shape[0]
    groups = 2 * chips
    slots = tile_weight.shape[1]
    swap = [(0, 1), (1, 0)]

    (x_pay,) = call(
        spread_kernel,
        (features,),
        [((parts, rows, T), BF16)],
        in_specs=[HBM],
        out_specs=[HBM],
        scratch=[pltpu.VMEM((rows, T), BF16), pltpu.SemaphoreType.DMA, pltpu.SemaphoreType.DMA((parts,))],
    )
    x_all = lax.all_to_all(x_pay, "f", 0, 0, tiled=True)
    adj, adj_send, adj_back, inverse, flags = call(
        adjacency_kernel,
        (tile_count, tile_dst, tile_src, tile_weight[0]),
        [
            ((groups, rows, T), BF16),
            ((chips - 1, rows, T), BF16),
            ((chips - 1, rows, T), BF16),
            ((rows, T), F32),
            ((groups, T), F32),
        ],
        in_specs=[SMEM, HBM, HBM, HBM],
        out_specs=[VMEM, HBM, HBM, VMEM, VMEM],
        scratch=[
            pltpu.SMEM(tile_dst.shape, jnp.int32),
            pltpu.SMEM(tile_src.shape, jnp.int32),
            pltpu.VMEM((slots, T, T), jnp.int32),
            pltpu.VMEM((groups, rows, T), jnp.int32),
            pltpu.SMEM((groups,), jnp.int32),
            pltpu.VMEM((chips - 1, rows, T), BF16),
            pltpu.VMEM((chips - 1, rows, T), BF16),
            pltpu.SemaphoreType.DMA((2,)),
            pltpu.SemaphoreType.DMA((2,)),
            pltpu.SemaphoreType.DMA((slots // CHUNK,)),
        ],
        limit=20,
    )
    adj_pair, adj_back = lax.ppermute(adj_send, "c", swap), lax.ppermute(adj_back, "c", swap)
    y, flags_pair, adj_pair = call(
        neighbour_kernel,
        (x_all, w_neigh, lax.ppermute(flags, "c", swap), adj_pair),
        [((rows, T), BF16), (flags.shape, F32), (adj_pair.shape, BF16)],
        in_specs=[VMEM] * 2 + [ANY, HBM],
        out_specs=[VMEM, ANY, HBM],
        aliases={2: 1, 3: 2},
    )
    (pair,) = call(join_kernel, (y, lax.ppermute(y, "c", swap)), [((2,) + y.shape, BF16)])
    two, one = along(pair, 2, chips), along(pair, 1, chips)
    (half,) = call(half_kernel, (two,), [(y.shape, BF16)])
    three, far = along(two, 1, chips), along(half, 2, chips)
    one, adj_pair, adj_back = call(
        fetch_kernel,
        (one, adj_pair, adj_back),
        [(one.shape, BF16), (adj_pair.shape, BF16), (adj_back.shape, BF16)],
        in_specs=[ANY, HBM, HBM],
        out_specs=[ANY, VMEM, VMEM],
        scratch=[pltpu.SemaphoreType.DMA((2,))],
        aliases={0: 0},
    )
    mine, theirs = call(
        aggregate_kernel,
        (flags, flags_pair, adj, adj_pair, pair, one, two, three, far),
        [((rows, T), F32)] * 2,
    )
    came = lax.ppermute(theirs, "c", swap)
    (z_self,) = call(self_kernel, (x_all, w_self), [((rows, T), F32)])
    output, gt, scaled = call(
        activation_kernel,
        (inverse, mine, came, z_self, out_grad),
        [((rows, T), BF16), ((T, rows), BF16), ((2 * T, rows), BF16)],
    )

    def sends(block):
        pair = (2,) + block
        return [(block, BF16), (pair, BF16), (pair, BF16), (pair, F32), (block, F32)]

    def reduce(far, three, one, two, own):
        block = own.shape
        (two,) = call(
            relay_kernel, (two, along(three, 1, chips), along(far, 2, chips)), [((2,) + block, BF16)]
        )
        two, one = along(two, 2, chips), along(one, 1, chips)
        mine, theirs = call(fold_kernel, (own, two, one), [(block, F32)] * 2)
        return mine, lax.ppermute(theirs, "c", swap)

    parts_sent = call(
        transpose_kernel,
        (flags, flags_pair, adj, adj_pair, adj_back, scaled, lax.ppermute(scaled, "c", swap)),
        sends((T, rows)),
    )
    mine, came = reduce(*parts_sent)
    bt, keep, send = call(
        weight_grad_kernel,
        (mine, came, gt, x_all),
        [((T, rows), BF16), ((chips, 2 * T, T), F32), ((chips, 2 * T, T), BF16)],
    )
    came = lax.ppermute(send, "c", swap)
    (p_pay,) = call(
        feature_grad_kernel,
        (gt, bt, w_self, w_neigh),
        [((parts, T, rows), BF16)],
        out_specs=[HBM],
        scratch=[pltpu.VMEM((parts, T, rows), BF16), pltpu.SemaphoreType.DMA((parts,))],
    )
    *parts_sent, p_pay = call(
        pair_kernel,
        (keep, came, p_pay),
        sends((2 * T, T)) + [(p_pay.shape, BF16)],
        in_specs=[VMEM, VMEM, HBM],
        out_specs=[VMEM] * 5 + [HBM],
        aliases={2: 5},
    )
    p_all = lax.all_to_all(p_pay, "f", 0, 0, tiled=True)
    mine, came = reduce(*parts_sent)
    (grad_features,) = call(sum_kernel, (p_all,), [((rows, T), BF16)])
    grad_self, grad_neigh, grad_features = call(
        last_kernel,
        (mine, came, grad_features),
        [((T, T), F32), ((T, T), F32), ((rows, T), BF16)],
        in_specs=[VMEM] * 2 + [ANY],
        out_specs=[VMEM, VMEM, ANY],
        aliases={2: 2},
    )
    return output, grad_features, grad_self, grad_neigh


def solution(mesh):
    row_count, part_count = mesh.shape["rows"], mesh.shape["feat"]
    split = Mesh(mesh.devices.reshape(row_count // 2, 2, part_count), ("z", "c", "f"))
    rows, feat = ("z", "c"), "f"
    return jax.shard_map(
        functools.partial(per_device, chips=row_count // 2, parts=part_count),
        mesh=split,
        in_specs=(
            P(rows, feat),
            P(None, feat),
            P(None, feat),
            P(rows, feat),
            P(rows),
            P(rows, None),
            P(rows, None),
            P(rows, None, None, None),
        ),
        out_specs=(P(rows, feat),) * 4,
        check_vma=False,
    )
```
